32 devices in a mesh: dp: 8 (over z, x), tensor: 4 (over y, core).
Axes of the slice: x: 2, y: 2, z: 4, core: 2. Of those that a mesh axis runs over, the one named last changes fastest.
Arguments:
- frames: bfloat16 [16, 1500, 768], P('dp', 'tensor'), may hold values from -6 to 6
- cotangent: bfloat16 [16, 1500, 768], P('dp', 'tensor'), may hold values from -6 to 6
- qkv_weight: bfloat16 [2, 768, 3, 768], P(None, 'dp', None, 'tensor'), may hold values from -0.21875 to 0.21875
- out_weight: bfloat16 [2, 768, 768], P(None, 'tensor', 'dp'), may hold values from -6 to 6
- up_weight: bfloat16 [2, 768, 3072], P(None, 'dp', 'tensor'), may hold values from -0.21875 to 0.21875
- down_weight: bfloat16 [2, 3072, 768], P(None, 'tensor', 'dp'), may hold values from -0.109375 to 0.109375
- qv_bias: float32 [2, 2, 768], P(None, None, ('tensor', 'dp')), may hold values from -0.3 to 0.3
- up_bias: float32 [2, 3072], P(None, ('tensor', 'dp')), may hold values from -3 to 3
- norm_gains: float32 [2, 2, 768], P(None, None, ('dp', 'tensor')), may hold values from 0.5 to 1.5
- norm_shifts: float32 [2, 2, 768], P(None, None, ('dp', 'tensor')), may hold values from -0.3 to 0.3
- out_biases: float32 [2, 2, 768], P(None, None, ('dp', 'tensor')), may hold values from -2 to 2
Outputs:
- encoded: float32 [16, 1500, 768], P('dp', 'tensor')
- frames_grad: float32 [16, 1500, 768], P('dp', 'tensor')
- qkv_grad: float32 [2, 768, 3, 768], P(None, 'dp', None, 'tensor')
- out_grad: float32 [2, 768, 768], P(None, 'tensor', 'dp')
- up_grad: float32 [2, 768, 3072], P(None, 'dp', 'tensor')
- down_grad: float32 [2, 3072, 768], P(None, 'tensor', 'dp')
- qv_bias_grad: float32 [2, 2, 768], P(None, None, ('tensor', 'dp'))
- up_bias_grad: float32 [2, 3072], P(None, ('tensor', 'dp'))
- gains_grad: float32 [2, 2, 768], P(None, None, ('dp', 'tensor'))
- shifts_grad: float32 [2, 2, 768], P(None, None, ('dp', 'tensor'))
- out_biases_grad: float32 [2, 2, 768], P(None, None, ('dp', 'tensor'))
The draws below stay inside these ranges and needn't reach their ends.
All inputs are finite; a program needn't handle non-finite values.
Results may differ from the reference program's by a relative error of at most 0.023.
Values may be sent and summed in bfloat16 or wider, within the bound.
No kernel may reach another device: no remote copies, remote signals or barrier semaphores. Data moves between devices by JAX's collectives and lax.ppermute only.
A program may use at most 320 MiB of HBM per device.

```python
import jax
import jax.numpy as jnp
from jax import lax

D = 768
HD = 64
FF = 3072
FRAMES = 1500
LAYERS = 2
CLIPS = 16


def steps_of(own_key, dims, shards, smallest, high):
    level = 1.0
    for axis_at, shards_of in shards:
        steps = jax.random.uniform(jax.random.fold_in(jax.random.fold_in(own_key, 6), axis_at), (shards_of,), jnp.float32, smallest / len(shards), high / len(shards))
        level = level * jnp.repeat(jnp.exp(steps), dims[axis_at] // shards_of).reshape((-1,) + (1,) * (len(dims) - 1 - axis_at))
    return level


def bell_draw(own_key, shape, scale, limit, split=(), kind=jnp.bfloat16):
    result = jax.random.normal(own_key, shape, jnp.float32) * scale
    if len(split) > 0:
        result = steps_of(own_key, shape, split, -0.22, 0.18) * result
    return jnp.clip(result, min=-limit, max=limit).astype(kind)


def setup_inputs(seed: int = 0) -> dict:
    key_list = jax.random.split(jax.random.key(seed), 12)
    return {
        "frames": bell_draw(key_list[0], (CLIPS, FRAMES, D), 1.0, 6.0, ((0, 8), (1, 4))),
        "cotangent": bell_draw(key_list[1], (CLIPS, FRAMES, D), 1.0, 6.0, ((0, 8), (1, 4))),
        "qkv_weight": bell_draw(key_list[2], (LAYERS, D, 3, D), D ** -0.5, 0.21875, ((1, 8), (3, 4))),
        "out_weight": bell_draw(key_list[3], (LAYERS, D, D), (max(3 * D // FRAMES, 1)) ** -0.5, 6.0, ((1, 4), (2, 8))),
        "up_weight": bell_draw(key_list[4], (LAYERS, D, FF), D ** -0.5, 0.21875, ((1, 8), (2, 4))),
        "down_weight": bell_draw(key_list[5], (LAYERS, FF, D), FF ** -0.5, 0.109375, ((1, 4), (2, 8))),
        "qv_bias": bell_draw(key_list[6], (LAYERS, 2, D), 0.05, 0.3, ((2, 32),), jnp.float32),
        "up_bias": bell_draw(key_list[7], (LAYERS, FF), 0.5, 3.0, ((1, 32),), jnp.float32),
        "norm_gains": jnp.clip(1.0 + 0.1 * jax.random.normal(key_list[8], (LAYERS, 2, D), jnp.float32), 0.5, 1.5),
        "norm_shifts": bell_draw(key_list[9], (LAYERS, 2, D), 0.05, 0.3, ((2, 32),), jnp.float32),
        "out_biases": bell_draw(key_list[10], (LAYERS, 2, D), 0.3, 2.0, ((2, 32),), jnp.float32),
    }


@jax.custom_vjp
def low(v):
    return lax.optimization_barrier(v.astype(jnp.bfloat16)).astype(jnp.float32)

@jax.custom_vjp
def low_back(v):
    return v

def low_keep(v):
    return (low(v), None)

def low_pass(kept, grad):
    return (grad,)

def back_keep(v):
    return (v, None)

def back_low(kept, grad):
    return (low(grad),)
low.defvjp(low_keep, low_pass)
low_back.defvjp(back_keep, back_low)
eps = 1e-05
highest = lax.Precision.HIGHEST

def both_ways(value):
    return low(low_back(value))

def layer_norm(value, gain, shift):
    centre = lax.optimization_barrier(jnp.mean(value, axis=-1, keepdims=True))
    centred = value - centre
    spread = lax.optimization_barrier(jnp.mean(centred * centred, axis=-1, keepdims=True))
    return centred * lax.rsqrt(spread + eps) * gain + shift

def attend_clip(operands):
    queries, key_rows, value_rows = operands
    score_scale = queries.shape[-1] ** (-0.5)
    scores = low_back(score_scale * jnp.einsum('qhd,khd->hqk', queries, key_rows, precision=highest))
    probs = low(jax.nn.softmax(scores, axis=-1))
    return jnp.einsum('hqk,khd->qhd', probs, value_rows, precision=highest)

def encoder_layer(current, w_qkv, w_out, w_up, w_down, b_qv, b_up, gain, shift, obias):
    clip_count, frame_count, width = current.shape
    head_count = width // HD
    normed = low(layer_norm(current, gain[0], shift[0]))
    projected = jnp.einsum('cfd,dkh->cfkh', normed, w_qkv, precision=highest)
    queries = both_ways(projected[:, :, 0] + b_qv[0])
    key_rows = both_ways(projected[:, :, 1])
    value_rows = both_ways(projected[:, :, 2] + b_qv[1])
    shape_heads = (clip_count, frame_count, head_count, HD)
    attended = lax.map(jax.checkpoint(attend_clip), (queries.reshape(shape_heads), key_rows.reshape(shape_heads), value_rows.reshape(shape_heads)))
    attended = both_ways(attended.reshape(clip_count, frame_count, width))
    branch = low_back(jnp.einsum('cfh,hd->cfd', attended, w_out, precision=highest) + obias[0])
    middle = current + branch
    normed_two = low(layer_norm(middle, gain[1], shift[1]))
    upward = low_back(jnp.einsum('cfd,dk->cfk', normed_two, w_up, precision=highest) + b_up)
    activated = low(jax.nn.gelu(upward, approximate=False))
    feed_out = low_back(jnp.einsum('cfk,kd->cfd', activated, w_down, precision=highest) + obias[1])
    return middle + feed_out

def forward(current, qkv_weight, out_weight, up_weight, down_weight, qv_bias, up_bias, norm_gains, norm_shifts, out_biases):
    for layer_at in range(LAYERS):
        current = encoder_layer(current, qkv_weight[layer_at], out_weight[layer_at], up_weight[layer_at], down_weight[layer_at], qv_bias[layer_at], up_bias[layer_at], norm_gains[layer_at], norm_shifts[layer_at], out_biases[layer_at])
    return current

def reference(frames, cotangent, qkv_weight, out_weight, up_weight, down_weight, qv_bias, up_bias, norm_gains, norm_shifts, out_biases):
    weights_in = (qkv_weight.astype(jnp.float32), out_weight.astype(jnp.float32), up_weight.astype(jnp.float32), down_weight.astype(jnp.float32), qv_bias.astype(jnp.float32), up_bias.astype(jnp.float32), norm_gains.astype(jnp.float32), norm_shifts.astype(jnp.float32), out_biases.astype(jnp.float32))
    encoded, pullback = jax.vjp(forward, frames.astype(jnp.float32), *weights_in)
    gradients = pullback(cotangent.astype(jnp.float32))
    return (encoded, gradients[0], gradients[1], gradients[2], gradients[3], gradients[4], gradients[5], gradients[6], gradients[7], gradients[8], gradients[9])
```

```python
import functools
import math

import jax
import jax.numpy as jnp
from jax import lax
from jax.experimental import pallas as pl
from jax.experimental.pallas import tpu as pltpu
from jax.sharding import PartitionSpec as P

HD = 64
WIDE = 128
eps = 1e-05
LOG2E = 1.0 / math.log(2.0)
LN2 = math.log(2.0)
MASKED = -1e30
bf16 = jnp.bfloat16
f32 = jnp.float32


def exchange(value, axis, mask):
    count = lax.axis_size(axis)
    return lax.ppermute(value, axis, [(i, i ^ mask) for i in range(count)])


def dp_masks():
    count = lax.axis_size("dp")
    masks = []
    while count > 1:
        count //= 2
        masks.append(count)
    return masks


def relative_mask(position):
    result = 0
    for at, mask in enumerate(dp_masks()):
        result = result + ((position >> at) & 1) * mask
    return result


def spread(block, y_last):
    masks = dp_masks()
    early = masks if y_last else masks[:-1]
    for mask in early:
        block = jnp.concatenate([block, exchange(block, "dp", mask)], axis=0)
    other = exchange(block, "tensor", 2)
    if y_last:
        return [block, other]
    return [
        jnp.concatenate([part, exchange(part, "dp", masks[-1])], axis=0) for part in (block, other)
    ]


def add_low(kept, received):
    return (kept.astype(f32) + received.astype(f32)).astype(bf16)


def halve(value, mask):
    half = value.shape[0] // 2
    return add_low(value[:half], exchange(value[half:], "dp", mask))


def fold(own, other, y_first):
    masks = dp_masks()
    if not y_first:
        own, other = halve(own, masks[-1]), halve(other, masks[-1])
    own = add_low(own, exchange(other, "tensor", 2))
    for mask in reversed(masks if y_first else masks[:-1]):
        own = halve(own, mask)
    return own


def split_low(value):
    high = value.astype(bf16)
    rest = value - high.astype(f32)
    mid = rest.astype(bf16)
    return high, mid, (rest - mid.astype(f32)).astype(bf16)


def lane_at(rows):
    return lax.broadcasted_iota(jnp.int32, (rows, WIDE - HD), 1)


def key_extra(rows, row_count, quarter, ones):
    lane = lane_at(rows)
    row = lax.broadcasted_iota(jnp.int32, (rows, WIDE - HD), 0)
    masked = lax.rem(row, quarter) >= row_count
    bias = jnp.where(masked, MASKED, 0.0).astype(f32)
    value = jnp.where(lane == 0, bias, jnp.where(lane <= ones, 1.0, 0.0))
    return value.astype(bf16)


def ones_extra(rows, ones):
    return jnp.where(lane_at(rows) < ones, 1.0, 0.0).astype(bf16)


def widen(part, extra):
    return jnp.concatenate([part, extra], axis=1)


def nt_dot(left, right):
    return lax.dot_general(left, right, (((1,), (1,)), ((), ())), preferred_element_type=f32)


def nn_dot(left, right):
    return lax.dot_general(left, right, (((1,), (0,)), ((), ())), preferred_element_type=f32)


def tn_dot(left, right):
    return lax.dot_general(left, right, (((0,), (0,)), ((), ())), preferred_element_type=f32)


def attend_kernel(row_count, quarter, step, qk_a, v_a, qk_b, v_b, o_a, o_b, lse, q_s, k_s, v_s, o_s):
    rows = qk_a.shape[1]
    wide = v_a.shape[2]
    heads = wide // HD
    k_more = key_extra(rows, row_count, quarter, 0)
    one = ones_extra(rows, 1)
    for half, (qk, v) in enumerate(((qk_a, v_a), (qk_b, v_b))):
        at = pl.ds(half * rows, rows)
        for h in range(heads):
            low, high = h * HD, (h + 1) * HD
            q_s[h, at, :] = widen(qk[0, :, low:high], one)
            k_s[h, at, :] = widen(qk[0, :, wide + low : wide + high], k_more)
            v_s[h, at, :] = widen(v[0, :, low:high], one)

    for h in range(heads):

        def work(i, carry, h=h):
            for part in range(2):
                at = pl.ds(pl.multiple_of((2 * i + part) * step, step), step)
                scores = nt_dot(q_s[h, at, :], k_s[h])
                top = jnp.max(scores, axis=-1, keepdims=True)
                weights = jnp.exp2(scores - top).astype(bf16)
                summed = nn_dot(weights, v_s[h])
                total = summed[:, HD : HD + 1]
                o_s[at, h * HD : (h + 1) * HD] = (summed[:, :HD] / total).astype(bf16)
                lse[0, at, h : h + 1] = top + jnp.log2(total)
            return carry

        lax.fori_loop(0, rows // step, work, 0)
    o_a[0] = o_s[pl.ds(0, rows), :]
    o_b[0] = o_s[pl.ds(rows, rows), :]


def block_of(shape):
    return pl.BlockSpec((1,) + shape, lambda t: (t, 0, 0))


def attend(row_count, quarter, qk_a, v_a, qk_b, v_b):
    groups, rows, wide = v_a.shape
    heads = wide // HD
    return pl.pallas_call(
        functools.partial(attend_kernel, row_count, quarter, min(256, rows)),
        grid=(groups,),
        in_specs=[block_of((rows, 2 * wide)), block_of((rows, wide))] * 2,
        out_specs=[block_of((rows, wide))] * 2 + [block_of((2 * rows, 8))],
        out_shape=[jax.ShapeDtypeStruct((groups, rows, wide), bf16)] * 2
        + [jax.ShapeDtypeStruct((groups, 2 * rows, 8), f32)],
        scratch_shapes=[pltpu.VMEM((heads, 2 * rows, WIDE), bf16)] * 3
        + [pltpu.VMEM((2 * rows, wide), bf16)],
        compiler_params=pltpu.CompilerParams(vmem_limit_bytes=48 * 2**20),
    )(qk_a, v_a, qk_b, v_b)


def attend_back_kernel(
    row_count, quarter, step,
    qk_a, v_a, qk_b, v_b, o_a, o_b, do_a, do_b, lse,
    dqk_a, dv_a, dqk_b, dv_b,
    q_s, k_s, kt_s, v_s, do_s, dq_s, dk_s, dv_s,
):
    rows = qk_a.shape[1]
    wide = v_a.shape[2]
    heads = wide // HD
    k_more = key_extra(rows, row_count, quarter, 3)
    three = ones_extra(rows, 3)
    lane = lane_at(rows)

    def spread_lanes(first, parts):
        value = jnp.where(lane < first, 1.0, 0.0).astype(f32)
        for at, part in enumerate(parts):
            value = jnp.where(lane == first + at, part.astype(f32), value)
        return value.astype(bf16)

    for half, (qk, v, o, do) in enumerate(((qk_a, v_a, o_a, do_a), (qk_b, v_b, o_b, do_b))):
        at = pl.ds(half * rows, rows)
        for h in range(heads):
            low, high = h * HD, (h + 1) * HD
            minus_lse = split_low(-lse[0, at, h : h + 1])
            q_s[h, at, :] = widen(qk[0, :, low:high], spread_lanes(1, minus_lse))
            keys = widen(qk[0, :, wide + low : wide + high], k_more)
            k_s[h, at, :] = keys
            kt_s[h, :, at] = jnp.transpose(keys.astype(f32)).astype(bf16)
            v_s[h, at, :] = widen(v[0, :, low:high], three)
            grad = do[0, :, low:high]
            inner = jnp.sum(grad.astype(f32) * o[0, :, low:high].astype(f32), axis=1, keepdims=True)
            do_s[h, at, :] = widen(grad, spread_lanes(0, split_low(-inner)))

    dk_s[...] = jnp.zeros_like(dk_s)
    dv_s[...] = jnp.zeros_like(dv_s)
    chunks = 2 * rows // step

    def work(i, carry):
        h = i // chunks
        at = pl.ds(pl.multiple_of(lax.rem(i, chunks) * step, step), step)
        queries = q_s[h, at, :]
        grad_out = do_s[h, at, :]
        probs = jnp.exp2(nt_dot(k_s[h], queries))
        grad_scores = (probs * nt_dot(v_s[h], grad_out)).astype(bf16)
        dv_s[h] += nn_dot(probs.astype(bf16), grad_out)
        dk_s[h] += nn_dot(grad_scores, queries)
        dq_s[h, at, :] = jnp.transpose(nn_dot(kt_s[h], grad_scores))
        return carry

    lax.fori_loop(0, heads * chunks, work, 0)
    for half, (dqk, dv) in enumerate(((dqk_a, dv_a), (dqk_b, dv_b))):
        at = pl.ds(half * rows, rows)
        for h in range(heads):
            low, high = h * HD, (h + 1) * HD
            dqk[0, :, low:high] = (dq_s[h, at, :][:, :HD] * HD**-0.5).astype(bf16)
            dqk[0, :, wide + low : wide + high] = (dk_s[h, at, :][:, :HD] * LN2).astype(bf16)
            dv[0, :, low:high] = dv_s[h, at, :][:, :HD].astype(bf16)


def attend_back(row_count, quarter, qk_a, v_a, qk_b, v_b, o_a, o_b, do_a, do_b, lse):
    groups, rows, wide = v_a.shape
    heads = wide // HD
    return pl.pallas_call(
        functools.partial(attend_back_kernel, row_count, quarter, min(256, rows)),
        grid=(groups,),
        in_specs=[block_of((rows, 2 * wide)), block_of((rows, wide))] * 2
        + [block_of((rows, wide))] * 4
        + [block_of((2 * rows, 8))],
        out_specs=[block_of((rows, 2 * wide)), block_of((rows, wide))] * 2,
        out_shape=[
            jax.ShapeDtypeStruct((groups, rows, 2 * wide), bf16),
            jax.ShapeDtypeStruct((groups, rows, wide), bf16),
        ]
        * 2,
        scratch_shapes=[
            pltpu.VMEM((heads, 2 * rows, WIDE), bf16),
            pltpu.VMEM((heads, 2 * rows, WIDE), bf16),
            pltpu.VMEM((heads, WIDE, 2 * rows), bf16),
            pltpu.VMEM((heads, 2 * rows, WIDE), bf16),
            pltpu.VMEM((heads, 2 * rows, WIDE), bf16),
            pltpu.VMEM((heads, 2 * rows, WIDE), f32),
            pltpu.VMEM((heads, 2 * rows, WIDE), f32),
            pltpu.VMEM((heads, 2 * rows, WIDE), f32),
        ],
        compiler_params=pltpu.CompilerParams(vmem_limit_bytes=56 * 2**20),
    )(qk_a, v_a, qk_b, v_b, o_a, o_b, do_a, do_b, lse)


def normalized(value):
    centred = value - jnp.mean(value, axis=-1, keepdims=True)
    scale = lax.rsqrt(jnp.mean(centred * centred, axis=-1, keepdims=True) + eps)
    return centred * scale, scale


def norm_back(value, gain, grad):
    unit, scale = normalized(value)
    scaled = grad * gain
    result = scale * (
        scaled
        - jnp.mean(scaled, axis=-1, keepdims=True)
        - unit * jnp.mean(scaled * unit, axis=-1, keepdims=True)
    )
    return result, jnp.sum(grad * unit, axis=0), jnp.sum(grad, axis=0)


def gelu_both(value):
    share = 0.5 * (1.0 + lax.erf(value * math.sqrt(0.5)))
    density = jnp.exp(-0.5 * value * value) * (1.0 / math.sqrt(2.0 * math.pi))
    return (value * share).astype(bf16), (share + value * density).astype(bf16)


def local(
    frames,
    cotangent,
    qkv_weight,
    out_weight,
    up_weight,
    down_weight,
    qv_bias,
    up_bias,
    norm_gains,
    norm_shifts,
    out_biases,
):
    layers, block = qkv_weight.shape[:2]
    wide = qkv_weight.shape[3]
    row_count, width = frames.shape[1:]
    hidden = up_weight.shape[2]
    quarter = -(-row_count // 128) * 128
    rows = 2 * quarter
    count_dp = lax.axis_size("dp")
    me = lax.axis_index("dp")
    t_me = lax.axis_index("tensor")
    y_me = t_me // 2
    t_order = jnp.arange(4) ^ t_me
    positions = jnp.arange(count_dp)
    block_at = relative_mask(positions) ^ me
    place_of = jnp.argmax(block_at[None, :] == positions[:, None], axis=1)

    small_parts = (norm_gains, norm_shifts, out_biases, qv_bias, up_bias)
    small_sizes = [part.size for part in small_parts]
    small = jnp.concatenate([part.reshape(1, -1) for part in small_parts], axis=1)
    for mask in dp_masks():
        small = jnp.concatenate([small, exchange(small, "dp", mask)], axis=0)
    small = jnp.stack([small, exchange(small, "tensor", 1)])
    small = jnp.stack([small, exchange(small, "tensor", 2)])
    small = small.reshape(4, count_dp, -1)
    by_part = jnp.split(small, [sum(small_sizes[: i + 1]) for i in range(4)], axis=2)

    def by_width(part):
        part = jnp.take(part, t_order, axis=0).reshape(4, count_dp, layers, 2, -1)
        return part.transpose(2, 3, 1, 0, 4).reshape(layers, 2, width)

    gain_all, shift_all, obias_all = [by_width(part) for part in by_part[:3]]
    qv_all = jnp.take(by_part[3][0::2], place_of, axis=1).reshape(2, count_dp, layers, 2, -1)
    qv_all = qv_all.transpose(2, 3, 0, 1, 4).reshape(layers, 2, 2, wide)
    up_all = jnp.take(by_part[4], place_of, axis=1).reshape(4, count_dp, layers, -1)
    up_all = up_all.transpose(2, 0, 1, 3).reshape(layers, 4, hidden)

    source = jnp.repeat(block_at, block) * block + jnp.tile(jnp.arange(block), count_dp)
    to_relative = (jnp.arange(width)[:, None] == source[None, :]).astype(bf16)

    def take_clip(value):
        mine = lax.dynamic_index_in_dim(value, y_me, 0, keepdims=False)
        theirs = exchange(lax.dynamic_index_in_dim(value, 1 - y_me, 0, keepdims=False), "tensor", 2)
        padding = ((0, 0), (0, quarter - row_count), (0, 0))
        both = jnp.pad(jnp.stack([mine, theirs]), padding).reshape(rows, width)
        return nn_dot(both, to_relative)

    def give_clip(value):
        mine, theirs = value[:quarter], value[quarter:].astype(bf16)
        theirs = nt_dot(exchange(theirs, "tensor", 2), to_relative)[:row_count]
        high = mine.astype(bf16)
        low = (mine - high.astype(f32)).astype(bf16)
        mine = (nt_dot(high, to_relative) + nt_dot(low, to_relative))[:row_count]
        first = y_me == 0
        return jnp.stack([jnp.where(first, mine, theirs), jnp.where(first, theirs, mine)])

    current = take_clip(frames)
    gradient = take_clip(cotangent)

    weights = []
    for at in range(layers):
        qk = jnp.concatenate([qkv_weight[at, :, 0], qkv_weight[at, :, 1]], axis=1)
        vo = jnp.concatenate([qkv_weight[at, :, 2], out_weight[at].T], axis=1)
        w_qk = jnp.stack(spread(qk, True))
        w_vo = jnp.stack(spread(vo, False))
        w_up = spread(up_weight[at], True)
        w_down = spread(down_weight[at].T, False)
        w_up = [
            w_up[0], exchange(w_up[0], "tensor", 1), w_up[1], exchange(w_up[1], "tensor", 1)
        ]
        w_down = [
            w_down[0], exchange(w_down[0], "tensor", 1), w_down[1], exchange(w_down[1], "tensor", 1)
        ]
        weights.append((w_qk, w_vo[:, :, :wide], w_vo[:, :, wide:], w_up, w_down))

    def project(value, weight):
        return jnp.einsum("fd,tdk->tfk", value, weight, preferred_element_type=f32)

    saved = []
    q_scale = HD**-0.5 * LOG2E
    for at in range(layers):
        w_qk, w_v, w_o, w_up, w_down = weights[at]
        unit, _ = normalized(current)
        normed_a = (unit * gain_all[at, 0] + shift_all[at, 0]).astype(bf16)
        normed_b = exchange(normed_a, "tensor", 1)
        qk_scale = jnp.where(jnp.arange(2 * wide) < wide, q_scale, 1.0)
        qk_bias = jnp.concatenate([qv_all[at, 0], jnp.zeros_like(qv_all[at, 0])], axis=1)

        def heads_of(normed):
            qk = ((project(normed, w_qk) + qk_bias[:, None]) * qk_scale).astype(bf16)
            v = (project(normed, w_v) + qv_all[at, 1][:, None]).astype(bf16)
            return qk, v

        qk_a, v_a = heads_of(normed_a)
        qk_b, v_b = heads_of(normed_b)
        o_a, o_b, lse = attend(row_count, quarter, qk_a, v_a, qk_b, v_b)
        share_b = nt_dot(o_b[0], w_o[0]) + nt_dot(o_b[1], w_o[1])
        share_b = exchange(share_b.astype(bf16), "tensor", 1)
        share_a = nt_dot(o_a[0], w_o[0]) + nt_dot(o_a[1], w_o[1])
        middle = current + (share_a + share_b.astype(f32) + obias_all[at, 0])
        unit, _ = normalized(middle)
        normed_two = (unit * gain_all[at, 1] + shift_all[at, 1]).astype(bf16)
        activated = [gelu_both(nn_dot(normed_two, w_up[t]) + up_all[at, t]) for t in range(4)]
        feed = obias_all[at, 1]
        for t in range(4):
            feed = feed + nt_dot(activated[t][0], w_down[t])
        saved.append(
            (current, normed_a, normed_b, qk_a, v_a, qk_b, v_b, o_a, o_b, lse, middle, normed_two, activated)
        )
        current = middle + feed
    encoded = give_clip(current)

    small_grads = [None] * layers
    weight_grads = [None] * layers
    for at in reversed(range(layers)):
        w_qk, w_v, w_o, w_up, w_down = weights[at]
        (layer_in, normed_a, normed_b, qk_a, v_a, qk_b, v_b, o_a, o_b, lse, middle, normed_two, activated) = saved[at]
        grad_feed = gradient.astype(bf16)
        obias_two = jnp.sum(grad_feed, axis=0, dtype=f32)
        grad_up = [
            (nn_dot(grad_feed, w_down[t]) * activated[t][1].astype(f32)).astype(bf16)
            for t in range(4)
        ]
        grad_normed = sum(nt_dot(grad_up[t], w_up[t]) for t in range(4))
        bup = jnp.stack([jnp.sum(part, axis=0, dtype=f32) for part in grad_up])
        dw_up = [tn_dot(normed_two, grad_up[t]).astype(bf16) for t in range(4)]
        dw_down = [tn_dot(grad_feed, activated[t][0]).astype(bf16) for t in range(4)]
        for dw in (dw_up, dw_down):
            for t in (0, 2):
                dw[t] = add_low(dw[t], exchange(dw[t + 1], "tensor", 1))
        dw_up = fold(dw_up[0], dw_up[2], True)
        dw_down = fold(dw_down[0], dw_down[2], False)

        grad_middle, gain_two, shift_two = norm_back(middle, gain_all[at, 1], grad_normed)
        gradient = gradient + grad_middle
        branch_a = gradient.astype(bf16)
        branch_b = exchange(branch_a, "tensor", 1)
        obias_one = jnp.sum(branch_a, axis=0, dtype=f32)
        do_a = project(branch_a, w_o).astype(bf16)
        do_b = project(branch_b, w_o).astype(bf16)
        dqk_a, dv_a, dqk_b, dv_b = attend_back(
            row_count, quarter, qk_a, v_a, qk_b, v_b, o_a, o_b, do_a, do_b, lse
        )

        def back_normed(dqk, dv):
            return sum(nt_dot(dqk[t], w_qk[t]) + nt_dot(dv[t], w_v[t]) for t in range(2))

        share_b = exchange(back_normed(dqk_b, dv_b).astype(bf16), "tensor", 1)
        grad_normed = back_normed(dqk_a, dv_a) + share_b.astype(f32)
        dw_qk = [
            (tn_dot(normed_a, dqk_a[t]) + tn_dot(normed_b, dqk_b[t])).astype(bf16) for t in range(2)
        ]
        dw_vo = [
            jnp.concatenate(
                [
                    (tn_dot(normed_a, dv_a[t]) + tn_dot(normed_b, dv_b[t])).astype(bf16),
                    (tn_dot(branch_a, o_a[t]) + tn_dot(branch_b, o_b[t])).astype(bf16),
                ],
                axis=1,
            )
            for t in range(2)
        ]
        dw_qk = fold(dw_qk[0], dw_qk[1], True)
        dw_vo = fold(dw_vo[0], dw_vo[1], False)
        weight_grads[at] = [part.astype(f32) for part in (dw_qk, dw_vo, dw_up, dw_down)]
        bq = jnp.sum(dqk_a[:, :, :wide], axis=1, dtype=f32)
        bq = bq + jnp.sum(dqk_b[:, :, :wide], axis=1, dtype=f32)
        bv = jnp.sum(dv_a, axis=1, dtype=f32) + jnp.sum(dv_b, axis=1, dtype=f32)
        grad_in, gain_one, shift_one = norm_back(layer_in, gain_all[at, 0], grad_normed)
        gradient = gradient + grad_in
        small_grads[at] = (
            jnp.stack([gain_one, gain_two]),
            jnp.stack([shift_one, shift_two]),
            jnp.stack([obias_one, obias_two]),
            jnp.stack([bq, bv]),
            bup,
        )
    frames_grad = give_clip(gradient)

    gains, shifts, obiases, bqv, bups = [
        jnp.stack([small_grads[at][i] for at in range(layers)]) for i in range(5)
    ]

    def from_width(part):
        part = part.reshape(layers, 2, count_dp, 4, -1).transpose(3, 2, 0, 1, 4)
        return jnp.take(part.reshape(4, count_dp, -1), t_order, axis=0)

    bqv = bqv.reshape(layers, 2, 2, count_dp, -1).transpose(2, 3, 0, 1, 4)
    bqv = jnp.take(bqv.reshape(2, count_dp, -1), block_at, axis=1)
    bqv = jnp.stack([bqv, jnp.zeros_like(bqv)], axis=1).reshape(4, count_dp, -1)
    bups = bups.reshape(layers, 4, count_dp, -1).transpose(1, 2, 0, 3)
    bups = jnp.take(bups.reshape(4, count_dp, -1), block_at, axis=1)
    small = jnp.concatenate(
        [from_width(gains), from_width(shifts), from_width(obiases), bqv, bups], axis=2
    )
    small = small.reshape(2, 2, count_dp, -1)
    small = small[0] + exchange(small[1], "tensor", 2)
    small = small[0] + exchange(small[1], "tensor", 1)
    for mask in reversed(dp_masks()):
        half = small.shape[0] // 2
        small = small[:half] + exchange(small[half:], "dp", mask)
    pieces = jnp.split(small[0], [sum(small_sizes[: i + 1]) for i in range(4)])
    gains, shifts, obiases, bqv, bups = [
        piece.reshape(part.shape) for piece, part in zip(pieces, small_parts)
    ]

    def stacked(make):
        return jnp.stack([make(*weight_grads[at]) for at in range(layers)])

    return (
        encoded,
        frames_grad,
        stacked(lambda qk, vo, up, down: jnp.stack([qk[:, :wide], qk[:, wide:], vo[:, :wide]], axis=1)),
        stacked(lambda qk, vo, up, down: vo[:, wide:].T),
        stacked(lambda qk, vo, up, down: up),
        stacked(lambda qk, vo, up, down: down.T),
        bqv,
        bups,
        gains,
        shifts,
        obiases,
    )


def solution(mesh):
    in_specs = (
        P("dp", "tensor", None),
        P("dp", "tensor", None),
        P(None, "dp", None, "tensor"),
        P(None, "tensor", "dp"),
        P(None, "dp", "tensor"),
        P(None, "tensor", "dp"),
        P(None, None, ("tensor", "dp")),
        P(None, ("tensor", "dp")),
        P(None, None, ("dp", "tensor")),
        P(None, None, ("dp", "tensor")),
        P(None, None, ("dp", "tensor")),
    )
    out_specs = (
        P("dp", "tensor", None),
        P("dp", "tensor", None),
        P(None, "dp", None, "tensor"),
        P(None, "tensor", "dp"),
        P(None, "dp", "tensor"),
        P(None, "tensor", "dp"),
        P(None, None, ("tensor", "dp")),
        P(None, ("tensor", "dp")),
        P(None, None, ("dp", "tensor")),
        P(None, None, ("dp", "tensor")),
        P(None, None, ("dp", "tensor")),
    )
    return jax.shard_map(local, mesh=mesh, in_specs=in_specs, out_specs=out_specs, check_vma=False)
```

```python
import functools
import math

import jax
import jax.numpy as jnp
from jax import lax
from jax.experimental import pallas as pl
from jax.experimental.pallas import tpu as pltpu
from jax.sharding import PartitionSpec as P

HD = 64
WIDE = 128
eps = 1e-05
LOG2E = 1.0 / math.log(2.0)
LN2 = math.log(2.0)
MASKED = -1e30
bf16 = jnp.bfloat16
f32 = jnp.float32


def exchange(value, axis, mask):
    count = lax.axis_size(axis)
    return lax.ppermute(value, axis, [(i, i ^ mask) for i in range(count)])


def dp_masks():
    count = lax.axis_size("dp")
    masks = []
    while count > 1:
        count //= 2
        masks.append(count)
    return masks


def relative_mask(position):
    result = 0
    for at, mask in enumerate(dp_masks()):
        result = result + ((position >> at) & 1) * mask
    return result


def together(*values):
    return lax.optimization_barrier(values)


def spread(first, second, small=None):
    masks = dp_masks()
    cut = first.shape[1]
    block = jnp.concatenate([first, second], axis=1)
    for mask in masks[:-1]:
        more = exchange(block, "dp", mask)
        if small is not None:
            more, small_more = together(more, exchange(small, "dp", mask))
            small = jnp.concatenate([small, small_more], axis=0)
        block = jnp.concatenate([block, more], axis=0)
    if small is not None:
        small = jnp.concatenate([small, exchange(small, "dp", masks[-1])], axis=0)
        small = jnp.stack([small, exchange(small, "tensor", 1)])
        small = jnp.stack([small, exchange(small, "tensor", 2)])
    first, second = block[:, :cut], block[:, cut:]
    first, second = together(first, second)
    first_more, second_other = together(
        exchange(first, "dp", masks[-1]), exchange(second, "tensor", 2)
    )
    first = jnp.concatenate([first, first_more], axis=0)
    second = jnp.stack([second, second_other])
    first, second = together(first, second)
    first_other, second_more = together(
        exchange(first, "tensor", 2), exchange(second, "dp", masks[-1])
    )
    second = [jnp.concatenate([second[i], second_more[i]], axis=0) for i in range(2)]
    return [first, first_other], second, second_other, small


def behind(values, *tokens):
    return together(*values, *tokens)[: len(values)]


def add_low(kept, received):
    return (kept.astype(f32) + received.astype(f32)).astype(bf16)


def near_one(first, second):
    mask = dp_masks()[-1]
    half = first.shape[1] // 2
    return (
        add_low(first[0], exchange(first[1], "tensor", 2)),
        add_low(second[:, :half], exchange(second[:, half:], "dp", mask)),
    )


def near_two(first, second):
    mask = dp_masks()[-1]
    half = first.shape[0] // 2
    return (
        add_low(first[:half], exchange(first[half:], "dp", mask)),
        add_low(second[0], exchange(second[1], "tensor", 2)),
    )


def far(value, masks):
    for mask in masks:
        half = value.shape[0] // 2
        value = add_low(value[:half], exchange(value[half:], "dp", mask))
    return value


class Folding:
    def __init__(self, qk, vo, up, down):
        masks = dp_masks()[-2::-1]
        self.masks = masks[:-1], masks[-1:]
        self.attn = together(qk, vo)
        self.feed = jnp.concatenate([up, down], axis=1)
        self.step = 0

    def advance(self):
        step = self.step
        self.step += 1
        if step < 2:
            attn = (near_one, near_two)[step](*self.attn)
            *attn, self.feed = together(*attn, far(self.feed, self.masks[step]))
            self.attn = attn if step == 0 else jnp.concatenate(attn, axis=1)
        else:
            (self.attn,) = together(far(self.attn, self.masks[step - 2]))

    def token(self):
        return (self.feed, self.attn) if self.step > 1 else (self.feed, *self.attn)

    def result(self):
        half, low = self.attn.shape[1] // 2, self.feed.shape[1] // 2
        parts = self.attn[:, :half], self.attn[:, half:], self.feed[:, :low], self.feed[:, low:]
        return [part.astype(f32) for part in parts]


def split_low(value):
    high = value.astype(bf16)
    rest = value - high.astype(f32)
    mid = rest.astype(bf16)
    return high, mid, (rest - mid.astype(f32)).astype(bf16)


def lane_at(rows):
    return lax.broadcasted_iota(jnp.int32, (rows, WIDE - HD), 1)


def key_extra(rows, row_count, quarter, ones):
    lane = lane_at(rows)
    row = lax.broadcasted_iota(jnp.int32, (rows, WIDE - HD), 0)
    masked = lax.rem(row, quarter) >= row_count
    bias = jnp.where(masked, MASKED, 0.0).astype(f32)
    value = jnp.where(lane == 0, bias, jnp.where(lane <= ones, 1.0, 0.0))
    return value.astype(bf16)


def ones_extra(rows, ones):
    return jnp.where(lane_at(rows) < ones, 1.0, 0.0).astype(bf16)


def widen(part, extra):
    return jnp.concatenate([part, extra], axis=1)


def nt_dot(left, right):
    return lax.dot_general(left, right, (((1,), (1,)), ((), ())), preferred_element_type=f32)


def nn_dot(left, right):
    return lax.dot_general(left, right, (((1,), (0,)), ((), ())), preferred_element_type=f32)


def tn_dot(left, right):
    return lax.dot_general(left, right, (((0,), (0,)), ((), ())), preferred_element_type=f32)


def attend_kernel(row_count, quarter, step, qk_a, v_a, qk_b, v_b, o_a, o_b, lse, q_s, k_s, v_s, o_s):
    rows = qk_a.shape[1]
    wide = v_a.shape[2]
    heads = wide // HD
    k_more = key_extra(rows, row_count, quarter, 0)
    one = ones_extra(rows, 1)
    for half, (qk, v) in enumerate(((qk_a, v_a), (qk_b, v_b))):
        at = pl.ds(half * rows, rows)
        for h in range(heads):
            low, high = h * HD, (h + 1) * HD
            q_s[h, at, :] = widen(qk[0, :, low:high], one)
            k_s[h, at, :] = widen(qk[0, :, wide + low : wide + high], k_more)
            v_s[h, at, :] = widen(v[0, :, low:high], one)

    for h in range(heads):

        def work(i, carry, h=h):
            for part in range(2):
                at = pl.ds(pl.multiple_of((2 * i + part) * step, step), step)
                scores = nt_dot(q_s[h, at, :], k_s[h])
                top = jnp.max(scores, axis=-1, keepdims=True)
                weights = jnp.exp2(scores - top).astype(bf16)
                summed = nn_dot(weights, v_s[h])
                total = summed[:, HD : HD + 1]
                o_s[at, h * HD : (h + 1) * HD] = (summed[:, :HD] / total).astype(bf16)
                lse[0, at, h : h + 1] = top + jnp.log2(total)
            return carry

        lax.fori_loop(0, rows // step, work, 0)
    o_a[0] = o_s[pl.ds(0, rows), :]
    o_b[0] = o_s[pl.ds(rows, rows), :]


def block_of(shape):
    return pl.BlockSpec((1,) + shape, lambda t: (t, 0, 0))


def attend(row_count, quarter, qk_a, v_a, qk_b, v_b):
    groups, rows, wide = v_a.shape
    heads = wide // HD
    return pl.pallas_call(
        functools.partial(attend_kernel, row_count, quarter, min(256, rows)),
        grid=(groups,),
        in_specs=[block_of((rows, 2 * wide)), block_of((rows, wide))] * 2,
        out_specs=[block_of((rows, wide))] * 2 + [block_of((2 * rows, 8))],
        out_shape=[jax.ShapeDtypeStruct((groups, rows, wide), bf16)] * 2
        + [jax.ShapeDtypeStruct((groups, 2 * rows, 8), f32)],
        scratch_shapes=[pltpu.VMEM((heads, 2 * rows, WIDE), bf16)] * 3
        + [pltpu.VMEM((2 * rows, wide), bf16)],
        compiler_params=pltpu.CompilerParams(vmem_limit_bytes=48 * 2**20),
    )(qk_a, v_a, qk_b, v_b)


def attend_back_kernel(
    row_count, quarter, step,
    qk_a, v_a, qk_b, v_b, o_a, o_b, do_a, do_b, lse,
    dqk_a, dv_a, dqk_b, dv_b,
    q_s, k_s, kt_s, v_s, do_s, dq_s, dk_s, dv_s,
):
    rows = qk_a.shape[1]
    wide = v_a.shape[2]
    heads = wide // HD
    k_more = key_extra(rows, row_count, quarter, 3)
    three = ones_extra(rows, 3)
    lane = lane_at(rows)

    def spread_lanes(first, parts):
        value = jnp.where(lane < first, 1.0, 0.0).astype(f32)
        for at, part in enumerate(parts):
            value = jnp.where(lane == first + at, part.astype(f32), value)
        return value.astype(bf16)

    for half, (qk, v, o, do) in enumerate(((qk_a, v_a, o_a, do_a), (qk_b, v_b, o_b, do_b))):
        at = pl.ds(half * rows, rows)
        for h in range(heads):
            low, high = h * HD, (h + 1) * HD
            minus_lse = split_low(-lse[0, at, h : h + 1])
            q_s[h, at, :] = widen(qk[0, :, low:high], spread_lanes(1, minus_lse))
            keys = widen(qk[0, :, wide + low : wide + high], k_more)
            k_s[h, at, :] = keys
            kt_s[h, :, at] = jnp.transpose(keys.astype(f32)).astype(bf16)
            v_s[h, at, :] = widen(v[0, :, low:high], three)
            grad = do[0, :, low:high]
            inner = jnp.sum(grad.astype(f32) * o[0, :, low:high].astype(f32), axis=1, keepdims=True)
            do_s[h, at, :] = widen(grad, spread_lanes(0, split_low(-inner)))

    dk_s[...] = jnp.zeros_like(dk_s)
    dv_s[...] = jnp.zeros_like(dv_s)
    chunks = 2 * rows // step

    def work(i, carry):
        h = i // chunks
        at = pl.ds(pl.multiple_of(lax.rem(i, chunks) * step, step), step)
        queries = q_s[h, at, :]
        grad_out = do_s[h, at, :]
        probs = jnp.exp2(nt_dot(k_s[h], queries))
        grad_scores = (probs * nt_dot(v_s[h], grad_out)).astype(bf16)
        dv_s[h] += nn_dot(probs.astype(bf16), grad_out)
        dk_s[h] += nn_dot(grad_scores, queries)
        dq_s[h, at, :] = jnp.transpose(nn_dot(kt_s[h], grad_scores))
        return carry

    lax.fori_loop(0, heads * chunks, work, 0)
    for half, (dqk, dv) in enumerate(((dqk_a, dv_a), (dqk_b, dv_b))):
        at = pl.ds(half * rows, rows)
        for h in range(heads):
            low, high = h * HD, (h + 1) * HD
            dqk[0, :, low:high] = (dq_s[h, at, :][:, :HD] * HD**-0.5).astype(bf16)
            dqk[0, :, wide + low : wide + high] = (dk_s[h, at, :][:, :HD] * LN2).astype(bf16)
            dv[0, :, low:high] = dv_s[h, at, :][:, :HD].astype(bf16)


def attend_back(group, row_count, quarter, qk_a, v_a, qk_b, v_b, o_a, o_b, do_a, do_b, lse):
    _, rows, wide = v_a.shape
    heads = wide // HD

    def block_of(shape):
        return pl.BlockSpec((1,) + shape, lambda t: (group, 0, 0))

    def out_block(shape):
        return pl.BlockSpec((1,) + shape, lambda t: (0, 0, 0))

    return pl.pallas_call(
        functools.partial(attend_back_kernel, row_count, quarter, min(256, rows)),
        grid=(1,),
        in_specs=[block_of((rows, 2 * wide)), block_of((rows, wide))] * 2
        + [block_of((rows, wide))] * 4
        + [block_of((2 * rows, 8))],
        out_specs=[out_block((rows, 2 * wide)), out_block((rows, wide))] * 2,
        out_shape=[
            jax.ShapeDtypeStruct((1, rows, 2 * wide), bf16),
            jax.ShapeDtypeStruct((1, rows, wide), bf16),
        ]
        * 2,
        scratch_shapes=[
            pltpu.VMEM((heads, 2 * rows, WIDE), bf16),
            pltpu.VMEM((heads, 2 * rows, WIDE), bf16),
            pltpu.VMEM((heads, WIDE, 2 * rows), bf16),
            pltpu.VMEM((heads, 2 * rows, WIDE), bf16),
            pltpu.VMEM((heads, 2 * rows, WIDE), bf16),
            pltpu.VMEM((heads, 2 * rows, WIDE), f32),
            pltpu.VMEM((heads, 2 * rows, WIDE), f32),
            pltpu.VMEM((heads, 2 * rows, WIDE), f32),
        ],
        compiler_params=pltpu.CompilerParams(vmem_limit_bytes=56 * 2**20),
    )(qk_a, v_a, qk_b, v_b, o_a, o_b, do_a, do_b, lse)


def normalized(value):
    centred = value - jnp.mean(value, axis=-1, keepdims=True)
    scale = lax.rsqrt(jnp.mean(centred * centred, axis=-1, keepdims=True) + eps)
    return centred * scale, scale


def norm_back(value, gain, grad):
    unit, scale = normalized(value)
    scaled = grad * gain
    result = scale * (
        scaled
        - jnp.mean(scaled, axis=-1, keepdims=True)
        - unit * jnp.mean(scaled * unit, axis=-1, keepdims=True)
    )
    return result, jnp.sum(grad * unit, axis=0), jnp.sum(grad, axis=0)


def gelu_both(value):
    share = 0.5 * (1.0 + lax.erf(value * math.sqrt(0.5)))
    density = jnp.exp(-0.5 * value * value) * (1.0 / math.sqrt(2.0 * math.pi))
    return (value * share).astype(bf16), (share + value * density).astype(bf16)


def feed_kernel(normed, base, bias, *refs):
    ups, downs, activated, slopes, total = refs[:4], refs[4:8], refs[8:12], refs[12:16], refs[16]
    rows_in = normed[...]
    for t in range(4):
        upward = nn_dot(rows_in, ups[t][...]) + bias[t : t + 1, :]
        activated[t][...], slopes[t][...] = gelu_both(upward)
    joined = jnp.concatenate([ref[...] for ref in activated], axis=1)
    down = jnp.concatenate([ref[...] for ref in downs], axis=1)
    share = nt_dot(joined, down)

    @pl.when(pl.program_id(0) == 0)
    def _():
        total[...] = base[...] + share

    @pl.when(pl.program_id(0) > 0)
    def _():
        total[...] += share


def whole_block(shape):
    return pl.BlockSpec(shape, lambda j: (0, 0))


def column_block(rows, step):
    return pl.BlockSpec((rows, step), lambda j: (0, j))


def feed(normed, base, bias, ups, downs):
    rows, width = normed.shape
    hidden = bias.shape[1]
    step = min(256, hidden)
    return pl.pallas_call(
        feed_kernel,
        grid=(hidden // step,),
        in_specs=[whole_block((rows, width))] * 2
        + [column_block(4, step)]
        + [column_block(width, step)] * 8,
        out_specs=[column_block(rows, step)] * 8 + [whole_block((rows, width))],
        out_shape=[jax.ShapeDtypeStruct((rows, hidden), bf16)] * 8
        + [jax.ShapeDtypeStruct((rows, width), f32)],
        compiler_params=pltpu.CompilerParams(vmem_limit_bytes=56 * 2**20),
    )(normed, base, bias, *ups, *downs)


def feed_back_kernel(normed, grad, *refs):
    ups, downs, activated, slopes = refs[:4], refs[4:8], refs[8:12], refs[12:16]
    own, other, bias_grad, total, normed_t, grad_t = refs[16:]

    @pl.when(pl.program_id(0) == 0)
    def _():
        normed_t[...] = jnp.transpose(normed[...].astype(f32)).astype(bf16)
        grad_t[...] = jnp.transpose(grad[...].astype(f32)).astype(bf16)

    grad_rows = grad[...]
    grad_ups = []
    for t in range(4):
        grad_act = nn_dot(grad_rows, downs[t][...])
        scaled = grad_act * slopes[t][...].astype(f32)
        grad_ups.append(scaled.astype(bf16))
        bias_grad[t : t + 1, :] = jnp.sum(scaled, axis=0, keepdims=True)
        dest = (own, other)[t % 2]
        dest[t // 2] = nn_dot(normed_t[...], grad_ups[t]).astype(bf16)
        dest[2 + t // 2] = nn_dot(grad_t[...], activated[t][...]).astype(bf16)
    joined = jnp.concatenate(grad_ups, axis=1)
    up = jnp.concatenate([ref[...] for ref in ups], axis=1)
    share = nt_dot(joined, up)

    @pl.when(pl.program_id(0) == 0)
    def _():
        total[...] = share

    @pl.when(pl.program_id(0) > 0)
    def _():
        total[...] += share


def feed_back(normed, grad, ups, downs, activated, slopes):
    rows, width = normed.shape
    hidden = activated[0].shape[1]
    step = min(256, hidden)
    stack = pl.BlockSpec((4, width, step), lambda j: (0, 0, j))
    return pl.pallas_call(
        feed_back_kernel,
        grid=(hidden // step,),
        in_specs=[whole_block((rows, width))] * 2
        + [column_block(width, step)] * 8
        + [column_block(rows, step)] * 8,
        out_specs=[stack] * 2 + [column_block(4, step), whole_block((rows, width))],
        out_shape=[jax.ShapeDtypeStruct((4, width, hidden), bf16)] * 2
        + [jax.ShapeDtypeStruct((4, hidden), f32), jax.ShapeDtypeStruct((rows, width), f32)],
        scratch_shapes=[pltpu.VMEM((width, rows), bf16)] * 2,
        compiler_params=pltpu.CompilerParams(vmem_limit_bytes=60 * 2**20),
    )(normed, grad, *ups, *downs, *activated, *slopes)


def local(
    frames,
    cotangent,
    qkv_weight,
    out_weight,
    up_weight,
    down_weight,
    qv_bias,
    up_bias,
    norm_gains,
    norm_shifts,
    out_biases,
):
    layers, block = qkv_weight.shape[:2]
    wide = qkv_weight.shape[3]
    row_count, width = frames.shape[1:]
    hidden = up_weight.shape[2]
    quarter = -(-row_count // 128) * 128
    rows = 2 * quarter
    count_dp = lax.axis_size("dp")
    me = lax.axis_index("dp")
    t_me = lax.axis_index("tensor")
    y_me = t_me // 2
    t_order = jnp.arange(4) ^ t_me
    positions = jnp.arange(count_dp)
    block_at = relative_mask(positions) ^ me
    place_of = jnp.argmax(block_at[None, :] == positions[:, None], axis=1)

    small_parts = (norm_gains, norm_shifts, out_biases, qv_bias, up_bias)
    small_sizes = [part.size for part in small_parts]
    small = jnp.concatenate([part.reshape(1, -1) for part in small_parts], axis=1)

    source = jnp.repeat(block_at, block) * block + jnp.tile(jnp.arange(block), count_dp)
    to_relative = (jnp.arange(width)[:, None] == source[None, :]).astype(bf16)

    def take_clip(value):
        mine = lax.dynamic_index_in_dim(value, y_me, 0, keepdims=False)
        theirs = exchange(lax.dynamic_index_in_dim(value, 1 - y_me, 0, keepdims=False), "tensor", 2)
        padding = ((0, 0), (0, quarter - row_count), (0, 0))
        both = jnp.pad(jnp.stack([mine, theirs]), padding).reshape(rows, width)
        return nn_dot(both, to_relative)

    def give_clip(value):
        mine, theirs = value[:quarter], value[quarter:].astype(bf16)
        theirs = nt_dot(exchange(theirs, "tensor", 2), to_relative)[:row_count]
        high = mine.astype(bf16)
        low = (mine - high.astype(f32)).astype(bf16)
        mine = (nt_dot(high, to_relative) + nt_dot(low, to_relative))[:row_count]
        first = y_me == 0
        return jnp.stack([jnp.where(first, mine, theirs), jnp.where(first, theirs, mine)])

    current = take_clip(frames)
    gradient = take_clip(cotangent)

    def attn_blocks(at):
        qk = jnp.concatenate([qkv_weight[at, :, 0], qkv_weight[at, :, 1]], axis=1)
        return qk, jnp.concatenate([qkv_weight[at, :, 2], out_weight[at].T], axis=1)

    def feed_blocks(at):
        return up_weight[at], down_weight[at].T

    def attn_weights(qk, vo):
        vo = jnp.stack(vo)
        return jnp.stack(qk), vo[:, :, :wide], vo[:, :, wide:]

    def feed_weights(ups, downs):
        ups = [ups[0], exchange(ups[0], "tensor", 1), ups[1], exchange(ups[1], "tensor", 1)]
        downs = [
            downs[0], exchange(downs[0], "tensor", 1), downs[1], exchange(downs[1], "tensor", 1)
        ]
        return ups, downs

    qk, vo, token, small = spread(*attn_blocks(0), small)
    weights = [attn_weights(qk, vo)]
    ups, downs, token, _ = spread(*behind(feed_blocks(0), token))
    weights[0] += feed_weights(ups, downs)
    for at in range(1, layers):
        (up, down), (qk, vo) = feed_blocks(at), attn_blocks(at)
        first, second = jnp.concatenate([up, qk], axis=1), jnp.concatenate([down, vo], axis=1)
        first, second, token, _ = spread(*behind((first, second), token))
        weights.append(
            attn_weights([part[:, hidden:] for part in first], [part[:, hidden:] for part in second])
            + feed_weights(
                [part[:, :hidden] for part in first], [part[:, :hidden] for part in second]
            )
        )

    small = small.reshape(4, count_dp, -1)
    by_part = jnp.split(small, [sum(small_sizes[: i + 1]) for i in range(4)], axis=2)

    def by_width(part):
        part = jnp.take(part, t_order, axis=0).reshape(4, count_dp, layers, 2, -1)
        return part.transpose(2, 3, 1, 0, 4).reshape(layers, 2, width)

    gain_all, shift_all, obias_all = [by_width(part) for part in by_part[:3]]
    qv_all = jnp.take(by_part[3][0::2], place_of, axis=1).reshape(2, count_dp, layers, 2, -1)
    qv_all = qv_all.transpose(2, 3, 0, 1, 4).reshape(layers, 2, 2, wide)
    up_all = jnp.take(by_part[4], place_of, axis=1).reshape(4, count_dp, layers, -1)
    up_all = up_all.transpose(2, 0, 1, 3).reshape(layers, 4, hidden)

    def project(value, weight):
        return jnp.einsum("fd,tdk->tfk", value, weight, preferred_element_type=f32)

    saved = []
    q_scale = HD**-0.5 * LOG2E
    for at in range(layers):
        w_qk, w_v, w_o, w_up, w_down = weights[at]
        unit, _ = normalized(current)
        normed_a = (unit * gain_all[at, 0] + shift_all[at, 0]).astype(bf16)
        normed_b = exchange(normed_a, "tensor", 1)
        qk_scale = jnp.where(jnp.arange(2 * wide) < wide, q_scale, 1.0)
        qk_bias = jnp.concatenate([qv_all[at, 0], jnp.zeros_like(qv_all[at, 0])], axis=1)

        def heads_of(normed):
            qk = ((project(normed, w_qk) + qk_bias[:, None]) * qk_scale).astype(bf16)
            v = (project(normed, w_v) + qv_all[at, 1][:, None]).astype(bf16)
            return qk, v

        qk_a, v_a = heads_of(normed_a)
        qk_b, v_b = heads_of(normed_b)
        o_a, o_b, lse = attend(row_count, quarter, qk_a, v_a, qk_b, v_b)
        share_b = nt_dot(o_b[0], w_o[0]) + nt_dot(o_b[1], w_o[1])
        share_b = exchange(share_b.astype(bf16), "tensor", 1)
        share_a = nt_dot(o_a[0], w_o[0]) + nt_dot(o_a[1], w_o[1])
        middle = current + (share_a + share_b.astype(f32) + obias_all[at, 0])
        unit, _ = normalized(middle)
        normed_two = (unit * gain_all[at, 1] + shift_all[at, 1]).astype(bf16)
        fed = feed(normed_two, middle + obias_all[at, 1], up_all[at], w_up, w_down)
        saved.append(
            (current, normed_a, normed_b, qk_a, v_a, qk_b, v_b, o_a, o_b, lse, middle, normed_two, fed[:4], fed[4:8])
        )
        current = fed[8]
    encoded = give_clip(current)

    small_grads = [None] * layers
    weight_grads = [None] * layers
    folding = None
    for at in reversed(range(layers)):
        w_qk, w_v, w_o, w_up, w_down = weights[at]
        (layer_in, normed_a, normed_b, qk_a, v_a, qk_b, v_b, o_a, o_b, lse, middle, normed_two, activated, slopes) = saved[at]
        grad_feed = gradient.astype(bf16)
        obias_two = jnp.sum(grad_feed, axis=0, dtype=f32)
        if folding is not None:
            folding.advance()
            (grad_feed,) = behind((grad_feed,), *folding.token())
        dw_feed, dw_other, bup, grad_normed = feed_back(
            normed_two, grad_feed, w_up, w_down, activated, slopes
        )
        dw_feed = add_low(dw_feed, exchange(dw_other, "tensor", 1))

        grad_middle, gain_two, shift_two = norm_back(middle, gain_all[at, 1], grad_normed)
        gradient = gradient + grad_middle
        branch_a = gradient.astype(bf16)
        branch_b = exchange(branch_a, "tensor", 1)
        obias_one = jnp.sum(branch_a, axis=0, dtype=f32)
        do_a = project(branch_a, w_o).astype(bf16)
        do_b = project(branch_b, w_o).astype(bf16)
        parts = []
        for t in range(2):
            if folding is not None:
                folding.advance()
                do_a, do_b = behind((do_a, do_b), *folding.token())
            feed_state = (dw_feed,) if t == 0 else dw_feed
            ready = behind((do_a, do_b), *feed_state, *[part[0] for part in parts])
            parts.append(
                attend_back(t, row_count, quarter, qk_a, v_a, qk_b, v_b, o_a, o_b, *ready, lse)
            )
            dw_feed = near_two(*dw_feed) if t else near_one(dw_feed[:2], dw_feed[2:])
        if folding is not None:
            folding.advance()
            parts[1] = behind(parts[1], *dw_feed, *folding.token())
            weight_grads[at + 1] = folding.result()
        else:
            parts[1] = behind(parts[1], *dw_feed)
        dqk_a, dv_a, dqk_b, dv_b = [[parts[t][i][0] for t in range(2)] for i in range(4)]

        def back_normed(dqk, dv):
            return sum(nt_dot(dqk[t], w_qk[t]) + nt_dot(dv[t], w_v[t]) for t in range(2))

        share_b = exchange(back_normed(dqk_b, dv_b).astype(bf16), "tensor", 1)
        grad_normed = back_normed(dqk_a, dv_a) + share_b.astype(f32)
        dw_qk = jnp.stack(
            [
                (tn_dot(normed_a, dqk_a[t]) + tn_dot(normed_b, dqk_b[t])).astype(bf16)
                for t in range(2)
            ]
        )
        dw_vo = jnp.stack(
            [
                jnp.concatenate(
                    [
                        (tn_dot(normed_a, dv_a[t]) + tn_dot(normed_b, dv_b[t])).astype(bf16),
                        (tn_dot(branch_a, o_a[t]) + tn_dot(branch_b, o_b[t])).astype(bf16),
                    ],
                    axis=1,
                )
                for t in range(2)
            ]
        )
        folding = Folding(dw_qk, dw_vo, *dw_feed)
        bq = jnp.stack(
            [
                jnp.sum(dqk_a[t][:, :wide], axis=0, dtype=f32)
                + jnp.sum(dqk_b[t][:, :wide], axis=0, dtype=f32)
                for t in range(2)
            ]
        )
        bv = jnp.stack(
            [
                jnp.sum(dv_a[t], axis=0, dtype=f32) + jnp.sum(dv_b[t], axis=0, dtype=f32)
                for t in range(2)
            ]
        )
        grad_in, gain_one, shift_one = norm_back(layer_in, gain_all[at, 0], grad_normed)
        gradient = gradient + grad_in
        small_grads[at] = (
            jnp.stack([gain_one, gain_two]),
            jnp.stack([shift_one, shift_two]),
            jnp.stack([obias_one, obias_two]),
            jnp.stack([bq, bv]),
            bup,
        )
    for step in range(4):
        if step == 2:
            (folding.attn,) = behind((folding.attn,), gradient)
        folding.advance()
    weight_grads[0] = folding.result()
    frames_grad = give_clip(gradient)

    gains, shifts, obiases, bqv, bups = [
        jnp.stack([small_grads[at][i] for at in range(layers)]) for i in range(5)
    ]

    def from_width(part):
        part = part.reshape(layers, 2, count_dp, 4, -1).transpose(3, 2, 0, 1, 4)
        return jnp.take(part.reshape(4, count_dp, -1), t_order, axis=0)

    bqv = bqv.reshape(layers, 2, 2, count_dp, -1).transpose(2, 3, 0, 1, 4)
    bqv = jnp.take(bqv.reshape(2, count_dp, -1), block_at, axis=1)
    bqv = jnp.stack([bqv, jnp.zeros_like(bqv)], axis=1).reshape(4, count_dp, -1)
    bups = bups.reshape(layers, 4, count_dp, -1).transpose(1, 2, 0, 3)
    bups = jnp.take(bups.reshape(4, count_dp, -1), block_at, axis=1)
    small = jnp.concatenate(
        [from_width(gains), from_width(shifts), from_width(obiases), bqv, bups], axis=2
    )
    small = small.reshape(2, 2, count_dp, -1)
    small = small[0] + exchange(small[1], "tensor", 2)
    small = small[0] + exchange(small[1], "tensor", 1)
    for mask in reversed(dp_masks()):
        half = small.shape[0] // 2
        small = small[:half] + exchange(small[half:], "dp", mask)
    pieces = jnp.split(small[0], [sum(small_sizes[: i + 1]) for i in range(4)])
    gains, shifts, obiases, bqv, bups = [
        piece.reshape(part.shape) for piece, part in zip(pieces, small_parts)
    ]

    def stacked(make):
        return jnp.stack([make(*weight_grads[at]) for at in range(layers)])

    return (
        encoded,
        frames_grad,
        stacked(lambda qk, vo, up, down: jnp.stack([qk[:, :wide], qk[:, wide:], vo[:, :wide]], axis=1)),
        stacked(lambda qk, vo, up, down: vo[:, wide:].T),
        stacked(lambda qk, vo, up, down: up),
        stacked(lambda qk, vo, up, down: down.T),
        bqv,
        bups,
        gains,
        shifts,
        obiases,
    )


def solution(mesh):
    in_specs = (
        P("dp", "tensor", None),
        P("dp", "tensor", None),
        P(None, "dp", None, "tensor"),
        P(None, "tensor", "dp"),
        P(None, "dp", "tensor"),
        P(None, "tensor", "dp"),
        P(None, None, ("tensor", "dp")),
        P(None, ("tensor", "dp")),
        P(None, None, ("dp", "tensor")),
        P(None, None, ("dp", "tensor")),
        P(None, None, ("dp", "tensor")),
    )
    out_specs = (
        P("dp", "tensor", None),
        P("dp", "tensor", None),
        P(None, "dp", None, "tensor"),
        P(None, "tensor", "dp"),
        P(None, "dp", "tensor"),
        P(None, "tensor", "dp"),
        P(None, None, ("tensor", "dp")),
        P(None, ("tensor", "dp")),
        P(None, None, ("dp", "tensor")),
        P(None, None, ("dp", "tensor")),
        P(None, None, ("dp", "tensor")),
    )
    return jax.shard_map(local, mesh=mesh, in_specs=in_specs, out_specs=out_specs, check_vma=False)
```

```python
import functools
import math

import jax
import jax.numpy as jnp
from jax import lax
from jax.experimental import pallas as pl
from jax.experimental.pallas import tpu as pltpu
from jax.sharding import PartitionSpec as P

HD = 64
WIDE = 128
eps = 1e-05
LOG2E = 1.0 / math.log(2.0)
LN2 = math.log(2.0)
MASKED = -1e30
bf16 = jnp.bfloat16
f32 = jnp.float32


def exchange(value, axis, mask):
    count = lax.axis_size(axis)
    return lax.ppermute(value, axis, [(i, i ^ mask) for i in range(count)])


def dp_masks():
    count = lax.axis_size("dp")
    masks = []
    while count > 1:
        count //= 2
        masks.append(count)
    return masks


def relative_mask(position):
    result = 0
    for at, mask in enumerate(dp_masks()):
        result = result + ((position >> at) & 1) * mask
    return result


def together(*values):
    return lax.optimization_barrier(values)


def gather_steps(first, second):
    masks = dp_masks()
    cut = first.shape[1]

    def z_step(mask):
        def step(state):
            return (jnp.concatenate([state[0], exchange(state[0], "dp", mask)], axis=0),)

        return step

    def near(state):
        first, second = state[0][:, :cut], state[0][:, cut:]
        first, second = together(first, second)
        first_more, other = exchange(first, "dp", masks[-1]), exchange(second, "tensor", 2)
        return jnp.concatenate([first, first_more], axis=0), jnp.stack([second, other])

    def last(state):
        first, second = state
        other, more = exchange(first, "tensor", 2), exchange(second, "dp", masks[-1])
        second = [jnp.concatenate([second[i], more[i]], axis=0) for i in range(2)]
        return first, other, *second

    start = (jnp.concatenate([first, second], axis=1),)
    return start, [z_step(mask) for mask in masks[:-1]], [near, last]


class Gathering:
    def __init__(self, groups):
        made = [gather_steps(*group) for group in groups]
        self.states = [start for start, _, _ in made]
        self.plan = [[(0, step)] for step in made[0][1]]
        for at, (_, _, near) in enumerate(made):
            ahead = made[at + 1][1] if at + 1 < len(made) else []
            count = max(len(near), len(ahead))
            for i in range(count):
                stage = [(at, near[i])] if i < len(near) else []
                self.plan.append(stage + ([(at + 1, ahead[i])] if i < len(ahead) else []))
        self.ends = []
        for at in range(len(made)):
            self.ends.append(max(i for i, stage in enumerate(self.plan) for g, _ in stage if g == at))
        self.done = 0

    def advance(self, *others):
        stage = self.plan[self.done]
        self.done += 1
        results = [step(self.states[g]) for g, step in stage]
        flat = [part for result in results for part in result]
        flat = together(*flat, *others)
        at = 0
        for (g, _), result in zip(stage, results):
            self.states[g] = flat[at : at + len(result)]
            at += len(result)
        self.token = flat[0]
        return flat[at:]

    def until(self, group):
        while self.done <= self.ends[group]:
            self.advance()
        return self.states[group]


def behind(values, *tokens):
    return together(*values, *tokens)[: len(values)]


def add_low(kept, received):
    return (kept.astype(f32) + received.astype(f32)).astype(bf16)


def near_one(first, second):
    mask = dp_masks()[-1]
    half = first.shape[1] // 2
    return (
        add_low(first[0], exchange(first[1], "tensor", 2)),
        add_low(second[:, :half], exchange(second[:, half:], "dp", mask)),
    )


def near_core(own, received):
    mask = dp_masks()[-1]
    half = own.shape[1] // 2
    sent = together(add_low(own[1], received[1]), add_low(own[2:, half:], received[2:, half:]))

    def finish():
        first, second = exchange(sent[0], "tensor", 2), exchange(sent[1], "dp", mask)
        first = own[0].astype(f32) + received[0].astype(f32) + first.astype(f32)
        kept = own[2:, :half].astype(f32) + received[2:, :half].astype(f32)
        return first.astype(bf16), (kept + second.astype(f32)).astype(bf16)

    return sent, finish


def near_two(first, second):
    mask = dp_masks()[-1]
    half = first.shape[0] // 2
    return (
        add_low(first[:half], exchange(first[half:], "dp", mask)),
        add_low(second[0], exchange(second[1], "tensor", 2)),
    )


def far(value, masks):
    for mask in masks:
        half = value.shape[0] // 2
        value = add_low(value[:half], exchange(value[half:], "dp", mask))
    return value


class Folding:
    def __init__(self, qk, vo, up, down):
        masks = dp_masks()[-2::-1]
        self.masks = masks[:-1], masks[-1:]
        self.attn = together(qk, vo)
        self.feed = jnp.concatenate([up, down], axis=1)
        self.step = 0

    def advance(self):
        step = self.step
        self.step += 1
        if step < 2:
            attn = (near_one, near_two)[step](*self.attn)
            *attn, self.feed = together(*attn, far(self.feed, self.masks[step]))
            self.attn = attn if step == 0 else jnp.concatenate(attn, axis=1)
        else:
            (self.attn,) = together(far(self.attn, self.masks[step - 2]))

    def token(self):
        return (self.feed, self.attn) if self.step > 1 else (self.feed, *self.attn)

    def result(self):
        half, low = self.attn.shape[1] // 2, self.feed.shape[1] // 2
        parts = self.attn[:, :half], self.attn[:, half:], self.feed[:, :low], self.feed[:, low:]
        return [part.astype(f32) for part in parts]


def split_low(value):
    high = value.astype(bf16)
    rest = value - high.astype(f32)
    mid = rest.astype(bf16)
    return high, mid, (rest - mid.astype(f32)).astype(bf16)


def lane_at(rows):
    return lax.broadcasted_iota(jnp.int32, (rows, WIDE - HD), 1)


def key_extra(rows, row_count, quarter, ones):
    lane = lane_at(rows)
    row = lax.broadcasted_iota(jnp.int32, (rows, WIDE - HD), 0)
    masked = lax.rem(row, quarter) >= row_count
    bias = jnp.where(masked, MASKED, 0.0).astype(f32)
    value = jnp.where(lane == 0, bias, jnp.where(lane <= ones, 1.0, 0.0))
    return value.astype(bf16)


def ones_extra(rows, ones):
    return jnp.where(lane_at(rows) < ones, 1.0, 0.0).astype(bf16)


def widen(part, extra):
    return jnp.concatenate([part, extra], axis=1)


def nt_dot(left, right):
    return lax.dot_general(left, right, (((1,), (1,)), ((), ())), preferred_element_type=f32)


def nn_dot(left, right):
    return lax.dot_general(left, right, (((1,), (0,)), ((), ())), preferred_element_type=f32)


def tn_dot(left, right):
    return lax.dot_general(left, right, (((0,), (0,)), ((), ())), preferred_element_type=f32)


def whole(shape):
    return pl.BlockSpec(shape, lambda j: (0,) * len(shape))


def attend_kernel(row_count, quarter, step, first, *refs):
    normed_a, normed_b, w_qk, w_vo, bias = refs[:5]
    before = () if first else refs[5:7]
    share_a, share_b, qkv, o, lse, q_s, k_s, v_s = refs[5 + len(before) :]
    rows = normed_a.shape[0]
    wide = o.shape[1]
    heads = wide // HD
    k_more = key_extra(rows, row_count, quarter, 0)
    one = ones_extra(rows, 1)
    lane = lax.broadcasted_iota(jnp.int32, (1, 2 * wide), 1)
    scale = jnp.where(lane < wide, HD**-0.5 * LOG2E, 1.0)
    for half, normed in enumerate((normed_a, normed_b)):
        at = pl.ds(half * rows, rows)
        qk = ((nn_dot(normed[...], w_qk[...]) + bias[0:1, :]) * scale).astype(bf16)
        v = (nn_dot(normed[...], w_vo[:, :wide]) + bias[1:2, :wide]).astype(bf16)
        qkv[at, : 2 * wide] = qk
        qkv[at, 2 * wide :] = v
        for h in range(heads):
            low, high = h * HD, (h + 1) * HD
            q_s[h, at, :] = widen(qk[:, low:high], one)
            k_s[h, at, :] = widen(qk[:, wide + low : wide + high], k_more)
            v_s[h, at, :] = widen(v[:, low:high], one)

    for h in range(heads):

        def work(i, carry, h=h):
            for part in range(2):
                at = pl.ds(pl.multiple_of((2 * i + part) * step, step), step)
                scores = nt_dot(q_s[h, at, :], k_s[h])
                top = jnp.max(scores, axis=-1, keepdims=True)
                weights = jnp.exp2(scores - top).astype(bf16)
                summed = nn_dot(weights, v_s[h])
                total = summed[:, HD : HD + 1]
                o[at, h * HD : (h + 1) * HD] = (summed[:, :HD] / total).astype(bf16)
                lse[at, h : h + 1] = top + jnp.log2(total)
            return carry

        lax.fori_loop(0, rows // step, work, 0)
    w_o = w_vo[:, wide:]
    part_a = nt_dot(o[pl.ds(0, rows), :], w_o)
    part_b = nt_dot(o[pl.ds(rows, rows), :], w_o)
    if not first:
        part_a = part_a + before[0][...]
        part_b = part_b + before[1][...]
    share_a[...] = part_a
    share_b[...] = part_b.astype(share_b.dtype)


def attend(row_count, quarter, normed_a, normed_b, w_qk, w_vo, bias, before):
    rows, width = normed_a.shape
    wide = w_qk.shape[1] // 2
    heads = wide // HD
    operands = (normed_a, normed_b, w_qk, w_vo, bias, *before)
    outs = [
        jax.ShapeDtypeStruct((rows, width), f32),
        jax.ShapeDtypeStruct((rows, width), bf16 if before else f32),
        jax.ShapeDtypeStruct((2 * rows, 3 * wide), bf16),
        jax.ShapeDtypeStruct((2 * rows, wide), bf16),
        jax.ShapeDtypeStruct((2 * rows, 8), f32),
    ]
    return pl.pallas_call(
        functools.partial(attend_kernel, row_count, quarter, min(256, rows), not before),
        grid=(1,),
        in_specs=[whole(part.shape) for part in operands],
        out_specs=[whole(part.shape) for part in outs],
        out_shape=outs,
        scratch_shapes=[pltpu.VMEM((heads, 2 * rows, WIDE), bf16)] * 3,
        compiler_params=pltpu.CompilerParams(vmem_limit_bytes=56 * 2**20),
    )(*operands)


def attend_back_kernel(row_count, quarter, step, first, *refs):
    branch_a, branch_b, w_qk, w_vo, qkv, o, lse = refs[:7]
    before = () if first else refs[7:9]
    dn_a, dn_b, dqkv, q_s, k_s, kt_s, v_s, do_s, dq_s, dk_s, dv_s = refs[7 + len(before) :]
    rows = branch_a.shape[0]
    wide = o.shape[1]
    heads = wide // HD
    k_more = key_extra(rows, row_count, quarter, 3)
    three = ones_extra(rows, 3)
    lane = lane_at(rows)

    def spread_lanes(first, parts):
        value = jnp.where(lane < first, 1.0, 0.0).astype(f32)
        for at, part in enumerate(parts):
            value = jnp.where(lane == first + at, part.astype(f32), value)
        return value.astype(bf16)

    for half, branch in enumerate((branch_a, branch_b)):
        at = pl.ds(half * rows, rows)
        grad_all = nn_dot(branch[...], w_vo[:, wide:]).astype(bf16)
        for h in range(heads):
            low, high = h * HD, (h + 1) * HD
            minus_lse = split_low(-lse[at, h : h + 1])
            q_s[h, at, :] = widen(qkv[at, low:high], spread_lanes(1, minus_lse))
            keys = widen(qkv[at, wide + low : wide + high], k_more)
            k_s[h, at, :] = keys
            kt_s[h, :, at] = jnp.transpose(keys.astype(f32)).astype(bf16)
            v_s[h, at, :] = widen(qkv[at, 2 * wide + low : 2 * wide + high], three)
            grad = grad_all[:, low:high]
            inner = jnp.sum(grad.astype(f32) * o[at, low:high].astype(f32), axis=1, keepdims=True)
            do_s[h, at, :] = widen(grad, spread_lanes(0, split_low(-inner)))

    dk_s[...] = jnp.zeros_like(dk_s)
    dv_s[...] = jnp.zeros_like(dv_s)
    chunks = 2 * rows // step

    def work(i, carry):
        h = i // chunks
        at = pl.ds(pl.multiple_of(lax.rem(i, chunks) * step, step), step)
        queries = q_s[h, at, :]
        grad_out = do_s[h, at, :]
        probs = jnp.exp2(nt_dot(k_s[h], queries))
        grad_scores = (probs * nt_dot(v_s[h], grad_out)).astype(bf16)
        dv_s[h] += nn_dot(probs.astype(bf16), grad_out)
        dk_s[h] += nn_dot(grad_scores, queries)
        dq_s[h, at, :] = jnp.transpose(nn_dot(kt_s[h], grad_scores))
        return carry

    lax.fori_loop(0, heads * chunks, work, 0)
    for h in range(heads):
        low, high = h * HD, (h + 1) * HD
        dqkv[:, low:high] = (dq_s[h][:, :HD] * HD**-0.5).astype(bf16)
        dqkv[:, wide + low : wide + high] = (dk_s[h][:, :HD] * LN2).astype(bf16)
        dqkv[:, 2 * wide + low : 2 * wide + high] = dv_s[h][:, :HD].astype(bf16)
    for half, dest in enumerate((dn_a, dn_b)):
        at = pl.ds(half * rows, rows)
        part = nt_dot(dqkv[at, : 2 * wide], w_qk[...])
        part = part + nt_dot(dqkv[at, 2 * wide :], w_vo[:, :wide])
        if not first:
            part = part + before[half][...]
        dest[...] = part.astype(dest.dtype)


def attend_back(row_count, quarter, branch_a, branch_b, w_qk, w_vo, qkv, o, lse, before):
    rows, width = branch_a.shape
    wide = o.shape[1]
    heads = wide // HD
    operands = (branch_a, branch_b, w_qk, w_vo, qkv, o, lse, *before)
    outs = [
        jax.ShapeDtypeStruct((rows, width), f32),
        jax.ShapeDtypeStruct((rows, width), bf16 if before else f32),
        jax.ShapeDtypeStruct((2 * rows, 3 * wide), bf16),
    ]
    return pl.pallas_call(
        functools.partial(attend_back_kernel, row_count, quarter, min(256, rows), not before),
        grid=(1,),
        in_specs=[whole(part.shape) for part in operands],
        out_specs=[whole(part.shape) for part in outs],
        out_shape=outs,
        scratch_shapes=[
            pltpu.VMEM((heads, 2 * rows, WIDE), bf16),
            pltpu.VMEM((heads, 2 * rows, WIDE), bf16),
            pltpu.VMEM((heads, WIDE, 2 * rows), bf16),
            pltpu.VMEM((heads, 2 * rows, WIDE), bf16),
            pltpu.VMEM((heads, 2 * rows, WIDE), bf16),
            pltpu.VMEM((heads, 2 * rows, WIDE), f32),
            pltpu.VMEM((heads, 2 * rows, WIDE), f32),
            pltpu.VMEM((heads, 2 * rows, WIDE), f32),
        ],
        compiler_params=pltpu.CompilerParams(vmem_limit_bytes=60 * 2**20),
    )(*operands)


def normalized(value):
    centred = value - jnp.mean(value, axis=-1, keepdims=True)
    scale = lax.rsqrt(jnp.mean(centred * centred, axis=-1, keepdims=True) + eps)
    return centred * scale, scale


def norm_back(value, gain, grad):
    unit, scale = normalized(value)
    scaled = grad * gain
    result = scale * (
        scaled
        - jnp.mean(scaled, axis=-1, keepdims=True)
        - unit * jnp.mean(scaled * unit, axis=-1, keepdims=True)
    )
    sums = [jnp.sum(part, axis=0, keepdims=True) for part in (grad * unit, grad)]
    return result, *sums


def gelu_both(value):
    share = 0.5 * (1.0 + lax.erf(value * math.sqrt(0.5)))
    density = jnp.exp(-0.5 * value * value) * (1.0 / math.sqrt(2.0 * math.pi))
    return (value * share).astype(bf16), (share + value * density).astype(bf16)


def feed_kernel(final, *refs):
    current, share_a, share_b, vectors, bias = refs[:5]
    ups, downs, activated, slopes = [refs[5 + 4 * i : 9 + 4 * i] for i in range(4)]
    middle, normed, total = refs[21:24]
    j = pl.program_id(0)

    @pl.when(j == 0)
    def _():
        value = current[...] + (share_a[...] + share_b[...].astype(f32) + vectors[0:1, :])
        middle[...] = value
        normed[...] = (normalized(value)[0] * vectors[1:2, :] + vectors[2:3, :]).astype(bf16)
        total[...] = value + vectors[3:4, :]

    rows_in = normed[...]
    for t in range(4):
        upward = nn_dot(rows_in, ups[t][...]) + bias[t : t + 1, :]
        activated[t][...], slopes[t][...] = gelu_both(upward)
    joined = jnp.concatenate([ref[...] for ref in activated], axis=1)
    down = jnp.concatenate([ref[...] for ref in downs], axis=1)
    total[...] += nt_dot(joined, down)
    if not final:
        following = refs[24]

        @pl.when(j == pl.num_programs(0) - 1)
        def _():
            unit, _ = normalized(total[...])
            following[...] = (unit * vectors[4:5, :] + vectors[5:6, :]).astype(bf16)


def single(shape):
    return pl.BlockSpec(shape, lambda j: (0,) * len(shape), pipeline_mode=pl.Buffered(1))


def column_block(rows, step):
    return pl.BlockSpec((rows, step), lambda j: (0, j))


def feed(final, current, share_a, share_b, vectors, bias, ups, downs):
    rows, width = current.shape
    hidden = bias.shape[1]
    step = min(256, hidden)
    rest = [f32, bf16, f32] if final else [f32, bf16, f32, bf16]
    fronts = (current, share_a, share_b, vectors)
    return pl.pallas_call(
        functools.partial(feed_kernel, final),
        grid=(hidden // step,),
        in_specs=[single(part.shape) for part in fronts]
        + [column_block(4, step)]
        + [column_block(width, step)] * 8,
        out_specs=[column_block(rows, step)] * 8 + [whole((rows, width))] * len(rest),
        out_shape=[jax.ShapeDtypeStruct((rows, hidden), bf16)] * 8
        + [jax.ShapeDtypeStruct((rows, width), kind) for kind in rest],
        compiler_params=pltpu.CompilerParams(vmem_limit_bytes=60 * 2**20),
    )(*fronts, bias, *ups, *downs)


def feed_back_kernel(final, *refs):
    count = 1 if final else 4
    fronts, refs = refs[:count], refs[count:]
    middle, normed, vectors = refs[:3]
    ups, downs, activated, slopes = [refs[3 + 4 * i : 7 + 4 * i] for i in range(4)]
    own, other, bias_grad, grad_out, branch, sums = refs[19:25]
    total, grad, grad_low, normed_t, grad_t = refs[25:]
    j = pl.program_id(0)

    @pl.when(j == 0)
    def _():
        sums[...] = jnp.zeros_like(sums)
        if final:
            value = fronts[0][...].astype(f32)
        else:
            above, layer_out, share_a, share_b = fronts
            grad_normed = share_a[...] + share_b[...].astype(f32)
            value, gain_one, shift_one = norm_back(layer_out[...], vectors[1:2, :], grad_normed)
            value = value + above[...]
            sums[4:5, :], sums[5:6, :] = gain_one, shift_one
        grad[...] = value
        low = value.astype(bf16)
        grad_low[...] = low
        sums[0:1, :] = jnp.sum(low.astype(f32), axis=0, keepdims=True)
        normed_t[...] = jnp.transpose(normed[...].astype(f32)).astype(bf16)
        grad_t[...] = jnp.transpose(low.astype(f32)).astype(bf16)
        total[...] = jnp.zeros_like(total)

    grad_rows = grad_low[...]
    grad_ups = []
    for t in range(4):
        grad_act = nn_dot(grad_rows, downs[t][...])
        scaled = grad_act * slopes[t][...].astype(f32)
        grad_ups.append(scaled.astype(bf16))
        bias_grad[t : t + 1, :] = jnp.sum(scaled, axis=0, keepdims=True)
        dest = (own, other)[t % 2]
        dest[t // 2] = nn_dot(normed_t[...], grad_ups[t]).astype(bf16)
        dest[2 + t // 2] = nn_dot(grad_t[...], activated[t][...]).astype(bf16)
    joined = jnp.concatenate(grad_ups, axis=1)
    up = jnp.concatenate([ref[...] for ref in ups], axis=1)
    total[...] += nt_dot(joined, up)

    @pl.when(j == pl.num_programs(0) - 1)
    def _():
        value, gain_two, shift_two = norm_back(middle[...], vectors[0:1, :], total[...])
        value = value + grad[...]
        grad_out[...] = value
        low = value.astype(bf16)
        branch[...] = low
        sums[1:2, :], sums[2:3, :] = gain_two, shift_two
        sums[3:4, :] = jnp.sum(low.astype(f32), axis=0, keepdims=True)


def feed_back(final, fronts, middle, normed, vectors, ups, downs, activated, slopes):
    rows, width = normed.shape
    hidden = activated[0].shape[1]
    step = min(256, hidden)
    stack = pl.BlockSpec((4, width, step), lambda j: (0, 0, j))
    singles = (*fronts, middle, normed, vectors)
    return pl.pallas_call(
        functools.partial(feed_back_kernel, final),
        grid=(hidden // step,),
        in_specs=[single(part.shape) for part in singles]
        + [column_block(width, step)] * 8
        + [column_block(rows, step)] * 8,
        out_specs=[stack] * 2
        + [column_block(4, step)]
        + [whole((rows, width))] * 2
        + [whole((8, width))],
        out_shape=[jax.ShapeDtypeStruct((4, width, hidden), bf16)] * 2
        + [
            jax.ShapeDtypeStruct((4, hidden), f32),
            jax.ShapeDtypeStruct((rows, width), f32),
            jax.ShapeDtypeStruct((rows, width), bf16),
            jax.ShapeDtypeStruct((8, width), f32),
        ],
        scratch_shapes=[pltpu.VMEM((rows, width), f32)] * 2
        + [pltpu.VMEM((rows, width), bf16)]
        + [pltpu.VMEM((width, rows), bf16)] * 2,
        compiler_params=pltpu.CompilerParams(vmem_limit_bytes=62 * 2**20),
    )(*singles, *ups, *downs, *activated, *slopes)


def local(
    frames,
    cotangent,
    qkv_weight,
    out_weight,
    up_weight,
    down_weight,
    qv_bias,
    up_bias,
    norm_gains,
    norm_shifts,
    out_biases,
):
    layers, block = qkv_weight.shape[:2]
    wide = qkv_weight.shape[3]
    row_count, width = frames.shape[1:]
    hidden = up_weight.shape[2]
    quarter = -(-row_count // 128) * 128
    rows = 2 * quarter
    count_dp = lax.axis_size("dp")
    me = lax.axis_index("dp")
    t_me = lax.axis_index("tensor")
    y_me = t_me // 2
    t_order = jnp.arange(4) ^ t_me
    positions = jnp.arange(count_dp)
    block_at = relative_mask(positions) ^ me
    place_of = jnp.argmax(block_at[None, :] == positions[:, None], axis=1)

    small_parts = (norm_gains, norm_shifts, out_biases, qv_bias, up_bias)
    small_sizes = [part.size for part in small_parts]
    small = jnp.concatenate([part.reshape(1, -1) for part in small_parts], axis=1)

    source = jnp.repeat(block_at, block) * block + jnp.tile(jnp.arange(block), count_dp)
    to_relative = (jnp.arange(width)[:, None] == source[None, :]).astype(bf16)

    def take_clip(value):
        mine = lax.dynamic_index_in_dim(value, y_me, 0, keepdims=False)
        theirs = exchange(lax.dynamic_index_in_dim(value, 1 - y_me, 0, keepdims=False), "tensor", 2)
        padding = ((0, 0), (0, quarter - row_count), (0, 0))
        both = jnp.pad(jnp.stack([mine, theirs]), padding).reshape(rows, width)
        return nn_dot(both, to_relative)

    def give_clip(value):
        mine, theirs = value[:quarter], value[quarter:].astype(bf16)
        theirs = nt_dot(exchange(theirs, "tensor", 2), to_relative)[:row_count]
        high = mine.astype(bf16)
        low = (mine - high.astype(f32)).astype(bf16)
        mine = (nt_dot(high, to_relative) + nt_dot(low, to_relative))[:row_count]
        first = y_me == 0
        return jnp.stack([jnp.where(first, mine, theirs), jnp.where(first, theirs, mine)])

    current = take_clip(frames)
    gradient = take_clip(cotangent)

    groups = []
    for at in range(layers):
        qk = jnp.concatenate([qkv_weight[at, :, 0], qkv_weight[at, :, 1]], axis=1)
        vo = jnp.concatenate([qkv_weight[at, :, 2], out_weight[at].T], axis=1)
        groups += [(qk, vo), (up_weight[at], down_weight[at].T)]
    gathering = Gathering(groups)
    for mask in dp_masks():
        more = exchange(small, "dp", mask)
        if mask > 1:
            (more,) = gathering.advance(more)
        small = jnp.concatenate([small, more], axis=0)
    small = jnp.stack([small, exchange(small, "tensor", 1)])
    small = jnp.stack([small, exchange(small, "tensor", 2)])
    small = small.reshape(4, count_dp, -1)
    by_part = jnp.split(small, [sum(small_sizes[: i + 1]) for i in range(4)], axis=2)

    def by_width(part):
        part = jnp.take(part, t_order, axis=0).reshape(4, count_dp, layers, 2, -1)
        return part.transpose(2, 3, 1, 0, 4).reshape(layers, 2, width)

    gain_all, shift_all, obias_all = [by_width(part) for part in by_part[:3]]
    qv_all = jnp.take(by_part[3][0::2], place_of, axis=1).reshape(2, count_dp, layers, 2, -1)
    qv_all = qv_all.transpose(2, 3, 0, 1, 4).reshape(layers, 2, 2, wide)
    up_all = jnp.take(by_part[4], place_of, axis=1).reshape(4, count_dp, layers, -1)
    up_all = up_all.transpose(2, 0, 1, 3).reshape(layers, 4, hidden)

    def feed_weights(group):
        parts = gathering.until(group)
        return [
            [parts[2 * i], exchange(parts[2 * i], "tensor", 1), parts[2 * i + 1], exchange(parts[2 * i + 1], "tensor", 1)]
            for i in range(2)
        ]

    weights = []
    saved = []
    unit, _ = normalized(current)
    normed_a = (unit * gain_all[0, 0] + shift_all[0, 0]).astype(bf16)
    normed_b = exchange(normed_a, "tensor", 1)
    for at in range(layers):
        final = at == layers - 1
        w_qk, w_qk_other, w_vo, w_vo_other = gathering.until(2 * at)
        w_attn = ((w_qk, w_vo), (w_qk_other, w_vo_other))
        bias = jnp.pad(qv_all[at].transpose(1, 0, 2), ((0, 0), (0, 0), (0, wide)))
        shares = ()
        heads = []
        for t in range(2):
            ready = (normed_a, normed_b)
            if t == 1:
                gathering.advance()
                ready = behind(ready, gathering.token, *shares)
            out = attend(row_count, quarter, *ready, *w_attn[t], bias[t], shares)
            shares = tuple(out[:2])
            heads.append(out[2:])
        share_b = exchange(shares[1], "tensor", 1)
        w_up, w_down = feed_weights(2 * at + 1)
        following = 0 if final else at + 1
        vectors = jnp.stack(
            [
                obias_all[at, 0],
                gain_all[at, 1],
                shift_all[at, 1],
                obias_all[at, 1],
                gain_all[following, 0],
                shift_all[following, 0],
            ]
        )
        vectors = jnp.pad(vectors, ((0, 2), (0, 0)))
        fed = feed(final, current, shares[0], share_b, vectors, up_all[at], w_up, w_down)
        weights.append((w_attn, w_up, w_down))
        normed = jnp.concatenate([normed_a, normed_b], axis=0)
        saved.append((current, normed, heads, fed[:4], fed[4:8], fed[8], fed[9]))
        current = fed[10]
        if not final:
            normed_a = fed[11]
            normed_b = exchange(normed_a, "tensor", 1)
    encoded = give_clip(current)

    small_grads = [None] * layers
    weight_grads = [None] * layers
    gains_one = [None] * layers
    folding = None
    fronts = (gradient,)
    for at in reversed(range(layers)):
        final = at == layers - 1
        w_attn, w_up, w_down = weights[at]
        layer_in, normed, heads, activated, slopes, middle, normed_two = saved[at]
        if folding is not None:
            folding.advance()
            fronts = behind(fronts, *folding.token())
        vectors = jnp.stack([gain_all[at, 1], gain_all[0 if final else at + 1, 0]])
        vectors = jnp.pad(vectors, ((0, 6), (0, 0)))
        own, other, bup, gradient, branch_a, sums = feed_back(
            final, fronts, middle, normed_two, vectors, w_up, w_down, activated, slopes
        )
        if not final:
            gains_one[at + 1] = sums[4:6]
        branch_b = exchange(branch_a, "tensor", 1)
        sent, finish = near_core(own, exchange(other, "tensor", 1))
        shares = ()
        dqkv = []
        for t in range(2):
            tokens = list(sent) if t == 0 else list(feed_state) + list(shares)
            if folding is not None:
                folding.advance()
                tokens += folding.token()
            ready = behind((branch_a, branch_b), *tokens)
            *shares, part = attend_back(
                row_count, quarter, *ready, *w_attn[t], *heads[t], tuple(shares)
            )
            dqkv.append(part)
            feed_state = near_two(*feed_state) if t else finish()
        tokens = list(feed_state)
        if folding is not None:
            folding.advance()
            tokens += folding.token()
            weight_grads[at + 1] = folding.result()
        *shares, dqkv[0], dqkv[1] = behind((*shares, *dqkv), *tokens)
        share_b = exchange(shares[1], "tensor", 1)
        branch = jnp.concatenate([branch_a, branch_b], axis=0)
        dw = [tn_dot(normed, dqkv[t]).astype(bf16) for t in range(2)]
        dw_o = [tn_dot(branch, heads[t][1]).astype(bf16) for t in range(2)]
        dw_qk = jnp.stack([dw[t][:, : 2 * wide] for t in range(2)])
        dw_vo = jnp.stack(
            [jnp.concatenate([dw[t][:, 2 * wide :], dw_o[t]], axis=1) for t in range(2)]
        )
        folding = Folding(dw_qk, dw_vo, *feed_state)
        dbias = jnp.stack([jnp.sum(part, axis=0, dtype=f32) for part in dqkv])
        dbias = dbias.reshape(2, 3, wide).transpose(1, 0, 2)
        fronts = (gradient, layer_in, shares[0], share_b)
        small_grads[at] = (sums, dbias[0::2], bup)
    grad_in, *last_sums = norm_back(
        layer_in, gain_all[0, 0], shares[0] + share_b.astype(f32)
    )
    gradient = gradient + grad_in
    gains_one[0] = jnp.concatenate(last_sums, axis=0)
    for step in range(4):
        if step == 2:
            (folding.attn,) = behind((folding.attn,), gradient)
        folding.advance()
    weight_grads[0] = folding.result()
    frames_grad = give_clip(gradient)

    sums, bqv, bups = [jnp.stack([small_grads[at][i] for at in range(layers)]) for i in range(3)]
    one = jnp.stack(gains_one)
    gains = jnp.stack([one[:, 0], sums[:, 1]], axis=1)
    shifts = jnp.stack([one[:, 1], sums[:, 2]], axis=1)
    obiases = jnp.stack([sums[:, 3], sums[:, 0]], axis=1)

    def from_width(part):
        part = part.reshape(layers, 2, count_dp, 4, -1).transpose(3, 2, 0, 1, 4)
        return jnp.take(part.reshape(4, count_dp, -1), t_order, axis=0)

    bqv = bqv.reshape(layers, 2, 2, count_dp, -1).transpose(2, 3, 0, 1, 4)
    bqv = jnp.take(bqv.reshape(2, count_dp, -1), block_at, axis=1)
    bqv = jnp.stack([bqv, jnp.zeros_like(bqv)], axis=1).reshape(4, count_dp, -1)
    bups = bups.reshape(layers, 4, count_dp, -1).transpose(1, 2, 0, 3)
    bups = jnp.take(bups.reshape(4, count_dp, -1), block_at, axis=1)
    small = jnp.concatenate(
        [from_width(gains), from_width(shifts), from_width(obiases), bqv, bups], axis=2
    )
    small = small.reshape(2, 2, count_dp, -1)
    small = small[0] + exchange(small[1], "tensor", 2)
    small = small[0] + exchange(small[1], "tensor", 1)
    for mask in reversed(dp_masks()):
        half = small.shape[0] // 2
        small = small[:half] + exchange(small[half:], "dp", mask)
    pieces = jnp.split(small[0], [sum(small_sizes[: i + 1]) for i in range(4)])
    gains, shifts, obiases, bqv, bups = [
        piece.reshape(part.shape) for piece, part in zip(pieces, small_parts)
    ]

    def stacked(make):
        return jnp.stack([make(*weight_grads[at]) for at in range(layers)])

    return (
        encoded,
        frames_grad,
        stacked(lambda qk, vo, up, down: jnp.stack([qk[:, :wide], qk[:, wide:], vo[:, :wide]], axis=1)),
        stacked(lambda qk, vo, up, down: vo[:, wide:].T),
        stacked(lambda qk, vo, up, down: up),
        stacked(lambda qk, vo, up, down: down.T),
        bqv,
        bups,
        gains,
        shifts,
        obiases,
    )


def solution(mesh):
    in_specs = (
        P("dp", "tensor", None),
        P("dp", "tensor", None),
        P(None, "dp", None, "tensor"),
        P(None, "tensor", "dp"),
        P(None, "dp", "tensor"),
        P(None, "tensor", "dp"),
        P(None, None, ("tensor", "dp")),
        P(None, ("tensor", "dp")),
        P(None, None, ("dp", "tensor")),
        P(None, None, ("dp", "tensor")),
        P(None, None, ("dp", "tensor")),
    )
    out_specs = (
        P("dp", "tensor", None),
        P("dp", "tensor", None),
        P(None, "dp", None, "tensor"),
        P(None, "tensor", "dp"),
        P(None, "dp", "tensor"),
        P(None, "tensor", "dp"),
        P(None, None, ("tensor", "dp")),
        P(None, ("tensor", "dp")),
        P(None, None, ("dp", "tensor")),
        P(None, None, ("dp", "tensor")),
        P(None, None, ("dp", "tensor")),
    )
    return jax.shard_map(local, mesh=mesh, in_specs=in_specs, out_specs=out_specs, check_vma=False)
```

```python
import functools
import math

import jax
import jax.numpy as jnp
from jax import lax
from jax.experimental import pallas as pl
from jax.experimental.pallas import tpu as pltpu
from jax.sharding import PartitionSpec as P

HD = 64
WIDE = 128
eps = 1e-05
LOG2E = 1.0 / math.log(2.0)
LN2 = math.log(2.0)
MASKED = -1e30
bf16 = jnp.bfloat16
f32 = jnp.float32


def exchange(value, axis, mask):
    count = lax.axis_size(axis)
    return lax.ppermute(value, axis, [(i, i ^ mask) for i in range(count)])


def dp_masks():
    count = lax.axis_size("dp")
    masks = []
    while count > 1:
        count //= 2
        masks.append(count)
    return masks


def relative_mask(position):
    result = 0
    for at, mask in enumerate(dp_masks()):
        result = result + ((position >> at) & 1) * mask
    return result


def together(*values):
    return lax.optimization_barrier(values)


def gather_steps(first, second):
    masks = dp_masks()
    cut = first.shape[1]

    def z_step(mask):
        return (
            lambda state: (exchange(state[0], "dp", mask),),
            lambda state, got: (jnp.concatenate([state[0], got[0]], axis=0),),
        )

    near = (
        lambda state: (exchange(state[0], "dp", masks[-1]), exchange(state[1], "tensor", 2)),
        lambda state, got: (
            jnp.concatenate([state[0], got[0]], axis=0),
            jnp.stack([state[1], got[1]]),
        ),
    )
    last = (
        lambda state: (exchange(state[0], "tensor", 2), exchange(state[1], "dp", masks[-1])),
        lambda state, got: (
            state[0],
            got[0],
            *[jnp.concatenate([state[1][i], got[1][i]], axis=0) for i in range(2)],
        ),
    )

    def split(finish):
        def cut_last(state, got):
            block = finish(state, got)[0]
            return block[:, :cut], block[:, cut:]

        return cut_last

    ahead = [z_step(mask) for mask in masks[:-1]]
    ahead[-1] = (ahead[-1][0], split(ahead[-1][1]))
    return (jnp.concatenate([first, second], axis=1),), ahead, [near, last]


class Gathering:
    def __init__(self, groups):
        made = [gather_steps(*group) for group in groups]
        self.states = [start for start, _, _ in made]
        self.plan = [[(0, step)] for step in made[0][1]]
        for at, (_, _, near) in enumerate(made):
            ahead = made[at + 1][1] if at + 1 < len(made) else []
            for i in range(max(len(near), len(ahead))):
                stage = [(at, near[i])] if i < len(near) else []
                self.plan.append(stage + ([(at + 1, ahead[i])] if i < len(ahead) else []))
        self.ends = [
            max(i for i, stage in enumerate(self.plan) for g, _ in stage if g == at)
            for at in range(len(made))
        ]
        self.done = 0
        self.tokens = ()

    def advance(self, *others):
        stage = self.plan[self.done]
        self.done += 1
        flat = [part for g, _ in stage for part in self.states[g]]
        flat = behind(flat, *self.tokens)
        states, received, at = [], [], 0
        for g, (send, _) in stage:
            states.append(flat[at : at + len(self.states[g])])
            at += len(self.states[g])
            received.append(send(states[-1]))
        flat = together(*[part for got in received for part in got], *others)
        at = 0
        for (g, (_, finish)), state, got in zip(stage, states, received):
            self.states[g] = finish(state, flat[at : at + len(got)])
            at += len(got)
        self.tokens = [part for g, _ in stage for part in self.states[g][:1]]
        return flat[at:]

    def until(self, group):
        while self.done <= self.ends[group]:
            self.advance()
        return self.states[group]


def behind(values, *tokens):
    return together(*values, *tokens)[: len(values)]


def add_low(kept, received):
    return (kept.astype(f32) + received.astype(f32)).astype(bf16)


def near_one_sent(first, second):
    return first[1], second[:, second.shape[1] // 2 :]


def near_one(sent):
    return exchange(sent[0], "tensor", 2), exchange(sent[1], "dp", dp_masks()[-1])


def near_one_sum(first, second, got):
    return add_low(first[0], got[0]), add_low(second[:, : second.shape[1] // 2], got[1])


def near_two(first, second):
    half = first.shape[0] // 2
    return exchange(first[half:], "dp", dp_masks()[-1]), exchange(second[1], "tensor", 2)


def near_two_sum(first, second, got):
    return add_low(first[: first.shape[0] // 2], got[0]), add_low(second[0], got[1])


def far(value, masks):
    for mask in masks[:-1]:
        value = far_sum(value, exchange(value[value.shape[0] // 2 :], "dp", mask))
    return value, exchange(value[value.shape[0] // 2 :], "dp", masks[-1])


def far_sum(value, got):
    return add_low(value[: value.shape[0] // 2], got)


class CoreFold:
    def __init__(self, own, received):
        half = own.shape[1] // 2
        self.half = half
        self.kept = (own[0], received[0], own[2:, :half], received[2:, :half])
        self.state = together(
            add_low(own[1], received[1]), add_low(own[2:, half:], received[2:, half:])
        )
        self.step = 0

    def send(self):
        return near_two(*self.state) if self.step else near_one(self.state)

    def finish(self, got):
        if self.step:
            self.state = near_two_sum(*self.state, got)
        else:
            first = self.kept[0].astype(f32) + self.kept[1].astype(f32) + got[0].astype(f32)
            second = self.kept[2].astype(f32) + self.kept[3].astype(f32) + got[1].astype(f32)
            self.state = together(first.astype(bf16), second.astype(bf16))
        self.step += 1


class Folding:
    def __init__(self, qk, vo, up, down):
        masks = dp_masks()[-2::-1]
        self.masks = masks[:-1], masks[-1:]
        self.attn = together(qk, vo)
        self.feed = jnp.concatenate([up, down], axis=1)
        self.step = 0

    def send(self):
        if self.step < 2:
            got = near_two(*self.attn) if self.step else near_one(near_one_sent(*self.attn))
            self.feed, more = far(self.feed, self.masks[self.step])
            return *got, more
        self.attn, more = far(self.attn, self.masks[self.step - 2])
        return (more,)

    def finish(self, got):
        if self.step < 2:
            self.attn = (near_two_sum if self.step else near_one_sum)(*self.attn, got[:2])
            self.feed = far_sum(self.feed, got[2])
            *self.attn, self.feed = together(*self.attn, self.feed)
            if self.step == 1:
                self.attn = jnp.concatenate(self.attn, axis=1)
        else:
            (self.attn,) = together(far_sum(self.attn, got[0]))
        self.step += 1

    def tokens(self):
        return (self.feed, self.attn) if self.step > 1 else (self.feed, *self.attn)

    def result(self):
        half, low = self.attn.shape[1] // 2, self.feed.shape[1] // 2
        parts = self.attn[:, :half], self.attn[:, half:], self.feed[:, :low], self.feed[:, low:]
        return [part.astype(f32) for part in parts]


def advance(folds, *others):
    received = [fold.send() for fold in folds]
    flat = together(*[part for got in received for part in got], *others)
    at = 0
    for fold, got in zip(folds, received):
        fold.finish(flat[at : at + len(got)])
        at += len(got)
    return flat[at:]


def split_low(value):
    high = value.astype(bf16)
    rest = value - high.astype(f32)
    mid = rest.astype(bf16)
    return high, mid, (rest - mid.astype(f32)).astype(bf16)


def lane_at(rows):
    return lax.broadcasted_iota(jnp.int32, (rows, WIDE - HD), 1)


def key_extra(rows, row_count, quarter, ones):
    lane = lane_at(rows)
    row = lax.broadcasted_iota(jnp.int32, (rows, WIDE - HD), 0)
    masked = lax.rem(row, quarter) >= row_count
    bias = jnp.where(masked, MASKED, 0.0).astype(f32)
    value = jnp.where(lane == 0, bias, jnp.where(lane <= ones, 1.0, 0.0))
    return value.astype(bf16)


def ones_extra(rows, ones):
    return jnp.where(lane_at(rows) < ones, 1.0, 0.0).astype(bf16)


def widen(part, extra):
    return jnp.concatenate([part, extra], axis=1)


def nt_dot(left, right):
    return lax.dot_general(left, right, (((1,), (1,)), ((), ())), preferred_element_type=f32)


def nn_dot(left, right):
    return lax.dot_general(left, right, (((1,), (0,)), ((), ())), preferred_element_type=f32)


def tn_dot(left, right):
    return lax.dot_general(left, right, (((0,), (0,)), ((), ())), preferred_element_type=f32)


def whole(shape):
    return pl.BlockSpec(shape, lambda j: (0,) * len(shape))


def attend_kernel(row_count, quarter, step, first, *refs):
    normed_a, normed_b, w_qk, w_vo, bias = refs[:5]
    before = () if first else refs[5:7]
    share_a, share_b, qkv, o, lse, q_s, k_s, v_s = refs[5 + len(before) :]
    rows = normed_a.shape[0]
    wide = o.shape[1]
    heads = wide // HD
    k_more = key_extra(rows, row_count, quarter, 0)
    one = ones_extra(rows, 1)
    lane = lax.broadcasted_iota(jnp.int32, (1, 2 * wide), 1)
    scale = jnp.where(lane < wide, HD**-0.5 * LOG2E, 1.0)
    for half, normed in enumerate((normed_a, normed_b)):
        at = pl.ds(half * rows, rows)
        qk = ((nn_dot(normed[...], w_qk[...]) + bias[0:1, :]) * scale).astype(bf16)
        v = (nn_dot(normed[...], w_vo[:, :wide]) + bias[1:2, :wide]).astype(bf16)
        qkv[at, : 2 * wide] = qk
        qkv[at, 2 * wide :] = v
        for h in range(heads):
            low, high = h * HD, (h + 1) * HD
            q_s[h, at, :] = widen(qk[:, low:high], one)
            k_s[h, at, :] = widen(qk[:, wide + low : wide + high], k_more)
            v_s[h, at, :] = widen(v[:, low:high], one)

    for h in range(heads):

        def work(i, carry, h=h):
            for part in range(2):
                at = pl.ds(pl.multiple_of((2 * i + part) * step, step), step)
                scores = nt_dot(q_s[h, at, :], k_s[h])
                top = jnp.max(scores, axis=-1, keepdims=True)
                weights = jnp.exp2(scores - top).astype(bf16)
                summed = nn_dot(weights, v_s[h])
                total = summed[:, HD : HD + 1]
                o[at, h * HD : (h + 1) * HD] = (summed[:, :HD] / total).astype(bf16)
                lse[at, h : h + 1] = top + jnp.log2(total)
            return carry

        lax.fori_loop(0, rows // step, work, 0)
    w_o = w_vo[:, wide:]
    part_a = nt_dot(o[pl.ds(0, rows), :], w_o)
    part_b = nt_dot(o[pl.ds(rows, rows), :], w_o)
    if not first:
        part_a = part_a + before[0][...]
        part_b = part_b + before[1][...]
    share_a[...] = part_a
    share_b[...] = part_b.astype(share_b.dtype)


def attend(row_count, quarter, normed_a, normed_b, w_qk, w_vo, bias, before):
    rows, width = normed_a.shape
    wide = w_qk.shape[1] // 2
    heads = wide // HD
    operands = (normed_a, normed_b, w_qk, w_vo, bias, *before)
    outs = [
        jax.ShapeDtypeStruct((rows, width), f32),
        jax.ShapeDtypeStruct((rows, width), bf16 if before else f32),
        jax.ShapeDtypeStruct((2 * rows, 3 * wide), bf16),
        jax.ShapeDtypeStruct((2 * rows, wide), bf16),
        jax.ShapeDtypeStruct((2 * rows, 8), f32),
    ]
    return pl.pallas_call(
        functools.partial(attend_kernel, row_count, quarter, min(256, rows), not before),
        grid=(1,),
        in_specs=[whole(part.shape) for part in operands],
        out_specs=[whole(part.shape) for part in outs],
        out_shape=outs,
        scratch_shapes=[pltpu.VMEM((heads, 2 * rows, WIDE), bf16)] * 3,
        compiler_params=pltpu.CompilerParams(vmem_limit_bytes=56 * 2**20),
    )(*operands)


def attend_back_kernel(row_count, quarter, step, first, *refs):
    branch_a, branch_b, w_qk, w_vo, qkv, o, lse = refs[:7]
    before = () if first else refs[7:9]
    dn_a, dn_b, dqkv, q_s, k_s, kt_s, v_s, do_s, dq_s, dk_s, dv_s = refs[7 + len(before) :]
    rows = branch_a.shape[0]
    wide = o.shape[1]
    heads = wide // HD
    k_more = key_extra(rows, row_count, quarter, 3)
    three = ones_extra(rows, 3)
    lane = lane_at(rows)

    def spread_lanes(first, parts):
        value = jnp.where(lane < first, 1.0, 0.0).astype(f32)
        for at, part in enumerate(parts):
            value = jnp.where(lane == first + at, part.astype(f32), value)
        return value.astype(bf16)

    for half, branch in enumerate((branch_a, branch_b)):
        at = pl.ds(half * rows, rows)
        grad_all = nn_dot(branch[...], w_vo[:, wide:]).astype(bf16)
        for h in range(heads):
            low, high = h * HD, (h + 1) * HD
            minus_lse = split_low(-lse[at, h : h + 1])
            q_s[h, at, :] = widen(qkv[at, low:high], spread_lanes(1, minus_lse))
            keys = widen(qkv[at, wide + low : wide + high], k_more)
            k_s[h, at, :] = keys
            kt_s[h, :, at] = jnp.transpose(keys.astype(f32)).astype(bf16)
            v_s[h, at, :] = widen(qkv[at, 2 * wide + low : 2 * wide + high], three)
            grad = grad_all[:, low:high]
            inner = jnp.sum(grad.astype(f32) * o[at, low:high].astype(f32), axis=1, keepdims=True)
            do_s[h, at, :] = widen(grad, spread_lanes(0, split_low(-inner)))

    dk_s[...] = jnp.zeros_like(dk_s)
    dv_s[...] = jnp.zeros_like(dv_s)
    chunks = 2 * rows // step

    def work(i, carry):
        h = i // chunks
        at = pl.ds(pl.multiple_of(lax.rem(i, chunks) * step, step), step)
        queries = q_s[h, at, :]
        grad_out = do_s[h, at, :]
        probs = jnp.exp2(nt_dot(k_s[h], queries))
        grad_scores = (probs * nt_dot(v_s[h], grad_out)).astype(bf16)
        dv_s[h] += nn_dot(probs.astype(bf16), grad_out)
        dk_s[h] += nn_dot(grad_scores, queries)
        dq_s[h, at, :] = jnp.transpose(nn_dot(kt_s[h], grad_scores))
        return carry

    lax.fori_loop(0, heads * chunks, work, 0)
    for h in range(heads):
        low, high = h * HD, (h + 1) * HD
        dqkv[:, low:high] = (dq_s[h][:, :HD] * HD**-0.5).astype(bf16)
        dqkv[:, wide + low : wide + high] = (dk_s[h][:, :HD] * LN2).astype(bf16)
        dqkv[:, 2 * wide + low : 2 * wide + high] = dv_s[h][:, :HD].astype(bf16)
    for half, dest in enumerate((dn_a, dn_b)):
        at = pl.ds(half * rows, rows)
        part = nt_dot(dqkv[at, : 2 * wide], w_qk[...])
        part = part + nt_dot(dqkv[at, 2 * wide :], w_vo[:, :wide])
        if not first:
            part = part + before[half][...]
        dest[...] = part.astype(dest.dtype)


def attend_back(row_count, quarter, branch_a, branch_b, w_qk, w_vo, qkv, o, lse, before):
    rows, width = branch_a.shape
    wide = o.shape[1]
    heads = wide // HD
    operands = (branch_a, branch_b, w_qk, w_vo, qkv, o, lse, *before)
    outs = [
        jax.ShapeDtypeStruct((rows, width), f32),
        jax.ShapeDtypeStruct((rows, width), bf16 if before else f32),
        jax.ShapeDtypeStruct((2 * rows, 3 * wide), bf16),
    ]
    return pl.pallas_call(
        functools.partial(attend_back_kernel, row_count, quarter, min(256, rows), not before),
        grid=(1,),
        in_specs=[whole(part.shape) for part in operands],
        out_specs=[whole(part.shape) for part in outs],
        out_shape=outs,
        scratch_shapes=[
            pltpu.VMEM((heads, 2 * rows, WIDE), bf16),
            pltpu.VMEM((heads, 2 * rows, WIDE), bf16),
            pltpu.VMEM((heads, WIDE, 2 * rows), bf16),
            pltpu.VMEM((heads, 2 * rows, WIDE), bf16),
            pltpu.VMEM((heads, 2 * rows, WIDE), bf16),
            pltpu.VMEM((heads, 2 * rows, WIDE), f32),
            pltpu.VMEM((heads, 2 * rows, WIDE), f32),
            pltpu.VMEM((heads, 2 * rows, WIDE), f32),
        ],
        compiler_params=pltpu.CompilerParams(vmem_limit_bytes=60 * 2**20),
    )(*operands)


def normalized(value):
    centred = value - jnp.mean(value, axis=-1, keepdims=True)
    scale = lax.rsqrt(jnp.mean(centred * centred, axis=-1, keepdims=True) + eps)
    return centred * scale, scale


def norm_back(value, gain, grad):
    unit, scale = normalized(value)
    scaled = grad * gain
    result = scale * (
        scaled
        - jnp.mean(scaled, axis=-1, keepdims=True)
        - unit * jnp.mean(scaled * unit, axis=-1, keepdims=True)
    )
    sums = [jnp.sum(part, axis=0, keepdims=True) for part in (grad * unit, grad)]
    return result, *sums


def gelu_both(value):
    share = 0.5 * (1.0 + lax.erf(value * math.sqrt(0.5)))
    density = jnp.exp(-0.5 * value * value) * (1.0 / math.sqrt(2.0 * math.pi))
    return (value * share).astype(bf16), (share + value * density).astype(bf16)


def feed_kernel(final, *refs):
    current, share_a, share_b, vectors, bias = refs[:5]
    ups, downs, activated, slopes = [refs[5 + 4 * i : 9 + 4 * i] for i in range(4)]
    middle, normed, total = refs[21:24]
    j = pl.program_id(0)

    @pl.when(j == 0)
    def _():
        value = current[...] + (share_a[...] + share_b[...].astype(f32) + vectors[0:1, :])
        middle[...] = value
        normed[...] = (normalized(value)[0] * vectors[1:2, :] + vectors[2:3, :]).astype(bf16)
        total[...] = value + vectors[3:4, :]

    rows_in = normed[...]
    for t in range(4):
        upward = nn_dot(rows_in, ups[t][...]) + bias[t : t + 1, :]
        activated[t][...], slopes[t][...] = gelu_both(upward)
    joined = jnp.concatenate([ref[...] for ref in activated], axis=1)
    down = jnp.concatenate([ref[...] for ref in downs], axis=1)
    total[...] += nt_dot(joined, down)
    if not final:
        following = refs[24]

        @pl.when(j == pl.num_programs(0) - 1)
        def _():
            unit, _ = normalized(total[...])
            following[...] = (unit * vectors[4:5, :] + vectors[5:6, :]).astype(bf16)


def single(shape):
    return pl.BlockSpec(shape, lambda j: (0,) * len(shape), pipeline_mode=pl.Buffered(1))


def column_block(rows, step):
    return pl.BlockSpec((rows, step), lambda j: (0, j))


def feed(final, current, share_a, share_b, vectors, bias, ups, downs):
    rows, width = current.shape
    hidden = bias.shape[1]
    step = min(256, hidden)
    rest = [f32, bf16, f32] if final else [f32, bf16, f32, bf16]
    fronts = (current, share_a, share_b, vectors)
    return pl.pallas_call(
        functools.partial(feed_kernel, final),
        grid=(hidden // step,),
        in_specs=[single(part.shape) for part in fronts]
        + [column_block(4, step)]
        + [column_block(width, step)] * 8,
        out_specs=[column_block(rows, step)] * 8 + [whole((rows, width))] * len(rest),
        out_shape=[jax.ShapeDtypeStruct((rows, hidden), bf16)] * 8
        + [jax.ShapeDtypeStruct((rows, width), kind) for kind in rest],
        compiler_params=pltpu.CompilerParams(vmem_limit_bytes=60 * 2**20),
    )(*fronts, bias, *ups, *downs)


def feed_back_kernel(final, *refs):
    count = 1 if final else 4
    fronts, refs = refs[:count], refs[count:]
    middle, normed, vectors = refs[:3]
    ups, downs, activated, slopes = [refs[3 + 4 * i : 7 + 4 * i] for i in range(4)]
    own, other, bias_grad, grad_out, branch, sums = refs[19:25]
    total, grad, grad_low, normed_t, grad_t = refs[25:]
    j = pl.program_id(0)

    @pl.when(j == 0)
    def _():
        sums[...] = jnp.zeros_like(sums)
        if final:
            value = fronts[0][...].astype(f32)
        else:
            above, layer_out, share_a, share_b = fronts
            grad_normed = share_a[...] + share_b[...].astype(f32)
            value, gain_one, shift_one = norm_back(layer_out[...], vectors[1:2, :], grad_normed)
            value = value + above[...]
            sums[4:5, :], sums[5:6, :] = gain_one, shift_one
        grad[...] = value
        low = value.astype(bf16)
        grad_low[...] = low
        sums[0:1, :] = jnp.sum(low.astype(f32), axis=0, keepdims=True)
        normed_t[...] = jnp.transpose(normed[...].astype(f32)).astype(bf16)
        grad_t[...] = jnp.transpose(low.astype(f32)).astype(bf16)
        total[...] = jnp.zeros_like(total)

    grad_rows = grad_low[...]
    grad_ups = []
    for t in range(4):
        grad_act = nn_dot(grad_rows, downs[t][...])
        scaled = grad_act * slopes[t][...].astype(f32)
        grad_ups.append(scaled.astype(bf16))
        bias_grad[t : t + 1, :] = jnp.sum(scaled, axis=0, keepdims=True)
        dest = (own, other)[t % 2]
        dest[t // 2] = nn_dot(normed_t[...], grad_ups[t]).astype(bf16)
        dest[2 + t // 2] = nn_dot(grad_t[...], activated[t][...]).astype(bf16)
    joined = jnp.concatenate(grad_ups, axis=1)
    up = jnp.concatenate([ref[...] for ref in ups], axis=1)
    total[...] += nt_dot(joined, up)

    @pl.when(j == pl.num_programs(0) - 1)
    def _():
        value, gain_two, shift_two = norm_back(middle[...], vectors[0:1, :], total[...])
        value = value + grad[...]
        grad_out[...] = value
        low = value.astype(bf16)
        branch[...] = low
        sums[1:2, :], sums[2:3, :] = gain_two, shift_two
        sums[3:4, :] = jnp.sum(low.astype(f32), axis=0, keepdims=True)


def feed_back(final, fronts, middle, normed, vectors, ups, downs, activated, slopes):
    rows, width = normed.shape
    hidden = activated[0].shape[1]
    step = min(256, hidden)
    stack = pl.BlockSpec((4, width, step), lambda j: (0, 0, j))
    singles = (*fronts, middle, normed, vectors)
    return pl.pallas_call(
        functools.partial(feed_back_kernel, final),
        grid=(hidden // step,),
        in_specs=[single(part.shape) for part in singles]
        + [column_block(width, step)] * 8
        + [column_block(rows, step)] * 8,
        out_specs=[stack] * 2
        + [column_block(4, step)]
        + [whole((rows, width))] * 2
        + [whole((8, width))],
        out_shape=[jax.ShapeDtypeStruct((4, width, hidden), bf16)] * 2
        + [
            jax.ShapeDtypeStruct((4, hidden), f32),
            jax.ShapeDtypeStruct((rows, width), f32),
            jax.ShapeDtypeStruct((rows, width), bf16),
            jax.ShapeDtypeStruct((8, width), f32),
        ],
        scratch_shapes=[pltpu.VMEM((rows, width), f32)] * 2
        + [pltpu.VMEM((rows, width), bf16)]
        + [pltpu.VMEM((width, rows), bf16)] * 2,
        compiler_params=pltpu.CompilerParams(vmem_limit_bytes=62 * 2**20),
    )(*singles, *ups, *downs, *activated, *slopes)


def local(
    frames,
    cotangent,
    qkv_weight,
    out_weight,
    up_weight,
    down_weight,
    qv_bias,
    up_bias,
    norm_gains,
    norm_shifts,
    out_biases,
):
    layers, block = qkv_weight.shape[:2]
    wide = qkv_weight.shape[3]
    row_count, width = frames.shape[1:]
    hidden = up_weight.shape[2]
    quarter = -(-row_count // 128) * 128
    rows = 2 * quarter
    count_dp = lax.axis_size("dp")
    me = lax.axis_index("dp")
    t_me = lax.axis_index("tensor")
    y_me = t_me // 2
    block_at = relative_mask(jnp.arange(count_dp)) ^ me

    norm_part, up_part, qv_part = norm_gains.shape[2], up_bias.shape[1], qv_bias.shape[2]
    lanes = max(4 * norm_part, up_part)

    def place(part, size, at):
        room = jnp.zeros((part.shape[0], size), f32)
        return lax.dynamic_update_slice(room, part, (0, at))

    def to_lanes(part):
        return jnp.pad(part, ((0, 0), (0, lanes - part.shape[1])))

    by_width = jnp.stack([norm_gains, norm_shifts, out_biases]).reshape(6 * layers, norm_part)
    by_width = to_lanes(place(by_width, 4 * norm_part, t_me * norm_part))
    own = jnp.concatenate(
        [by_width, to_lanes(qv_bias.reshape(2 * layers, qv_part)), to_lanes(up_bias)]
    )
    cut, end = 6 * layers, 8 * layers
    got = exchange(own, "tensor", 1)
    own = jnp.concatenate([own[:cut] + got[:cut], own[cut:], got[end:]])
    got = exchange(own, "tensor", 2)
    by_width = (own[:cut] + got[:cut])[:, : 4 * norm_part]
    by_hidden = jnp.concatenate(
        [
            place(jnp.concatenate([own[end:], got[end:]])[:, :up_part], hidden, me * up_part),
            place(
                jnp.concatenate([own[cut:end], got[cut:end]])[:, :qv_part], hidden, me * qv_part
            ),
        ]
    )

    source = jnp.repeat(block_at, block) * block + jnp.tile(jnp.arange(block), count_dp)
    to_relative = (jnp.arange(width)[:, None] == source[None, :]).astype(bf16)

    first = y_me == 0

    def take_clip(value):
        mine = jnp.where(first, value[0], value[1])
        theirs = exchange(jnp.where(first, value[1], value[0]), "tensor", 2)
        padding = ((0, 0), (0, quarter - row_count), (0, 0))
        both = jnp.pad(jnp.stack([mine, theirs]), padding).reshape(rows, width)
        return nn_dot(both, to_relative)

    def give_clip(value):
        mine, theirs = value[:quarter], value[quarter:].astype(bf16)
        theirs = nt_dot(exchange(theirs, "tensor", 2), to_relative)[:row_count]
        high = mine.astype(bf16)
        low = (mine - high.astype(f32)).astype(bf16)
        mine = (nt_dot(high, to_relative) + nt_dot(low, to_relative))[:row_count]
        return jnp.stack([jnp.where(first, mine, theirs), jnp.where(first, theirs, mine)])

    current = take_clip(frames)
    gradient = take_clip(cotangent)

    groups = []
    for at in range(layers):
        qk = jnp.concatenate([qkv_weight[at, :, 0], qkv_weight[at, :, 1]], axis=1)
        vo = jnp.concatenate([qkv_weight[at, :, 2], out_weight[at].T], axis=1)
        groups += [(qk, vo), (up_weight[at], down_weight[at].T)]
    gathering = Gathering(groups)
    for mask in dp_masks():
        got = exchange(by_width, "dp", mask), exchange(by_hidden, "dp", mask)
        if mask > 1:
            got = gathering.advance(*got)
        by_width = jnp.concatenate([by_width, got[0]], axis=1)
        by_hidden = by_hidden + got[1]
    gain_all, shift_all, obias_all = by_width.reshape(3, layers, 2, width)
    up_all = by_hidden[: 4 * layers].reshape(4, layers, hidden).transpose(1, 0, 2)
    qv_all = by_hidden[4 * layers :, :wide].reshape(2, layers, 2, wide).transpose(1, 0, 2, 3)

    def feed_weights(group):
        parts = gathering.until(group)
        return [
            [parts[2 * i], exchange(parts[2 * i], "tensor", 1), parts[2 * i + 1], exchange(parts[2 * i + 1], "tensor", 1)]
            for i in range(2)
        ]

    weights = []
    saved = []
    unit, _ = normalized(current)
    normed_a = (unit * gain_all[0, 0] + shift_all[0, 0]).astype(bf16)
    normed_b = exchange(normed_a, "tensor", 1)
    for at in range(layers):
        final = at == layers - 1
        w_qk, w_qk_other, w_vo, w_vo_other = gathering.until(2 * at)
        w_attn = ((w_qk, w_vo), (w_qk_other, w_vo_other))
        bias = jnp.pad(qv_all[at], ((0, 0), (0, 0), (0, wide)))
        shares = ()
        heads = []
        for t in range(2):
            ready = behind((normed_a, normed_b), *gathering.tokens, *shares)
            out = attend(row_count, quarter, *ready, *w_attn[t], bias[t], shares)
            out = gathering.advance(*out)
            shares = tuple(out[:2])
            heads.append(out[2:])
        share_b = exchange(shares[1], "tensor", 1)
        w_up, w_down = feed_weights(2 * at + 1)
        following = 0 if final else at + 1
        vectors = jnp.stack(
            [
                obias_all[at, 0],
                gain_all[at, 1],
                shift_all[at, 1],
                obias_all[at, 1],
                gain_all[following, 0],
                shift_all[following, 0],
            ]
        )
        vectors = jnp.pad(vectors, ((0, 2), (0, 0)))
        fed = feed(final, current, shares[0], share_b, vectors, up_all[at], w_up, w_down)
        if not final:
            fed = gathering.advance(*fed)
        weights.append((w_attn, w_up, w_down))
        normed = jnp.concatenate([normed_a, normed_b], axis=0)
        saved.append((current, normed, heads, fed[:4], fed[4:8], fed[8], fed[9]))
        current = fed[10]
        if not final:
            normed_a = fed[11]
            normed_b = exchange(normed_a, "tensor", 1)
    encoded = give_clip(current)

    small_grads = [None] * layers
    weight_grads = [None] * layers
    gains_one = [None] * layers
    folding = None
    fronts = (gradient,)
    for at in reversed(range(layers)):
        final = at == layers - 1
        w_attn, w_up, w_down = weights[at]
        layer_in, normed, heads, activated, slopes, middle, normed_two = saved[at]
        uppers = [] if folding is None else [folding]
        vectors = jnp.stack([gain_all[at, 1], gain_all[0 if final else at + 1, 0]])
        vectors = jnp.pad(vectors, ((0, 6), (0, 0)))
        if uppers:
            fronts = behind(fronts, *folding.attn, folding.feed)
        fed = feed_back(
            final, fronts, middle, normed_two, vectors, w_up, w_down, activated, slopes
        )
        own, other, bup, gradient, branch_a, sums = advance(uppers, *fed)
        if not final:
            gains_one[at + 1] = sums[4:6]
        branch_b = exchange(branch_a, "tensor", 1)
        core = CoreFold(own, exchange(other, "tensor", 1))
        shares = ()
        dqkv = []
        for t in range(2):
            tokens = [*core.state, *shares]
            if uppers:
                tokens += folding.tokens()
            ready = behind((branch_a, branch_b), *tokens)
            *shares, part = advance(
                [core, *uppers],
                *attend_back(row_count, quarter, *ready, *w_attn[t], *heads[t], tuple(shares)),
            )
            dqkv.append(part)
        *shares, dqkv[0], dqkv[1] = behind((*shares, *dqkv), *core.state)
        if uppers:
            advance(uppers)
            weight_grads[at + 1] = folding.result()
        share_b = exchange(shares[1], "tensor", 1)
        branch = jnp.concatenate([branch_a, branch_b], axis=0)
        dw = [tn_dot(normed, dqkv[t]).astype(bf16) for t in range(2)]
        dw_o = [tn_dot(branch, heads[t][1]).astype(bf16) for t in range(2)]
        dw_qk = jnp.stack([dw[t][:, : 2 * wide] for t in range(2)])
        dw_vo = jnp.stack(
            [jnp.concatenate([dw[t][:, 2 * wide :], dw_o[t]], axis=1) for t in range(2)]
        )
        folding = Folding(dw_qk, dw_vo, *core.state)
        dbias = jnp.stack([jnp.sum(part, axis=0, dtype=f32) for part in dqkv])
        dbias = dbias.reshape(2, 3, wide).transpose(1, 0, 2)
        fronts = (gradient, layer_in, shares[0], share_b)
        small_grads[at] = (sums, dbias[0::2], bup)
    grad_in, *last_sums = norm_back(
        layer_in, gain_all[0, 0], shares[0] + share_b.astype(f32)
    )
    gradient = gradient + grad_in
    gains_one[0] = jnp.concatenate(last_sums, axis=0)
    sums, bqv, bups = [jnp.stack([small_grads[at][i] for at in range(layers)]) for i in range(3)]
    one = jnp.stack(gains_one)
    by_width = jnp.stack(
        [
            jnp.stack([one[:, 0], sums[:, 1]], axis=1),
            jnp.stack([one[:, 1], sums[:, 2]], axis=1),
            jnp.stack([sums[:, 3], sums[:, 0]], axis=1),
        ]
    ).reshape(6 * layers, width)
    by_hidden = [
        jnp.concatenate(
            [
                bups[:, 2 * i : 2 * i + 2].reshape(2 * layers, hidden),
                jnp.pad(bqv[:, :, i].reshape(2 * layers, wide), ((0, 0), (0, hidden - wide))),
            ]
        )
        for i in range(2)
    ]
    (got,) = advance([folding], exchange(by_hidden[1], "tensor", 2))
    by_hidden = by_hidden[0] + got
    parts = by_hidden[: 2 * layers].reshape(layers, 2, hidden)
    gradient, by_width, *folding.attn, folding.feed = together(
        gradient, by_width, *folding.attn, folding.feed
    )
    got = advance(
        [folding], exchange(by_width, "tensor", 2), exchange(parts[:, 1], "tensor", 1)
    )
    by_width = by_width + got[0]
    by_hidden = jnp.concatenate([parts[:, 0] + got[1], by_hidden[2 * layers :]])
    got = exchange(by_width, "tensor", 1)
    for mask in reversed(dp_masks()):
        if folding.step < 4:
            got, more = advance([folding], got, exchange(by_hidden, "dp", mask))
        else:
            got, more = together(got, exchange(by_hidden, "dp", mask))
        by_hidden = by_hidden + more
        by_width = by_width + got if mask == 1 else by_width[:, : by_width.shape[1] // 2] + got
        got = exchange(by_width[:, by_width.shape[1] // 2 :], "dp", mask)
    by_width = by_width[:, : by_width.shape[1] // 2] + got
    weight_grads[0] = folding.result()
    frames_grad = give_clip(gradient)
    by_width = lax.dynamic_slice(by_width, (0, t_me * norm_part), (6 * layers, norm_part))
    gains, shifts, obiases = by_width.reshape(3, layers, 2, norm_part)
    bups = lax.dynamic_slice(by_hidden, (0, me * up_part), (layers, up_part))
    bqv = lax.dynamic_slice(by_hidden, (layers, me * qv_part), (2 * layers, qv_part))
    bqv = bqv.reshape(layers, 2, qv_part)

    def stacked(make):
        return jnp.stack([make(*weight_grads[at]) for at in range(layers)])

    return (
        encoded,
        frames_grad,
        stacked(lambda qk, vo, up, down: jnp.stack([qk[:, :wide], qk[:, wide:], vo[:, :wide]], axis=1)),
        stacked(lambda qk, vo, up, down: vo[:, wide:].T),
        stacked(lambda qk, vo, up, down: up),
        stacked(lambda qk, vo, up, down: down.T),
        bqv,
        bups,
        gains,
        shifts,
        obiases,
    )


def solution(mesh):
    in_specs = (
        P("dp", "tensor", None),
        P("dp", "tensor", None),
        P(None, "dp", None, "tensor"),
        P(None, "tensor", "dp"),
        P(None, "dp", "tensor"),
        P(None, "tensor", "dp"),
        P(None, None, ("tensor", "dp")),
        P(None, ("tensor", "dp")),
        P(None, None, ("dp", "tensor")),
        P(None, None, ("dp", "tensor")),
        P(None, None, ("dp", "tensor")),
    )
    out_specs = (
        P("dp", "tensor", None),
        P("dp", "tensor", None),
        P(None, "dp", None, "tensor"),
        P(None, "tensor", "dp"),
        P(None, "dp", "tensor"),
        P(None, "tensor", "dp"),
        P(None, None, ("tensor", "dp")),
        P(None, ("tensor", "dp")),
        P(None, None, ("dp", "tensor")),
        P(None, None, ("dp", "tensor")),
        P(None, None, ("dp", "tensor")),
    )
    return jax.shard_map(local, mesh=mesh, in_specs=in_specs, out_specs=out_specs, check_vma=False)
```

```python
import functools
import math

import jax
import jax.numpy as jnp
from jax import lax
from jax.experimental import pallas as pl
from jax.experimental.pallas import tpu as pltpu
from jax.sharding import PartitionSpec as P

HD = 64
WIDE = 128
eps = 1e-05
LOG2E = 1.0 / math.log(2.0)
LN2 = math.log(2.0)
MASKED = -1e30
bf16 = jnp.bfloat16
f32 = jnp.float32


def exchange(value, axis, mask):
    count = lax.axis_size(axis)
    return lax.ppermute(value, axis, [(i, i ^ mask) for i in range(count)])


def dp_masks():
    count = lax.axis_size("dp")
    masks = []
    while count > 1:
        count //= 2
        masks.append(count)
    return masks


def relative_mask(position):
    result = 0
    for at, mask in enumerate(dp_masks()):
        result = result + ((position >> at) & 1) * mask
    return result


def together(*values):
    return lax.optimization_barrier(values)


def gather_steps(first, second):
    masks = dp_masks()
    cut = first.shape[1]

    def z_step(mask):
        return (
            lambda state: (exchange(state[0], "dp", mask),),
            lambda state, got: (jnp.concatenate([state[0], got[0]], axis=0),),
        )

    near = (
        lambda state: (exchange(state[0], "dp", masks[-1]), exchange(state[1], "tensor", 2)),
        lambda state, got: (
            jnp.concatenate([state[0], got[0]], axis=0),
            jnp.stack([state[1], got[1]]),
        ),
    )
    last = (
        lambda state: (exchange(state[0], "tensor", 2), exchange(state[1], "dp", masks[-1])),
        lambda state, got: (
            state[0],
            got[0],
            *[jnp.concatenate([state[1][i], got[1][i]], axis=0) for i in range(2)],
        ),
    )

    def split(finish):
        def cut_last(state, got):
            block = finish(state, got)[0]
            return block[:, :cut], block[:, cut:]

        return cut_last

    ahead = [z_step(mask) for mask in masks[:-1]]
    ahead[-1] = (ahead[-1][0], split(ahead[-1][1]))
    return (jnp.concatenate([first, second], axis=1),), ahead, [near, last]


class Gathering:
    def __init__(self, groups):
        made = [gather_steps(*group) for group in groups]
        self.states = [start for start, _, _ in made]
        self.plan = [[(0, step)] for step in made[0][1]]
        for at, (_, _, near) in enumerate(made):
            ahead = made[at + 1][1] if at + 1 < len(made) else []
            for i in range(max(len(near), len(ahead))):
                stage = [(at, near[i])] if i < len(near) else []
                self.plan.append(stage + ([(at + 1, ahead[i])] if i < len(ahead) else []))
        self.ends = [
            max(i for i, stage in enumerate(self.plan) for g, _ in stage if g == at)
            for at in range(len(made))
        ]
        self.done = 0
        self.tokens = ()

    def advance(self, *others):
        stage = self.plan[self.done]
        self.done += 1
        flat = [part for g, _ in stage for part in self.states[g]]
        flat = behind(flat, *self.tokens)
        states, received, at = [], [], 0
        for g, (send, _) in stage:
            states.append(flat[at : at + len(self.states[g])])
            at += len(self.states[g])
            received.append(send(states[-1]))
        flat = together(*[part for got in received for part in got], *others)
        at = 0
        for (g, (_, finish)), state, got in zip(stage, states, received):
            self.states[g] = finish(state, flat[at : at + len(got)])
            at += len(got)
        self.tokens = [part for g, _ in stage for part in self.states[g][:1]]
        return flat[at:]

    def until(self, group):
        while self.done <= self.ends[group]:
            self.advance()
        return self.states[group]


def behind(values, *tokens):
    return together(*values, *tokens)[: len(values)]


def add_low(kept, received):
    return (kept.astype(f32) + received.astype(f32)).astype(bf16)


def near_one_sent(first, second):
    return first[1], second[:, second.shape[1] // 2 :]


def near_one(sent):
    return exchange(sent[0], "tensor", 2), exchange(sent[1], "dp", dp_masks()[-1])


def near_one_sum(first, second, got):
    return add_low(first[0], got[0]), add_low(second[:, : second.shape[1] // 2], got[1])


def near_two(first, second):
    half = first.shape[0] // 2
    return exchange(first[half:], "dp", dp_masks()[-1]), exchange(second[1], "tensor", 2)


def near_two_sum(first, second, got):
    return add_low(first[: first.shape[0] // 2], got[0]), add_low(second[0], got[1])


def far(value, masks):
    for mask in masks[:-1]:
        value = far_sum(value, exchange(value[value.shape[0] // 2 :], "dp", mask))
    return value, exchange(value[value.shape[0] // 2 :], "dp", masks[-1])


def far_sum(value, got):
    return add_low(value[: value.shape[0] // 2], got)


class CoreFold:
    def __init__(self, own, received):
        half = own.shape[1] // 2
        self.half = half
        self.kept = (own[0], received[0], own[2:, :half], received[2:, :half])
        self.state = together(
            add_low(own[1], received[1]), add_low(own[2:, half:], received[2:, half:])
        )
        self.step = 0

    def send(self):
        return near_two(*self.state) if self.step else near_one(self.state)

    def finish(self, got):
        if self.step:
            self.state = near_two_sum(*self.state, got)
        else:
            first = self.kept[0].astype(f32) + self.kept[1].astype(f32) + got[0].astype(f32)
            second = self.kept[2].astype(f32) + self.kept[3].astype(f32) + got[1].astype(f32)
            self.state = together(first.astype(bf16), second.astype(bf16))
        self.step += 1


class Folding:
    def __init__(self, qk, vo, up, down):
        masks = dp_masks()[-2::-1]
        self.masks = masks[:-1], masks[-1:]
        self.attn = together(qk, vo)
        self.feed = jnp.concatenate([up, down], axis=1)
        self.step = 0

    def send(self):
        if self.step < 2:
            got = near_two(*self.attn) if self.step else near_one(near_one_sent(*self.attn))
            self.feed, more = far(self.feed, self.masks[self.step])
            return *got, more
        self.attn, more = far(self.attn, self.masks[self.step - 2])
        return (more,)

    def finish(self, got):
        if self.step < 2:
            self.attn = (near_two_sum if self.step else near_one_sum)(*self.attn, got[:2])
            self.feed = far_sum(self.feed, got[2])
            *self.attn, self.feed = together(*self.attn, self.feed)
            if self.step == 1:
                self.attn = jnp.concatenate(self.attn, axis=1)
        else:
            (self.attn,) = together(far_sum(self.attn, got[0]))
        self.step += 1

    def tokens(self):
        return (self.feed, self.attn) if self.step > 1 else (self.feed, *self.attn)

    def result(self):
        half, low = self.attn.shape[1] // 2, self.feed.shape[1] // 2
        parts = self.attn[:, :half], self.attn[:, half:], self.feed[:, :low], self.feed[:, low:]
        return [part.astype(f32) for part in parts]


class LastFolding:
    def __init__(self, attn, up, down):
        self.masks = dp_masks()[-2::-1]
        self.attn = attn
        self.feed = jnp.concatenate([up, down], axis=1)
        self.step = 0

    def send(self):
        first, last = self.masks[:-1], self.masks[-1:]
        self.attn, *got = far(self.attn, (dp_masks()[-1:], first, last)[self.step])
        if self.step < 2:
            self.feed, more = far(self.feed, (first, last)[self.step])
            got.append(more)
        return got

    def finish(self, got):
        self.attn = far_sum(self.attn, got[0])
        if self.step < 2:
            self.feed = far_sum(self.feed, got[1])
        self.attn, self.feed = together(self.attn, self.feed)
        self.step += 1

    result = Folding.result


def advance(folds, *others):
    received = [fold.send() for fold in folds]
    flat = together(*[part for got in received for part in got], *others)
    at = 0
    for fold, got in zip(folds, received):
        fold.finish(flat[at : at + len(got)])
        at += len(got)
    return flat[at:]


def split_low(value):
    high = value.astype(bf16)
    rest = value - high.astype(f32)
    mid = rest.astype(bf16)
    return high, mid, (rest - mid.astype(f32)).astype(bf16)


def lane_at(rows):
    return lax.broadcasted_iota(jnp.int32, (rows, WIDE - HD), 1)


def key_extra(rows, row_count, quarter, ones):
    lane = lane_at(rows)
    row = lax.broadcasted_iota(jnp.int32, (rows, WIDE - HD), 0)
    masked = lax.rem(row, quarter) >= row_count
    bias = jnp.where(masked, MASKED, 0.0).astype(f32)
    value = jnp.where(lane == 0, bias, jnp.where(lane <= ones, 1.0, 0.0))
    return value.astype(bf16)


def ones_extra(rows, ones):
    return jnp.where(lane_at(rows) < ones, 1.0, 0.0).astype(bf16)


def widen(part, extra):
    return jnp.concatenate([part, extra], axis=1)


def nt_dot(left, right):
    return lax.dot_general(left, right, (((1,), (1,)), ((), ())), preferred_element_type=f32)


def nn_dot(left, right):
    return lax.dot_general(left, right, (((1,), (0,)), ((), ())), preferred_element_type=f32)


def tn_dot(left, right):
    return lax.dot_general(left, right, (((0,), (0,)), ((), ())), preferred_element_type=f32)


def whole(shape):
    return pl.BlockSpec(shape, lambda j: (0,) * len(shape))


def single(shape):
    return pl.BlockSpec(shape, lambda j: (0,) * len(shape), pipeline_mode=pl.Buffered(1))


def attend_kernel(row_count, quarter, step, first, *refs):
    normed_a, normed_b, w_qk, w_vo, bias = refs[:5]
    if first:
        qkv, o, lse, q_s, k_s, v_s, o_s = refs[5:]
    else:
        o_before, w_before, share_a, share_b, qkv, o, lse, q_s, k_s, v_s, o_s = refs[5:]
    rows = normed_a.shape[0]
    wide = o.shape[1]
    heads = wide // HD
    k_more = key_extra(rows, row_count, quarter, 0)
    one = ones_extra(rows, 1)
    lane = lax.broadcasted_iota(jnp.int32, (1, 2 * wide), 1)
    scale = jnp.where(lane < wide, HD**-0.5 * LOG2E, 1.0)
    for half, normed in enumerate((normed_a, normed_b)):
        at = pl.ds(half * rows, rows)
        qk = ((nn_dot(normed[...], w_qk[...]) + bias[0:1, :]) * scale).astype(bf16)
        v = (nn_dot(normed[...], w_vo[:, :wide]) + bias[1:2, :wide]).astype(bf16)
        qkv[at, : 2 * wide] = qk
        qkv[at, 2 * wide :] = v
        for h in range(heads):
            low, high = h * HD, (h + 1) * HD
            q_s[h, at, :] = widen(qk[:, low:high], one)
            k_s[h, at, :] = widen(qk[:, wide + low : wide + high], k_more)
            v_s[h, at, :] = widen(v[:, low:high], one)

    def work(h, carry):
        is_total = lax.broadcasted_iota(jnp.int32, (step, WIDE), 1) == HD
        for part in range(2 * rows // step):
            at = pl.ds(part * step, step)
            scores = nt_dot(q_s[h, at, :], k_s[h])
            top = jnp.max(scores, axis=-1, keepdims=True)
            summed = nn_dot(jnp.exp2(scores - top).astype(bf16), v_s[h])
            total = summed[:, HD : HD + 1]
            o_s[h, at, :] = jnp.where(is_total, top + jnp.log2(total), summed / total)
        return carry

    lax.fori_loop(0, heads, work, 0)
    for h in range(heads):
        o[:, h * HD : (h + 1) * HD] = o_s[h][:, :HD].astype(bf16)
        lse[:, h : h + 1] = o_s[h][:, HD : HD + 1]
    if not first:
        for half, share in enumerate((share_a, share_b)):
            at = pl.ds(half * rows, rows)
            value = nt_dot(o_before[at, :], w_before[:, wide:]) + nt_dot(o[at, :], w_vo[:, wide:])
            share[...] = value.astype(share.dtype)


def attend(row_count, quarter, normed_a, normed_b, w_qk, w_vo, bias, before):
    rows, width = normed_a.shape
    wide = w_qk.shape[1] // 2
    heads = wide // HD
    operands = (normed_a, normed_b, w_qk, w_vo, bias, *before)
    outs = [
        jax.ShapeDtypeStruct((2 * rows, 3 * wide), bf16),
        jax.ShapeDtypeStruct((2 * rows, wide), bf16),
        jax.ShapeDtypeStruct((2 * rows, 8), f32),
    ]
    if before:
        outs = [jax.ShapeDtypeStruct((rows, width), kind) for kind in (f32, bf16)] + outs
    return pl.pallas_call(
        functools.partial(attend_kernel, row_count, quarter, min(512, 2 * rows), not before),
        grid=(1,),
        in_specs=[single(part.shape) for part in operands],
        out_specs=[whole(part.shape) for part in outs],
        out_shape=outs,
        scratch_shapes=[pltpu.VMEM((heads, 2 * rows, WIDE), bf16)] * 3
        + [pltpu.VMEM((heads, 2 * rows, WIDE), f32)],
        compiler_params=pltpu.CompilerParams(vmem_limit_bytes=60 * 2**20),
    )(*operands)


def attend_back_kernel(row_count, quarter, step, first, *refs):
    branch_a, branch_b, w_qk, w_vo, qkv, o, lse = refs[:7]
    if first:
        dqkv, q_s, k_s, kt_s, v_s, do_s, dq_s, dk_s, dv_s = refs[7:]
    else:
        dqkv_before, w_qk_before, w_vo_before, dn_a, dn_b = refs[7:12]
        dqkv, q_s, k_s, kt_s, v_s, do_s, dq_s, dk_s, dv_s = refs[12:]
    rows = branch_a.shape[0]
    wide = o.shape[1]
    heads = wide // HD
    k_more = key_extra(rows, row_count, quarter, 3)
    three = ones_extra(rows, 3)
    lane = lane_at(rows)

    def spread_lanes(first, parts):
        value = jnp.where(lane < first, 1.0, 0.0).astype(f32)
        for at, part in enumerate(parts):
            value = jnp.where(lane == first + at, part.astype(f32), value)
        return value.astype(bf16)

    for half, branch in enumerate((branch_a, branch_b)):
        at = pl.ds(half * rows, rows)
        grad_all = nn_dot(branch[...], w_vo[:, wide:]).astype(bf16)
        for h in range(heads):
            low, high = h * HD, (h + 1) * HD
            minus_lse = split_low(-lse[at, h : h + 1])
            q_s[h, at, :] = widen(qkv[at, low:high], spread_lanes(1, minus_lse))
            keys = widen(qkv[at, wide + low : wide + high], k_more)
            k_s[h, at, :] = keys
            kt_s[h, :, at] = jnp.transpose(keys.astype(f32)).astype(bf16)
            v_s[h, at, :] = widen(qkv[at, 2 * wide + low : 2 * wide + high], three)
            grad = grad_all[:, low:high]
            inner = jnp.sum(grad.astype(f32) * o[at, low:high].astype(f32), axis=1, keepdims=True)
            do_s[h, at, :] = widen(grad, spread_lanes(0, split_low(-inner)))

    def work(h, carry):
        for part in range(2 * rows // step):
            at = pl.ds(part * step, step)
            queries = q_s[h, at, :]
            grad_out = do_s[h, at, :]
            probs = jnp.exp2(nt_dot(k_s[h], queries))
            grad_scores = (probs * nt_dot(v_s[h], grad_out)).astype(bf16)
            grad_values = nn_dot(probs.astype(bf16), grad_out)
            grad_keys = nn_dot(grad_scores, queries)
            if part == 0:
                dv_s[h] = grad_values
                dk_s[h] = grad_keys
            else:
                dv_s[h] += grad_values
                dk_s[h] += grad_keys
            dq_s[h, at, :] = jnp.transpose(nn_dot(kt_s[h], grad_scores))
        return carry

    lax.fori_loop(0, heads, work, 0)
    for h in range(heads):
        low, high = h * HD, (h + 1) * HD
        dqkv[:, low:high] = (dq_s[h][:, :HD] * HD**-0.5).astype(bf16)
        dqkv[:, wide + low : wide + high] = (dk_s[h][:, :HD] * LN2).astype(bf16)
        dqkv[:, 2 * wide + low : 2 * wide + high] = dv_s[h][:, :HD].astype(bf16)
    if not first:
        for half, dest in enumerate((dn_a, dn_b)):
            at = pl.ds(half * rows, rows)
            part = nt_dot(dqkv[at, : 2 * wide], w_qk[...])
            part = part + nt_dot(dqkv[at, 2 * wide :], w_vo[:, :wide])
            part = part + nt_dot(dqkv_before[at, : 2 * wide], w_qk_before[...])
            part = part + nt_dot(dqkv_before[at, 2 * wide :], w_vo_before[:, :wide])
            dest[...] = part.astype(dest.dtype)


def attend_back(row_count, quarter, branch_a, branch_b, w_qk, w_vo, qkv, o, lse, before):
    rows, width = branch_a.shape
    wide = o.shape[1]
    heads = wide // HD
    operands = (branch_a, branch_b, w_qk, w_vo, qkv, o, lse, *before)
    outs = [jax.ShapeDtypeStruct((2 * rows, 3 * wide), bf16)]
    if before:
        outs = [jax.ShapeDtypeStruct((rows, width), kind) for kind in (f32, bf16)] + outs
    return pl.pallas_call(
        functools.partial(attend_back_kernel, row_count, quarter, min(512, 2 * rows), not before),
        grid=(1,),
        in_specs=[single(part.shape) for part in operands],
        out_specs=[whole(part.shape) for part in outs],
        out_shape=outs,
        scratch_shapes=[
            pltpu.VMEM((heads, 2 * rows, WIDE), bf16),
            pltpu.VMEM((heads, 2 * rows, WIDE), bf16),
            pltpu.VMEM((heads, WIDE, 2 * rows), bf16),
            pltpu.VMEM((heads, 2 * rows, WIDE), bf16),
            pltpu.VMEM((heads, 2 * rows, WIDE), bf16),
            pltpu.VMEM((heads, 2 * rows, WIDE), f32),
            pltpu.VMEM((heads, 2 * rows, WIDE), f32),
            pltpu.VMEM((heads, 2 * rows, WIDE), f32),
        ],
        compiler_params=pltpu.CompilerParams(vmem_limit_bytes=62 * 2**20),
    )(*operands)


def normalized(value):
    centred = value - jnp.mean(value, axis=-1, keepdims=True)
    scale = lax.rsqrt(jnp.mean(centred * centred, axis=-1, keepdims=True) + eps)
    return centred * scale, scale


def norm_back(value, gain, grad):
    unit, scale = normalized(value)
    scaled = grad * gain
    result = scale * (
        scaled
        - jnp.mean(scaled, axis=-1, keepdims=True)
        - unit * jnp.mean(scaled * unit, axis=-1, keepdims=True)
    )
    sums = [jnp.sum(part, axis=0, keepdims=True) for part in (grad * unit, grad)]
    return result, *sums


def gelu_both(value):
    share = 0.5 * (1.0 + lax.erf(value * math.sqrt(0.5)))
    density = jnp.exp(-0.5 * value * value) * (1.0 / math.sqrt(2.0 * math.pi))
    return (value * share).astype(bf16), (share + value * density).astype(bf16)


def feed_kernel(final, *refs):
    current, share_a, share_b, vectors, bias = refs[:5]
    ups, downs, activated, slopes = [refs[5 + 4 * i : 9 + 4 * i] for i in range(4)]
    middle, normed, total = refs[21:24]
    j = pl.program_id(0)

    @pl.when(j == 0)
    def _():
        value = current[...] + (share_a[...] + share_b[...].astype(f32) + vectors[0:1, :])
        middle[...] = value
        normed[...] = (normalized(value)[0] * vectors[1:2, :] + vectors[2:3, :]).astype(bf16)
        total[...] = value + vectors[3:4, :]

    rows_in = normed[...]
    for t in range(4):
        upward = nn_dot(rows_in, ups[t][...]) + bias[t : t + 1, :]
        activated[t][...], slopes[t][...] = gelu_both(upward)
    joined = jnp.concatenate([ref[...] for ref in activated], axis=1)
    down = jnp.concatenate([ref[...] for ref in downs], axis=1)
    total[...] += nt_dot(joined, down)
    if not final:
        following = refs[24]

        @pl.when(j == pl.num_programs(0) - 1)
        def _():
            unit, _ = normalized(total[...])
            following[...] = (unit * vectors[4:5, :] + vectors[5:6, :]).astype(bf16)


def column_block(rows, step):
    return pl.BlockSpec((rows, step), lambda j: (0, j))


def feed(final, current, share_a, share_b, vectors, bias, ups, downs):
    rows, width = current.shape
    hidden = bias.shape[1]
    step = min(256, hidden)
    rest = [f32, bf16, f32] if final else [f32, bf16, f32, bf16]
    fronts = (current, share_a, share_b, vectors)
    return pl.pallas_call(
        functools.partial(feed_kernel, final),
        grid=(hidden // step,),
        in_specs=[single(part.shape) for part in fronts]
        + [column_block(4, step)]
        + [column_block(width, step)] * 8,
        out_specs=[column_block(rows, step)] * 8 + [whole((rows, width))] * len(rest),
        out_shape=[jax.ShapeDtypeStruct((rows, hidden), bf16)] * 8
        + [jax.ShapeDtypeStruct((rows, width), kind) for kind in rest],
        compiler_params=pltpu.CompilerParams(vmem_limit_bytes=60 * 2**20),
    )(*fronts, bias, *ups, *downs)


def feed_back_kernel(final, *refs):
    count = 1 if final else 4
    fronts, refs = refs[:count], refs[count:]
    middle, normed, vectors = refs[:3]
    ups, downs, activated, slopes = [refs[3 + 4 * i : 7 + 4 * i] for i in range(4)]
    own, other, bias_grad, grad_out, branch, sums = refs[19:25]
    total, grad, grad_low, normed_t, grad_t = refs[25:]
    j = pl.program_id(0)

    @pl.when(j == 0)
    def _():
        sums[...] = jnp.zeros_like(sums)
        if final:
            value = fronts[0][...].astype(f32)
        else:
            above, layer_out, share_a, share_b = fronts
            grad_normed = share_a[...] + share_b[...].astype(f32)
            value, gain_one, shift_one = norm_back(layer_out[...], vectors[1:2, :], grad_normed)
            value = value + above[...]
            sums[4:5, :], sums[5:6, :] = gain_one, shift_one
        grad[...] = value
        low = value.astype(bf16)
        grad_low[...] = low
        sums[0:1, :] = jnp.sum(low.astype(f32), axis=0, keepdims=True)
        normed_t[...] = jnp.transpose(normed[...].astype(f32)).astype(bf16)
        grad_t[...] = jnp.transpose(low.astype(f32)).astype(bf16)
        total[...] = jnp.zeros_like(total)

    grad_rows = grad_low[...]
    grad_ups = []
    for t in range(4):
        grad_act = nn_dot(grad_rows, downs[t][...])
        scaled = grad_act * slopes[t][...].astype(f32)
        grad_ups.append(scaled.astype(bf16))
        bias_grad[t : t + 1, :] = jnp.sum(scaled, axis=0, keepdims=True)
        dest = (own, other)[t % 2]
        dest[t // 2] = nn_dot(normed_t[...], grad_ups[t]).astype(bf16)
        dest[2 + t // 2] = nn_dot(grad_t[...], activated[t][...]).astype(bf16)
    joined = jnp.concatenate(grad_ups, axis=1)
    up = jnp.concatenate([ref[...] for ref in ups], axis=1)
    total[...] += nt_dot(joined, up)

    @pl.when(j == pl.num_programs(0) - 1)
    def _():
        value, gain_two, shift_two = norm_back(middle[...], vectors[0:1, :], total[...])
        value = value + grad[...]
        grad_out[...] = value
        low = value.astype(bf16)
        branch[...] = low
        sums[1:2, :], sums[2:3, :] = gain_two, shift_two
        sums[3:4, :] = jnp.sum(low.astype(f32), axis=0, keepdims=True)


def feed_back(final, fronts, middle, normed, vectors, ups, downs, activated, slopes):
    rows, width = normed.shape
    hidden = activated[0].shape[1]
    step = min(256, hidden)
    stack = pl.BlockSpec((4, width, step), lambda j: (0, 0, j))
    singles = (*fronts, middle, normed, vectors)
    return pl.pallas_call(
        functools.partial(feed_back_kernel, final),
        grid=(hidden // step,),
        in_specs=[single(part.shape) for part in singles]
        + [column_block(width, step)] * 8
        + [column_block(rows, step)] * 8,
        out_specs=[stack] * 2
        + [column_block(4, step)]
        + [whole((rows, width))] * 2
        + [whole((8, width))],
        out_shape=[jax.ShapeDtypeStruct((4, width, hidden), bf16)] * 2
        + [
            jax.ShapeDtypeStruct((4, hidden), f32),
            jax.ShapeDtypeStruct((rows, width), f32),
            jax.ShapeDtypeStruct((rows, width), bf16),
            jax.ShapeDtypeStruct((8, width), f32),
        ],
        scratch_shapes=[pltpu.VMEM((rows, width), f32)] * 2
        + [pltpu.VMEM((rows, width), bf16)]
        + [pltpu.VMEM((width, rows), bf16)] * 2,
        compiler_params=pltpu.CompilerParams(vmem_limit_bytes=62 * 2**20),
    )(*singles, *ups, *downs, *activated, *slopes)


def local(
    frames,
    cotangent,
    qkv_weight,
    out_weight,
    up_weight,
    down_weight,
    qv_bias,
    up_bias,
    norm_gains,
    norm_shifts,
    out_biases,
):
    layers, block = qkv_weight.shape[:2]
    wide = qkv_weight.shape[3]
    row_count, width = frames.shape[1:]
    hidden = up_weight.shape[2]
    quarter = -(-row_count // 128) * 128
    rows = 2 * quarter
    count_dp = lax.axis_size("dp")
    me = lax.axis_index("dp")
    t_me = lax.axis_index("tensor")
    y_me = t_me // 2
    block_at = relative_mask(jnp.arange(count_dp)) ^ me

    norm_part, up_part, qv_part = norm_gains.shape[2], up_bias.shape[1], qv_bias.shape[2]
    lanes = max(4 * norm_part, up_part)

    def place(part, size, at):
        room = jnp.zeros((part.shape[0], size), f32)
        return lax.dynamic_update_slice(room, part, (0, at))

    def to_lanes(part):
        return jnp.pad(part, ((0, 0), (0, lanes - part.shape[1])))

    by_width = jnp.stack([norm_gains, norm_shifts, out_biases]).reshape(6 * layers, norm_part)
    by_width = to_lanes(place(by_width, 4 * norm_part, t_me * norm_part))
    own = jnp.concatenate(
        [by_width, to_lanes(qv_bias.reshape(2 * layers, qv_part)), to_lanes(up_bias)]
    )
    cut, end = 6 * layers, 8 * layers
    got = exchange(own, "tensor", 1)
    own = jnp.concatenate([own[:cut] + got[:cut], own[cut:], got[end:]])
    got = exchange(own, "tensor", 2)
    frames, got = together(frames, got)
    by_width = (own[:cut] + got[:cut])[:, : 4 * norm_part]
    by_hidden = jnp.concatenate(
        [
            place(jnp.concatenate([own[end:], got[end:]])[:, :up_part], hidden, me * up_part),
            place(
                jnp.concatenate([own[cut:end], got[cut:end]])[:, :qv_part], hidden, me * qv_part
            ),
        ]
    )

    source = jnp.repeat(block_at, block) * block + jnp.tile(jnp.arange(block), count_dp)
    to_relative = (jnp.arange(width)[:, None] == source[None, :]).astype(bf16)

    first = y_me == 0

    def other_clip(value):
        return exchange(jnp.where(first, value[1], value[0]), "tensor", 2)

    def take_clip(value, theirs):
        mine = jnp.where(first, value[0], value[1])
        padding = ((0, 0), (0, quarter - row_count), (0, 0))
        both = jnp.pad(jnp.stack([mine, theirs]), padding).reshape(rows, width)
        return nn_dot(both, to_relative)

    def give_half(value):
        return exchange(value[quarter:].astype(bf16), "tensor", 2)

    def give_clip(value, theirs):
        mine = value[:quarter]
        theirs = nt_dot(theirs, to_relative)[:row_count]
        high = mine.astype(bf16)
        low = (mine - high.astype(f32)).astype(bf16)
        mine = (nt_dot(high, to_relative) + nt_dot(low, to_relative))[:row_count]
        return jnp.stack([jnp.where(first, mine, theirs), jnp.where(first, theirs, mine)])

    current = take_clip(frames, other_clip(frames))

    groups = []
    for at in range(layers):
        qk = jnp.concatenate([qkv_weight[at, :, 0], qkv_weight[at, :, 1]], axis=1)
        vo = jnp.concatenate([qkv_weight[at, :, 2], out_weight[at].T], axis=1)
        groups += [(qk, vo), (up_weight[at], down_weight[at].T)]
    gathering = Gathering(groups)
    by_width, by_hidden = gathering.advance(by_width, by_hidden)
    for at, mask in enumerate(dp_masks()):
        got = exchange(by_width, "dp", mask), exchange(by_hidden, "dp", mask)
        if mask <= 2:
            got = gathering.advance(*got)
        else:
            got = together(*got)
        by_width = jnp.concatenate([by_width, got[0]], axis=1)
        by_hidden = by_hidden + got[1]
    gain_all, shift_all, obias_all = by_width.reshape(3, layers, 2, width)
    up_all = by_hidden[: 4 * layers].reshape(4, layers, hidden).transpose(1, 0, 2)
    qv_all = by_hidden[4 * layers :, :wide].reshape(2, layers, 2, wide).transpose(1, 0, 2, 3)

    def feed_weights(group):
        parts = gathering.until(group)
        return [
            [parts[2 * i], exchange(parts[2 * i], "tensor", 1), parts[2 * i + 1], exchange(parts[2 * i + 1], "tensor", 1)]
            for i in range(2)
        ]

    weights = []
    saved = []
    unit, _ = normalized(current)
    normed_a = (unit * gain_all[0, 0] + shift_all[0, 0]).astype(bf16)
    (normed_b,) = gathering.advance(exchange(normed_a, "tensor", 1))
    for at in range(layers):
        final = at == layers - 1
        w_qk, w_qk_other, w_vo, w_vo_other = gathering.until(2 * at)
        w_attn = ((w_qk, w_vo), (w_qk_other, w_vo_other))
        bias = jnp.pad(qv_all[at], ((0, 0), (0, 0), (0, wide)))
        heads = []
        for t in range(2):
            before = (heads[0][1], w_attn[0][1]) if t else ()
            ready = behind((normed_a, normed_b), *gathering.tokens, *before[:1])
            out = attend(row_count, quarter, *ready, *w_attn[t], bias[t], before)
            *shares, qkv, o, lse = gathering.advance(*out)
            heads.append((qkv, o, lse))
        share_b = exchange(shares[1], "tensor", 1)
        w_up, w_down = feed_weights(2 * at + 1)
        following = 0 if final else at + 1
        vectors = jnp.stack(
            [
                obias_all[at, 0],
                gain_all[at, 1],
                shift_all[at, 1],
                obias_all[at, 1],
                gain_all[following, 0],
                shift_all[following, 0],
            ]
        )
        vectors = jnp.pad(vectors, ((0, 2), (0, 0)))
        fed = feed(final, current, shares[0], share_b, vectors, up_all[at], w_up, w_down)
        if not final:
            fed = gathering.advance(*fed, *([other_clip(cotangent)] if at == 0 else []))
            if at == 0:
                *fed, clip = fed
        weights.append((w_attn, w_up, w_down))
        normed = jnp.concatenate([normed_a, normed_b], axis=0)
        saved.append((current, normed, heads, fed[:4], fed[4:8], fed[8], fed[9]))
        current = fed[10]
        if not final:
            normed_a = fed[11]
            normed_b = exchange(normed_a, "tensor", 1)
    if layers == 1:
        clip = other_clip(cotangent)
    small_grads = [None] * layers
    weight_grads = [None] * layers
    gains_one = [None] * layers
    folding = None
    fronts = (take_clip(cotangent, clip),)
    for at in reversed(range(layers)):
        final = at == layers - 1
        w_attn, w_up, w_down = weights[at]
        layer_in, normed, heads, activated, slopes, middle, normed_two = saved[at]
        uppers = [] if folding is None else [folding]
        vectors = jnp.stack([gain_all[at, 1], gain_all[0 if final else at + 1, 0]])
        vectors = jnp.pad(vectors, ((0, 6), (0, 0)))
        if uppers:
            fronts = behind(fronts, *folding.attn, folding.feed)
        fed = feed_back(
            final, fronts, middle, normed_two, vectors, w_up, w_down, activated, slopes
        )
        if final:
            *fed, half = together(*fed, give_half(current))
            encoded = give_clip(current, half)
        own, other, bup, gradient, branch_a, sums = advance(uppers, *fed)
        if not final:
            gains_one[at + 1] = sums[4:6]
        branch_b = exchange(branch_a, "tensor", 1)
        core = CoreFold(own, exchange(other, "tensor", 1))
        branch = jnp.concatenate([branch_a, branch_b], axis=0)

        def weight_grad(t, dqkv):
            dw = tn_dot(normed, dqkv).astype(bf16)
            dw_o = tn_dot(branch, heads[t][1]).astype(bf16)
            return dw[:, : 2 * wide], jnp.concatenate([dw[:, 2 * wide :], dw_o], axis=1)

        def state_tokens():
            return [*core.state, *(folding.tokens() if uppers else ())]

        ready = behind((branch_a, branch_b), *state_tokens())
        (dqkv_other,) = advance(
            [core, *uppers],
            *attend_back(row_count, quarter, *ready, *w_attn[1], *heads[1], ()),
        )
        if at == 0:
            sent = jnp.concatenate(weight_grad(1, dqkv_other), axis=1)
            got = (exchange(sent, "tensor", 2),)
        else:
            sent, got = dqkv_other, ()
        ready = behind((branch_a, branch_b), sent, *state_tokens())
        *got, share_a, share_b, dqkv_own = advance(
            [core, *uppers],
            *got,
            *attend_back(
                row_count, quarter, *ready, *w_attn[0], *heads[0], (dqkv_other, *w_attn[1])
            ),
        )
        share_a, share_b, dqkv_own = behind((share_a, share_b, dqkv_own), *core.state)
        if uppers:
            advance(uppers)
            weight_grads[at + 1] = folding.result()
        share_b = exchange(share_b, "tensor", 1)
        dw_own = weight_grad(0, dqkv_own)
        if at == 0:
            dw_own = add_low(jnp.concatenate(dw_own, axis=1), got[0])
            folding = LastFolding(dw_own, *core.state)
        else:
            dw_other = weight_grad(1, dqkv_other)
            stacks = [jnp.stack(pair) for pair in zip(dw_own, dw_other)]
            folding = Folding(*stacks, *core.state)
        dbias = jnp.stack([jnp.sum(part, axis=0, dtype=f32) for part in (dqkv_own, dqkv_other)])
        dbias = dbias.reshape(2, 3, wide)[:, 0::2]
        fronts = (gradient, layer_in, share_a, share_b)
        small_grads[at] = (sums, dbias, bup)
    grad_in, *last_sums = norm_back(
        layer_in, gain_all[0, 0], share_a + share_b.astype(f32)
    )
    gradient = gradient + grad_in
    gains_one[0] = jnp.concatenate(last_sums, axis=0)
    sums, bqv, bups = [jnp.stack([small_grads[at][i] for at in range(layers)]) for i in range(3)]
    bqv = bqv.reshape(layers, 2, 2, count_dp, qv_part).transpose(1, 0, 2, 3, 4)
    bqv = jnp.pad(bqv, ((0, 0),) * 4 + ((0, block - qv_part),)).reshape(2, 2 * layers, width)
    bups = bups.reshape(layers, 2, 2, count_dp, up_part).transpose(1, 2, 0, 3, 4)
    bups = jnp.pad(bups, ((0, 0),) * 4 + ((0, block - up_part),)).reshape(2, 2 * layers, width)
    by_hidden = jnp.concatenate([bups, bqv], axis=1).reshape(8 * layers, width)
    by_hidden = lax.dot_general(
        by_hidden,
        to_relative.astype(f32),
        (((1,), (0,)), ((), ())),
        precision=lax.Precision.HIGHEST,
        preferred_element_type=f32,
    ).reshape(2, 4 * layers, width)
    one = jnp.stack(gains_one)
    by_width = jnp.stack(
        [
            jnp.stack([one[:, 0], sums[:, 1]], axis=1),
            jnp.stack([one[:, 1], sums[:, 2]], axis=1),
            jnp.stack([sums[:, 3], sums[:, 0]], axis=1),
        ]
    ).reshape(6 * layers, width)
    small = [jnp.concatenate([by_width, by_hidden[i]]) for i in range(2)]
    advance([folding])
    gradient, *small, folding.attn, folding.feed = together(
        gradient, *small, folding.attn, folding.feed
    )
    half = give_half(gradient)
    small = small[0] + exchange(small[1], "tensor", 2)
    cut = 6 * layers
    got = exchange(
        jnp.concatenate([small[:cut], small[cut + layers : cut + 2 * layers]]), "tensor", 1
    )
    small = jnp.concatenate(
        [small[: cut + layers] + got[: cut + layers], small[cut + 2 * layers :]]
    )
    half, small = advance([folding], half, small)
    frames_grad = give_clip(gradient, half)
    for mask in reversed(dp_masks()):
        got = exchange(small[:, small.shape[1] // 2 :], "dp", mask)
        if folding.step < 3:
            (got,) = advance([folding], got)
        small = small[:, : small.shape[1] // 2] + got
    weight_grads[0] = folding.result()
    by_width = lax.dynamic_slice(small, (0, t_me * norm_part), (cut, norm_part))
    gains, shifts, obiases = by_width.reshape(3, layers, 2, norm_part)
    bups = small[cut : cut + layers, :up_part]
    bqv = small[cut + layers :, :qv_part].reshape(layers, 2, qv_part)

    def stacked(make):
        return jnp.stack([make(*weight_grads[at]) for at in range(layers)])

    return (
        encoded,
        frames_grad,
        stacked(lambda qk, vo, up, down: jnp.stack([qk[:, :wide], qk[:, wide:], vo[:, :wide]], axis=1)),
        stacked(lambda qk, vo, up, down: vo[:, wide:].T),
        stacked(lambda qk, vo, up, down: up),
        stacked(lambda qk, vo, up, down: down.T),
        bqv,
        bups,
        gains,
        shifts,
        obiases,
    )


def solution(mesh):
    in_specs = (
        P("dp", "tensor", None),
        P("dp", "tensor", None),
        P(None, "dp", None, "tensor"),
        P(None, "tensor", "dp"),
        P(None, "dp", "tensor"),
        P(None, "tensor", "dp"),
        P(None, None, ("tensor", "dp")),
        P(None, ("tensor", "dp")),
        P(None, None, ("dp", "tensor")),
        P(None, None, ("dp", "tensor")),
        P(None, None, ("dp", "tensor")),
    )
    out_specs = (
        P("dp", "tensor", None),
        P("dp", "tensor", None),
        P(None, "dp", None, "tensor"),
        P(None, "tensor", "dp"),
        P(None, "dp", "tensor"),
        P(None, "tensor", "dp"),
        P(None, None, ("tensor", "dp")),
        P(None, ("tensor", "dp")),
        P(None, None, ("dp", "tensor")),
        P(None, None, ("dp", "tensor")),
        P(None, None, ("dp", "tensor")),
    )
    return jax.shard_map(local, mesh=mesh, in_specs=in_specs, out_specs=out_specs, check_vma=False)
```

```python
import functools
import math

import jax
import jax.numpy as jnp
from jax import lax
from jax.experimental import pallas as pl
from jax.experimental.pallas import tpu as pltpu
from jax.sharding import PartitionSpec as P

HD = 64
WIDE = 128
eps = 1e-05
LOG2E = 1.0 / math.log(2.0)
LN2 = math.log(2.0)
MASKED = -1e30
bf16 = jnp.bfloat16
f32 = jnp.float32


def exchange(value, axis, mask):
    count = lax.axis_size(axis)
    return lax.ppermute(value, axis, [(i, i ^ mask) for i in range(count)])


def dp_masks():
    count = lax.axis_size("dp")
    masks = []
    while count > 1:
        count //= 2
        masks.append(count)
    return masks


def relative_mask(position):
    result = 0
    for at, mask in enumerate(dp_masks()):
        result = result + ((position >> at) & 1) * mask
    return result


def together(*values):
    return lax.optimization_barrier(values)


def gather_steps(first, second):
    masks = dp_masks()
    cut = first.shape[1]

    def z_step(mask):
        return (
            lambda state: (exchange(state[0], "dp", mask),),
            lambda state, got: (jnp.concatenate([state[0], got[0]], axis=0),),
        )

    near = (
        lambda state: (exchange(state[0], "dp", masks[-1]), exchange(state[1], "tensor", 2)),
        lambda state, got: (
            jnp.concatenate([state[0], got[0]], axis=0),
            state[1],
            got[1],
        ),
    )
    last = (
        lambda state: (
            exchange(state[0], "tensor", 2),
            exchange(state[1], "dp", masks[-1]),
            exchange(state[2], "dp", masks[-1]),
        ),
        lambda state, got: (
            state[0],
            got[0],
            *[jnp.concatenate([state[1 + i], got[1 + i]], axis=0) for i in range(2)],
        ),
    )

    def split(finish):
        def cut_last(state, got):
            block = finish(state, got)[0]
            return block[:, :cut], block[:, cut:]

        return cut_last

    ahead = [z_step(mask) for mask in masks[:-1]]
    ahead[-1] = (ahead[-1][0], split(ahead[-1][1]))
    return (jnp.concatenate([first, second], axis=1),), ahead, [near, last]


class Gathering:
    def __init__(self, groups):
        made = [gather_steps(*group) for group in groups]
        self.states = [start for start, _, _ in made]
        self.plan = [[(0, step)] for step in made[0][1]]
        for at, (_, _, near) in enumerate(made):
            ahead = made[at + 1][1] if at + 1 < len(made) else []
            late = 1 if at % 2 == 0 and at > 0 else 0
            for i in range(max(len(near), len(ahead) + late)):
                stage = [(at, near[i])] if i < len(near) else []
                j = i - late
                self.plan.append(stage + ([(at + 1, ahead[j])] if 0 <= j < len(ahead) else []))
        self.ends = [
            max(i for i, stage in enumerate(self.plan) for g, _ in stage if g == at)
            for at in range(len(made))
        ]
        self.done = 0
        self.tokens = ()

    def advance(self, *others):
        stage = self.plan[self.done]
        self.done += 1
        flat = [part for g, _ in stage for part in self.states[g]]
        flat = behind(flat, *self.tokens)
        states, received, at = [], [], 0
        for g, (send, _) in stage:
            states.append(flat[at : at + len(self.states[g])])
            at += len(self.states[g])
            received.append(send(states[-1]))
        flat = together(*[part for got in received for part in got], *others)
        at = 0
        for (g, (_, finish)), state, got in zip(stage, states, received):
            self.states[g] = finish(state, flat[at : at + len(got)])
            at += len(got)
        self.tokens = [part for g, _ in stage for part in self.states[g][:1]]
        return flat[at:]

    def until(self, group):
        while self.done <= self.ends[group]:
            self.advance()
        return self.states[group]


def behind(values, *tokens):
    return together(*values, *tokens)[: len(values)]


def add_low(kept, received):
    return (kept.astype(f32) + received.astype(f32)).astype(bf16)


def near_one_sent(first, second):
    return first[1], second[:, second.shape[1] // 2 :]


def near_one(sent):
    return exchange(sent[0], "tensor", 2), exchange(sent[1], "dp", dp_masks()[-1])


def near_one_sum(first, second, got):
    return add_low(first[0], got[0]), add_low(second[:, : second.shape[1] // 2], got[1])


def near_two(first, second):
    half = first.shape[0] // 2
    return exchange(first[half:], "dp", dp_masks()[-1]), exchange(second[1], "tensor", 2)


def near_two_sum(first, second, got):
    return add_low(first[: first.shape[0] // 2], got[0]), add_low(second[0], got[1])


def far(value, masks):
    for mask in masks[:-1]:
        value = far_sum(value, exchange(value[value.shape[0] // 2 :], "dp", mask))
    return value, exchange(value[value.shape[0] // 2 :], "dp", masks[-1])


def far_sum(value, got):
    return add_low(value[: value.shape[0] // 2], got)


class Folding:
    def __init__(self, own, other):
        masks = dp_masks()[-2::-1]
        self.masks = masks[:-1], masks[-1:]
        self.own, self.other = own, other
        self.half = own.shape[1] // 2
        self.attn = None
        self.step = 0

    def send(self):
        step = self.step
        if step == 0:
            return (exchange(self.other, "tensor", 1),)
        if step == 1:
            return near_one(self.feed)
        if step == 2:
            got = near_two(*self.feed)
            return got if self.attn is None else got + near_one(near_one_sent(*self.attn))
        if step == 3:
            self.feed, more = far(self.feed, self.masks[0])
            return *near_two(*self.attn), more
        self.attn, *got = far(self.attn, self.masks[step - 4])
        if step == 4:
            self.feed, more = far(self.feed, self.masks[1])
            got.append(more)
        return got

    def finish(self, got):
        step, half = self.step, self.half
        self.step += 1
        if step == 0:
            own, other = self.own, got[0]
            self.kept = (own[0], other[0], own[2:, :half], other[2:, :half])
            self.feed = together(
                add_low(own[1], other[1]), add_low(own[2:, half:], other[2:, half:])
            )
        elif step == 1:
            first = self.kept[0].astype(f32) + self.kept[1].astype(f32) + got[0].astype(f32)
            second = self.kept[2].astype(f32) + self.kept[3].astype(f32) + got[1].astype(f32)
            self.feed = together(first.astype(bf16), second.astype(bf16))
        elif step == 2:
            self.feed = together(*near_two_sum(*self.feed, got[:2]))
            if self.attn is not None:
                self.feed = jnp.concatenate(self.feed, axis=1)
                self.attn = near_one_sum(*self.attn, got[2:])
                self.feed, *self.attn = together(self.feed, *self.attn)
        elif step == 3:
            self.attn = jnp.concatenate(near_two_sum(*self.attn, got[:2]), axis=1)
            self.feed = far_sum(self.feed, got[2])
            self.attn, self.feed = together(self.attn, self.feed)
        else:
            self.attn = far_sum(self.attn, got[0])
            if step == 4:
                self.feed = far_sum(self.feed, got[1])
            self.attn, self.feed = together(self.attn, self.feed)

    def tokens(self):
        if self.step == 0:
            return []
        parts = self.feed if self.step < 3 and isinstance(self.feed, (list, tuple)) else (self.feed,)
        if self.attn is None:
            return list(parts)
        return [*parts, *(self.attn if isinstance(self.attn, (list, tuple)) else (self.attn,))]

    def result(self):
        half, low = self.attn.shape[1] // 2, self.feed.shape[1] // 2
        parts = self.attn[:, :half], self.attn[:, half:], self.feed[:, :low], self.feed[:, low:]
        return [part.astype(f32) for part in parts]


class LastFolding:
    def __init__(self, attn, up, down):
        self.masks = dp_masks()[-2::-1]
        self.attn = attn
        self.feed = jnp.concatenate([up, down], axis=1)
        self.step = 0

    def send(self):
        first, last = self.masks[:-1], self.masks[-1:]
        self.attn, *got = far(self.attn, (dp_masks()[-1:], first, last)[self.step])
        if self.step < 2:
            self.feed, more = far(self.feed, (first, last)[self.step])
            got.append(more)
        return got

    def finish(self, got):
        self.attn = far_sum(self.attn, got[0])
        if self.step < 2:
            self.feed = far_sum(self.feed, got[1])
        self.attn, self.feed = together(self.attn, self.feed)
        self.step += 1

    result = Folding.result


def advance(folds, *others):
    received = [fold.send() for fold in folds]
    flat = together(*[part for got in received for part in got], *others)
    at = 0
    for fold, got in zip(folds, received):
        fold.finish(flat[at : at + len(got)])
        at += len(got)
    return flat[at:]


def split_low(value):
    high = value.astype(bf16)
    rest = value - high.astype(f32)
    mid = rest.astype(bf16)
    return high, mid, (rest - mid.astype(f32)).astype(bf16)


def lane_at(rows):
    return lax.broadcasted_iota(jnp.int32, (rows, WIDE - HD), 1)


def key_extra(rows, row_count, quarter, ones):
    lane = lane_at(rows)
    row = lax.broadcasted_iota(jnp.int32, (rows, WIDE - HD), 0)
    masked = lax.rem(row, quarter) >= row_count
    bias = jnp.where(masked, MASKED, 0.0).astype(f32)
    value = jnp.where(lane == 0, bias, jnp.where(lane <= ones, 1.0, 0.0))
    return value.astype(bf16)


def ones_extra(rows, ones):
    return jnp.where(lane_at(rows) < ones, 1.0, 0.0).astype(bf16)


def widen(part, extra):
    return jnp.concatenate([part, extra], axis=1)


def nt_dot(left, right):
    return lax.dot_general(left, right, (((1,), (1,)), ((), ())), preferred_element_type=f32)


def nn_dot(left, right):
    return lax.dot_general(left, right, (((1,), (0,)), ((), ())), preferred_element_type=f32)


def tn_dot(left, right):
    return lax.dot_general(left, right, (((0,), (0,)), ((), ())), preferred_element_type=f32)


def whole(shape):
    return pl.BlockSpec(shape, lambda j: (0,) * len(shape))


def single(shape):
    return pl.BlockSpec(shape, lambda j: (0,) * len(shape), pipeline_mode=pl.Buffered(1))


def attend_kernel(row_count, quarter, step, first, *refs):
    normed_a, normed_b, w_qk, w_vo, bias = refs[:5]
    if first:
        qkv, o, lse, q_s, k_s, v_s, o_s = refs[5:]
    else:
        o_before, w_before, share_a, share_b, qkv, o, lse, q_s, k_s, v_s, o_s = refs[5:]
    rows = normed_a.shape[0]
    wide = o.shape[1]
    heads = wide // HD
    k_more = key_extra(rows, row_count, quarter, 0)
    one = ones_extra(rows, 1)
    lane = lax.broadcasted_iota(jnp.int32, (1, 2 * wide), 1)
    scale = jnp.where(lane < wide, HD**-0.5 * LOG2E, 1.0)
    for half, normed in enumerate((normed_a, normed_b)):
        at = pl.ds(half * rows, rows)
        qk = ((nn_dot(normed[...], w_qk[...]) + bias[0:1, :]) * scale).astype(bf16)
        v = (nn_dot(normed[...], w_vo[:, :wide]) + bias[1:2, :wide]).astype(bf16)
        qkv[at, : 2 * wide] = qk
        qkv[at, 2 * wide :] = v
        for h in range(heads):
            low, high = h * HD, (h + 1) * HD
            q_s[h, at, :] = widen(qk[:, low:high], one)
            k_s[h, at, :] = widen(qk[:, wide + low : wide + high], k_more)
            v_s[h, at, :] = widen(v[:, low:high], one)

    def work(h, carry):
        is_total = lax.broadcasted_iota(jnp.int32, (step, WIDE), 1) == HD
        for part in range(2 * rows // step):
            at = pl.ds(part * step, step)
            scores = nt_dot(q_s[h, at, :], k_s[h])
            top = jnp.max(scores, axis=-1, keepdims=True)
            summed = nn_dot(jnp.exp2(scores - top).astype(bf16), v_s[h])
            total = summed[:, HD : HD + 1]
            o_s[h, at, :] = jnp.where(is_total, top + jnp.log2(total), summed / total)
        return carry

    lax.fori_loop(0, heads, work, 0)
    for h in range(heads):
        o[:, h * HD : (h + 1) * HD] = o_s[h][:, :HD].astype(bf16)
        lse[:, h : h + 1] = o_s[h][:, HD : HD + 1]
    if not first:
        for half, share in enumerate((share_a, share_b)):
            at = pl.ds(half * rows, rows)
            value = nt_dot(o_before[at, :], w_before[:, wide:]) + nt_dot(o[at, :], w_vo[:, wide:])
            share[...] = value.astype(share.dtype)


def attend(row_count, quarter, normed_a, normed_b, w_qk, w_vo, bias, before):
    rows, width = normed_a.shape
    wide = w_qk.shape[1] // 2
    heads = wide // HD
    operands = (normed_a, normed_b, w_qk, w_vo, bias, *before)
    outs = [
        jax.ShapeDtypeStruct((2 * rows, 3 * wide), bf16),
        jax.ShapeDtypeStruct((2 * rows, wide), bf16),
        jax.ShapeDtypeStruct((2 * rows, 8), f32),
    ]
    if before:
        outs = [jax.ShapeDtypeStruct((rows, width), kind) for kind in (f32, bf16)] + outs
    return pl.pallas_call(
        functools.partial(attend_kernel, row_count, quarter, min(512, 2 * rows), not before),
        grid=(1,),
        in_specs=[single(part.shape) for part in operands],
        out_specs=[whole(part.shape) for part in outs],
        out_shape=outs,
        scratch_shapes=[pltpu.VMEM((heads, 2 * rows, WIDE), bf16)] * 3
        + [pltpu.VMEM((heads, 2 * rows, WIDE), f32)],
        compiler_params=pltpu.CompilerParams(vmem_limit_bytes=60 * 2**20),
    )(*operands)


def attend_back_kernel(row_count, quarter, step, first, *refs):
    branch_a, branch_b, w_qk, w_vo, qkv, o, lse = refs[:7]
    if first:
        dqkv, q_s, k_s, kt_s, v_s, do_s, dq_s, dk_s, dv_s = refs[7:]
    else:
        dqkv_before, w_qk_before, w_vo_before, dn_a, dn_b = refs[7:12]
        dqkv, q_s, k_s, kt_s, v_s, do_s, dq_s, dk_s, dv_s = refs[12:]
    rows = branch_a.shape[0]
    wide = o.shape[1]
    heads = wide // HD
    k_more = key_extra(rows, row_count, quarter, 3)
    three = ones_extra(rows, 3)
    lane = lane_at(rows)

    def spread_lanes(first, parts):
        value = jnp.where(lane < first, 1.0, 0.0).astype(f32)
        for at, part in enumerate(parts):
            value = jnp.where(lane == first + at, part.astype(f32), value)
        return value.astype(bf16)

    for half, branch in enumerate((branch_a, branch_b)):
        at = pl.ds(half * rows, rows)
        grad_all = nn_dot(branch[...], w_vo[:, wide:]).astype(bf16)
        for h in range(heads):
            low, high = h * HD, (h + 1) * HD
            minus_lse = split_low(-lse[at, h : h + 1])
            q_s[h, at, :] = widen(qkv[at, low:high], spread_lanes(1, minus_lse))
            keys = widen(qkv[at, wide + low : wide + high], k_more)
            k_s[h, at, :] = keys
            kt_s[h, :, at] = jnp.transpose(keys.astype(f32)).astype(bf16)
            v_s[h, at, :] = widen(qkv[at, 2 * wide + low : 2 * wide + high], three)
            grad = grad_all[:, low:high]
            inner = jnp.sum(grad.astype(f32) * o[at, low:high].astype(f32), axis=1, keepdims=True)
            do_s[h, at, :] = widen(grad, spread_lanes(0, split_low(-inner)))

    def work(h, carry):
        for part in range(2 * rows // step):
            at = pl.ds(part * step, step)
            queries = q_s[h, at, :]
            grad_out = do_s[h, at, :]
            probs = jnp.exp2(nt_dot(k_s[h], queries))
            grad_scores = (probs * nt_dot(v_s[h], grad_out)).astype(bf16)
            grad_values = nn_dot(probs.astype(bf16), grad_out)
            grad_keys = nn_dot(grad_scores, queries)
            if part == 0:
                dv_s[h] = grad_values
                dk_s[h] = grad_keys
            else:
                dv_s[h] += grad_values
                dk_s[h] += grad_keys
            dq_s[h, at, :] = jnp.transpose(nn_dot(kt_s[h], grad_scores))
        return carry

    lax.fori_loop(0, heads, work, 0)
    for h in range(heads):
        low, high = h * HD, (h + 1) * HD
        dqkv[:, low:high] = (dq_s[h][:, :HD] * HD**-0.5).astype(bf16)
        dqkv[:, wide + low : wide + high] = (dk_s[h][:, :HD] * LN2).astype(bf16)
        dqkv[:, 2 * wide + low : 2 * wide + high] = dv_s[h][:, :HD].astype(bf16)
    if not first:
        for half, dest in enumerate((dn_a, dn_b)):
            at = pl.ds(half * rows, rows)
            part = nt_dot(dqkv[at, : 2 * wide], w_qk[...])
            part = part + nt_dot(dqkv[at, 2 * wide :], w_vo[:, :wide])
            part = part + nt_dot(dqkv_before[at, : 2 * wide], w_qk_before[...])
            part = part + nt_dot(dqkv_before[at, 2 * wide :], w_vo_before[:, :wide])
            dest[...] = part.astype(dest.dtype)


def attend_back(row_count, quarter, branch_a, branch_b, w_qk, w_vo, qkv, o, lse, before):
    rows, width = branch_a.shape
    wide = o.shape[1]
    heads = wide // HD
    operands = (branch_a, branch_b, w_qk, w_vo, qkv, o, lse, *before)
    outs = [jax.ShapeDtypeStruct((2 * rows, 3 * wide), bf16)]
    if before:
        outs = [jax.ShapeDtypeStruct((rows, width), kind) for kind in (f32, bf16)] + outs
    return pl.pallas_call(
        functools.partial(attend_back_kernel, row_count, quarter, min(512, 2 * rows), not before),
        grid=(1,),
        in_specs=[single(part.shape) for part in operands],
        out_specs=[whole(part.shape) for part in outs],
        out_shape=outs,
        scratch_shapes=[
            pltpu.VMEM((heads, 2 * rows, WIDE), bf16),
            pltpu.VMEM((heads, 2 * rows, WIDE), bf16),
            pltpu.VMEM((heads, WIDE, 2 * rows), bf16),
            pltpu.VMEM((heads, 2 * rows, WIDE), bf16),
            pltpu.VMEM((heads, 2 * rows, WIDE), bf16),
            pltpu.VMEM((heads, 2 * rows, WIDE), f32),
            pltpu.VMEM((heads, 2 * rows, WIDE), f32),
            pltpu.VMEM((heads, 2 * rows, WIDE), f32),
        ],
        compiler_params=pltpu.CompilerParams(vmem_limit_bytes=62 * 2**20),
    )(*operands)


def normalized(value):
    centred = value - jnp.mean(value, axis=-1, keepdims=True)
    scale = lax.rsqrt(jnp.mean(centred * centred, axis=-1, keepdims=True) + eps)
    return centred * scale, scale


def norm_back(value, gain, grad):
    unit, scale = normalized(value)
    scaled = grad * gain
    result = scale * (
        scaled
        - jnp.mean(scaled, axis=-1, keepdims=True)
        - unit * jnp.mean(scaled * unit, axis=-1, keepdims=True)
    )
    sums = [jnp.sum(part, axis=0, keepdims=True) for part in (grad * unit, grad)]
    return result, *sums


def gelu_both(value):
    share = 0.5 * (1.0 + lax.erf(value * math.sqrt(0.5)))
    density = jnp.exp(-0.5 * value * value) * (1.0 / math.sqrt(2.0 * math.pi))
    return (value * share).astype(bf16), (share + value * density).astype(bf16)


def feed_kernel(final, *refs):
    current, share_a, share_b, vectors, bias = refs[:5]
    ups, downs, activated, slopes = [refs[5 + 4 * i : 9 + 4 * i] for i in range(4)]
    middle, normed, total = refs[21:24]
    j = pl.program_id(0)

    @pl.when(j == 0)
    def _():
        value = current[...] + (share_a[...] + share_b[...].astype(f32) + vectors[0:1, :])
        middle[...] = value
        normed[...] = (normalized(value)[0] * vectors[1:2, :] + vectors[2:3, :]).astype(bf16)
        total[...] = value + vectors[3:4, :]

    rows_in = normed[...]
    for t in range(4):
        upward = nn_dot(rows_in, ups[t][...]) + bias[t : t + 1, :]
        activated[t][...], slopes[t][...] = gelu_both(upward)
    joined = jnp.concatenate([ref[...] for ref in activated], axis=1)
    down = jnp.concatenate([ref[...] for ref in downs], axis=1)
    total[...] += nt_dot(joined, down)
    if not final:
        following = refs[24]

        @pl.when(j == pl.num_programs(0) - 1)
        def _():
            unit, _ = normalized(total[...])
            following[...] = (unit * vectors[4:5, :] + vectors[5:6, :]).astype(bf16)


def column_block(rows, step):
    return pl.BlockSpec((rows, step), lambda j: (0, j))


def feed(final, current, share_a, share_b, vectors, bias, ups, downs):
    rows, width = current.shape
    hidden = bias.shape[1]
    step = min(256, hidden)
    rest = [f32, bf16, f32] if final else [f32, bf16, f32, bf16]
    fronts = (current, share_a, share_b, vectors)
    return pl.pallas_call(
        functools.partial(feed_kernel, final),
        grid=(hidden // step,),
        in_specs=[single(part.shape) for part in fronts]
        + [column_block(4, step)]
        + [column_block(width, step)] * 8,
        out_specs=[column_block(rows, step)] * 8 + [whole((rows, width))] * len(rest),
        out_shape=[jax.ShapeDtypeStruct((rows, hidden), bf16)] * 8
        + [jax.ShapeDtypeStruct((rows, width), kind) for kind in rest],
        compiler_params=pltpu.CompilerParams(vmem_limit_bytes=60 * 2**20),
    )(*fronts, bias, *ups, *downs)


def feed_back_kernel(final, *refs):
    count = 1 if final else 4
    fronts, refs = refs[:count], refs[count:]
    middle, normed, vectors = refs[:3]
    ups, downs, activated, slopes = [refs[3 + 4 * i : 7 + 4 * i] for i in range(4)]
    own, other, bias_grad, grad_out, branch, sums = refs[19:25]
    total, grad, grad_low, normed_t, grad_t = refs[25:]
    j = pl.program_id(0)

    @pl.when(j == 0)
    def _():
        sums[...] = jnp.zeros_like(sums)
        if final:
            value = fronts[0][...].astype(f32)
        else:
            above, layer_out, share_a, share_b = fronts
            grad_normed = share_a[...] + share_b[...].astype(f32)
            value, gain_one, shift_one = norm_back(layer_out[...], vectors[1:2, :], grad_normed)
            value = value + above[...]
            sums[4:5, :], sums[5:6, :] = gain_one, shift_one
        grad[...] = value
        low = value.astype(bf16)
        grad_low[...] = low
        sums[0:1, :] = jnp.sum(low.astype(f32), axis=0, keepdims=True)
        normed_t[...] = jnp.transpose(normed[...].astype(f32)).astype(bf16)
        grad_t[...] = jnp.transpose(low.astype(f32)).astype(bf16)
        total[...] = jnp.zeros_like(total)

    grad_rows = grad_low[...]
    grad_ups = []
    for t in range(4):
        grad_act = nn_dot(grad_rows, downs[t][...])
        scaled = grad_act * slopes[t][...].astype(f32)
        grad_ups.append(scaled.astype(bf16))
        bias_grad[t : t + 1, :] = jnp.sum(scaled, axis=0, keepdims=True)
        dest = (own, other)[t % 2]
        dest[t // 2] = nn_dot(normed_t[...], grad_ups[t]).astype(bf16)
        dest[2 + t // 2] = nn_dot(grad_t[...], activated[t][...]).astype(bf16)
    joined = jnp.concatenate(grad_ups, axis=1)
    up = jnp.concatenate([ref[...] for ref in ups], axis=1)
    total[...] += nt_dot(joined, up)

    @pl.when(j == pl.num_programs(0) - 1)
    def _():
        value, gain_two, shift_two = norm_back(middle[...], vectors[0:1, :], total[...])
        value = value + grad[...]
        grad_out[...] = value
        low = value.astype(bf16)
        branch[...] = low
        sums[1:2, :], sums[2:3, :] = gain_two, shift_two
        sums[3:4, :] = jnp.sum(low.astype(f32), axis=0, keepdims=True)


def feed_back(final, fronts, middle, normed, vectors, ups, downs, activated, slopes):
    rows, width = normed.shape
    hidden = activated[0].shape[1]
    step = min(256, hidden)
    stack = pl.BlockSpec((4, width, step), lambda j: (0, 0, j))
    singles = (*fronts, middle, normed, vectors)
    return pl.pallas_call(
        functools.partial(feed_back_kernel, final),
        grid=(hidden // step,),
        in_specs=[single(part.shape) for part in singles]
        + [column_block(width, step)] * 8
        + [column_block(rows, step)] * 8,
        out_specs=[stack] * 2
        + [column_block(4, step)]
        + [whole((rows, width))] * 2
        + [whole((8, width))],
        out_shape=[jax.ShapeDtypeStruct((4, width, hidden), bf16)] * 2
        + [
            jax.ShapeDtypeStruct((4, hidden), f32),
            jax.ShapeDtypeStruct((rows, width), f32),
            jax.ShapeDtypeStruct((rows, width), bf16),
            jax.ShapeDtypeStruct((8, width), f32),
        ],
        scratch_shapes=[pltpu.VMEM((rows, width), f32)] * 2
        + [pltpu.VMEM((rows, width), bf16)]
        + [pltpu.VMEM((width, rows), bf16)] * 2,
        compiler_params=pltpu.CompilerParams(vmem_limit_bytes=62 * 2**20),
    )(*singles, *ups, *downs, *activated, *slopes)


def local(
    frames,
    cotangent,
    qkv_weight,
    out_weight,
    up_weight,
    down_weight,
    qv_bias,
    up_bias,
    norm_gains,
    norm_shifts,
    out_biases,
):
    layers, block = qkv_weight.shape[:2]
    wide = qkv_weight.shape[3]
    row_count, width = frames.shape[1:]
    hidden = up_weight.shape[2]
    quarter = -(-row_count // 128) * 128
    rows = 2 * quarter
    count_dp = lax.axis_size("dp")
    me = lax.axis_index("dp")
    t_me = lax.axis_index("tensor")
    y_me = t_me // 2
    block_at = relative_mask(jnp.arange(count_dp)) ^ me

    norm_part, up_part, qv_part = norm_gains.shape[2], up_bias.shape[1], qv_bias.shape[2]
    lanes = max(4 * norm_part, up_part)

    def place(part, size, at):
        room = jnp.zeros((part.shape[0], size), f32)
        return lax.dynamic_update_slice(room, part, (0, at))

    def to_lanes(part):
        return jnp.pad(part, ((0, 0), (0, lanes - part.shape[1])))

    by_width = jnp.stack([norm_gains, norm_shifts, out_biases]).reshape(6 * layers, norm_part)
    by_width = to_lanes(place(by_width, 4 * norm_part, t_me * norm_part))
    own = jnp.concatenate(
        [by_width, to_lanes(qv_bias.reshape(2 * layers, qv_part)), to_lanes(up_bias)]
    )
    cut, end = 6 * layers, 8 * layers
    got = exchange(own, "tensor", 1)
    own = jnp.concatenate([own[:cut] + got[:cut], own[cut:], got[end:]])
    got = exchange(own, "tensor", 2)
    frames, got = together(frames, got)
    by_width = (own[:cut] + got[:cut])[:, : 4 * norm_part]
    by_hidden = jnp.concatenate(
        [
            place(jnp.concatenate([own[end:], got[end:]])[:, :up_part], hidden, me * up_part),
            place(
                jnp.concatenate([own[cut:end], got[cut:end]])[:, :qv_part], hidden, me * qv_part
            ),
        ]
    )

    source = jnp.repeat(block_at, block) * block + jnp.tile(jnp.arange(block), count_dp)
    to_relative = (jnp.arange(width)[:, None] == source[None, :]).astype(bf16)

    first = y_me == 0

    def other_clip(value):
        return jnp.where(first, value[1], value[0])

    def take_clip(value, theirs):
        mine = jnp.where(first, value[0], value[1])
        padding = ((0, 0), (0, quarter - row_count), (0, 0))
        both = jnp.pad(jnp.stack([mine, theirs]), padding).reshape(rows, width)
        return nn_dot(both, to_relative)

    def give_half(value):
        return exchange(value[quarter:].astype(bf16), "tensor", 2)

    def give_clip(value, theirs):
        mine = value[:quarter]
        theirs = nt_dot(theirs, to_relative)[:row_count]
        high = mine.astype(bf16)
        low = (mine - high.astype(f32)).astype(bf16)
        mine = (nt_dot(high, to_relative) + nt_dot(low, to_relative))[:row_count]
        return jnp.stack([jnp.where(first, mine, theirs), jnp.where(first, theirs, mine)])

    current = take_clip(frames, exchange(other_clip(frames), "tensor", 2))
    clip = other_clip(cotangent)

    groups = []
    for at in range(layers):
        qk = jnp.concatenate([qkv_weight[at, :, 0], qkv_weight[at, :, 1]], axis=1)
        vo = jnp.concatenate([qkv_weight[at, :, 2], out_weight[at].T], axis=1)
        groups += [(qk, vo), (up_weight[at], down_weight[at].T)]
    gathering = Gathering(groups)
    by_width, by_hidden = gathering.advance(by_width, by_hidden)
    for at, mask in enumerate(dp_masks()):
        got = exchange(by_width, "dp", mask), exchange(by_hidden, "dp", mask)
        if mask > 2:
            got = together(*got)
        elif mask == 2:
            *got, clip = gathering.advance(*got, clip)
        else:
            got = got[0], *gathering.advance(got[1])
        by_width = jnp.concatenate([by_width, got[0]], axis=1)
        by_hidden = by_hidden + got[1]
    gain_all, shift_all, obias_all = by_width.reshape(3, layers, 2, width)
    up_all = by_hidden[: 4 * layers].reshape(4, layers, hidden).transpose(1, 0, 2)
    qv_all = by_hidden[4 * layers :, :wide].reshape(2, layers, 2, wide).transpose(1, 0, 2, 3)

    def feed_weights(group):
        parts = gathering.until(group)
        return [
            [parts[2 * i], exchange(parts[2 * i], "tensor", 1), parts[2 * i + 1], exchange(parts[2 * i + 1], "tensor", 1)]
            for i in range(2)
        ]

    weights = []
    saved = []
    unit, _ = normalized(current)
    normed_a = (unit * gain_all[0, 0] + shift_all[0, 0]).astype(bf16)
    (normed_b,) = gathering.advance(exchange(normed_a, "tensor", 1))
    for at in range(layers):
        final = at == layers - 1
        w_qk, w_qk_other, w_vo, w_vo_other = gathering.until(2 * at)
        w_attn = ((w_qk, w_vo), (w_qk_other, w_vo_other))
        bias = jnp.pad(qv_all[at], ((0, 0), (0, 0), (0, wide)))
        heads = []
        for t in range(2):
            before = (heads[0][1], w_attn[0][1]) if t else ()
            ready = behind((normed_a, normed_b), *gathering.tokens, *before[:1])
            out = attend(row_count, quarter, *ready, *w_attn[t], bias[t], before)
            *shares, qkv, o, lse = gathering.advance(*out)
            heads.append((qkv, o, lse))
        share_b = exchange(shares[1], "tensor", 1)
        if not final:
            (share_b,) = gathering.advance(share_b)
        w_up, w_down = feed_weights(2 * at + 1)
        following = 0 if final else at + 1
        vectors = jnp.stack(
            [
                obias_all[at, 0],
                gain_all[at, 1],
                shift_all[at, 1],
                obias_all[at, 1],
                gain_all[following, 0],
                shift_all[following, 0],
            ]
        )
        vectors = jnp.pad(vectors, ((0, 2), (0, 0)))
        fed = feed(final, current, shares[0], share_b, vectors, up_all[at], w_up, w_down)
        if not final:
            fed = gathering.advance(*fed, *([exchange(clip, "tensor", 2)] if at == 0 else []))
            if at == 0:
                *fed, clip = fed
        weights.append((w_attn, w_up, w_down))
        normed = jnp.concatenate([normed_a, normed_b], axis=0)
        saved.append((current, normed, heads, fed[:4], fed[4:8], fed[8], fed[9]))
        current = fed[10]
        if not final:
            normed_a = fed[11]
            (normed_b,) = gathering.advance(exchange(normed_a, "tensor", 1))
    if layers == 1:
        clip = exchange(clip, "tensor", 2)
    small_grads = [None] * layers
    weight_grads = [None] * layers
    gains_one = [None] * layers
    folding = None
    fronts = (take_clip(cotangent, clip),)
    for at in reversed(range(layers)):
        final = at == layers - 1
        w_attn, w_up, w_down = weights[at]
        layer_in, normed, heads, activated, slopes, middle, normed_two = saved[at]
        uppers = [] if folding is None else [folding]
        vectors = jnp.stack([gain_all[at, 1], gain_all[0 if final else at + 1, 0]])
        vectors = jnp.pad(vectors, ((0, 6), (0, 0)))
        if uppers:
            fronts = behind(fronts, *folding.tokens())
        fed = feed_back(
            final, fronts, middle, normed_two, vectors, w_up, w_down, activated, slopes
        )
        if final:
            *fed, encoded_half = together(*fed, give_half(current))
        own, other, bup, gradient, branch_a, sums = advance(uppers, *fed)
        if not final:
            gains_one[at + 1] = sums[4:6]
        branch_b = exchange(branch_a, "tensor", 1)
        core = Folding(own, other)
        branch = jnp.concatenate([branch_a, branch_b], axis=0)

        def weight_grad(t, dqkv):
            dw = tn_dot(normed, dqkv).astype(bf16)
            dw_o = tn_dot(branch, heads[t][1]).astype(bf16)
            return dw[:, : 2 * wide], jnp.concatenate([dw[:, 2 * wide :], dw_o], axis=1)

        def state_tokens():
            return [part for fold in (core, *uppers) for part in fold.tokens()]

        if at == 0:
            advance([core, *uppers])
        elif uppers:
            advance(uppers)
        ready = behind((branch_a, branch_b), *state_tokens())
        (dqkv_other,) = advance(
            [core, *uppers],
            *attend_back(row_count, quarter, *ready, *w_attn[1], *heads[1], ()),
        )
        if at == 0:
            sent = jnp.concatenate(weight_grad(1, dqkv_other), axis=1)
            got = (exchange(sent, "tensor", 2),)
        else:
            sent, got = dqkv_other, ()
        ready = behind((branch_a, branch_b), sent, *state_tokens())
        *got, share_a, share_b, dqkv_own = advance(
            [core, *uppers],
            *got,
            *attend_back(
                row_count, quarter, *ready, *w_attn[0], *heads[0], (dqkv_other, *w_attn[1])
            ),
        )
        if uppers:
            weight_grads[at + 1] = folding.result()
        share_b = exchange(share_b, "tensor", 1)
        dw_own = weight_grad(0, dqkv_own)
        if at == 0:
            dw_own = add_low(jnp.concatenate(dw_own, axis=1), got[0])
            folding = LastFolding(dw_own, *core.feed)
        else:
            dw_other = weight_grad(1, dqkv_other)
            core.attn = together(*[jnp.stack(pair) for pair in zip(dw_own, dw_other)])
            folding = core
        fronts = (gradient, layer_in, share_a, share_b)
        small_grads[at] = (sums, (dqkv_own, dqkv_other), bup)
    grad_in, *last_sums = norm_back(
        layer_in, gain_all[0, 0], share_a + share_b.astype(f32)
    )
    gradient = gradient + grad_in
    gains_one[0] = jnp.concatenate(last_sums, axis=0)
    pairs = behind(
        [part for at in range(1, layers) for part in small_grads[at][1]], *small_grads[0][1]
    )
    pairs = [*small_grads[0][1], *pairs]
    bqv = jnp.stack([jnp.sum(part, axis=0, dtype=f32) for part in pairs])
    bqv = bqv.reshape(layers, 2, 3, count_dp, qv_part)[:, :, 0::2].transpose(1, 0, 2, 3, 4)
    bqv = jnp.pad(bqv, ((0, 0),) * 4 + ((0, block - qv_part),)).reshape(4 * layers, width)
    sums, bups = [jnp.stack([small_grads[at][i] for at in range(layers)]) for i in (0, 2)]
    bups = bups.reshape(layers, 4, count_dp, up_part).transpose(1, 0, 2, 3)
    bups = jnp.pad(bups, ((0, 0),) * 3 + ((0, block - up_part),)).reshape(4 * layers, width)
    by_hidden = lax.dot_general(
        jnp.concatenate([bups, bqv]),
        to_relative.astype(f32),
        (((1,), (0,)), ((), ())),
        precision=lax.Precision.HIGHEST,
        preferred_element_type=f32,
    )
    bups, bqv = by_hidden[: 4 * layers], by_hidden[4 * layers :]
    one = jnp.stack(gains_one)
    by_width = jnp.stack(
        [
            jnp.stack([one[:, 0], sums[:, 1]], axis=1),
            jnp.stack([one[:, 1], sums[:, 2]], axis=1),
            jnp.stack([sums[:, 3], sums[:, 0]], axis=1),
        ]
    ).reshape(6 * layers, width)
    small = [
        jnp.concatenate(
            [by_width, bups[t * layers : (t + 1) * layers]]
            + ([bqv[t * layers : (t + 2) * layers]] if t % 2 == 0 else [])
        )
        for t in range(4)
    ]
    advance([folding])
    gradient, *small, folding.attn, folding.feed = together(
        gradient, *small, folding.attn, folding.feed
    )
    half, *got = advance(
        [folding],
        give_half(gradient),
        *[exchange(small[t], "tensor", t) for t in range(1, 4)],
    )
    cut = 6 * layers
    small, more = small[0] + got[1], got[0] + got[2]
    small = jnp.concatenate([small[: cut + layers] + more, small[cut + layers :]])
    encoded = give_clip(*behind((current, encoded_half), *small_grads[0][1]))
    frames_grad = give_clip(gradient, half)
    for mask in reversed(dp_masks()):
        got = exchange(small[:, small.shape[1] // 2 :], "dp", mask)
        if folding.step < 3:
            (got,) = advance([folding], got)
        small = small[:, : small.shape[1] // 2] + got
    weight_grads[0] = folding.result()
    by_width = lax.dynamic_slice(small, (0, t_me * norm_part), (cut, norm_part))
    gains, shifts, obiases = by_width.reshape(3, layers, 2, norm_part)
    bups = small[cut : cut + layers, :up_part]
    bqv = small[cut + layers :, :qv_part].reshape(layers, 2, qv_part)

    def stacked(make):
        return jnp.stack([make(*weight_grads[at]) for at in range(layers)])

    return (
        encoded,
        frames_grad,
        stacked(lambda qk, vo, up, down: jnp.stack([qk[:, :wide], qk[:, wide:], vo[:, :wide]], axis=1)),
        stacked(lambda qk, vo, up, down: vo[:, wide:].T),
        stacked(lambda qk, vo, up, down: up),
        stacked(lambda qk, vo, up, down: down.T),
        bqv,
        bups,
        gains,
        shifts,
        obiases,
    )


def solution(mesh):
    in_specs = (
        P("dp", "tensor", None),
        P("dp", "tensor", None),
        P(None, "dp", None, "tensor"),
        P(None, "tensor", "dp"),
        P(None, "dp", "tensor"),
        P(None, "tensor", "dp"),
        P(None, None, ("tensor", "dp")),
        P(None, ("tensor", "dp")),
        P(None, None, ("dp", "tensor")),
        P(None, None, ("dp", "tensor")),
        P(None, None, ("dp", "tensor")),
    )
    out_specs = (
        P("dp", "tensor", None),
        P("dp", "tensor", None),
        P(None, "dp", None, "tensor"),
        P(None, "tensor", "dp"),
        P(None, "dp", "tensor"),
        P(None, "tensor", "dp"),
        P(None, None, ("tensor", "dp")),
        P(None, ("tensor", "dp")),
        P(None, None, ("dp", "tensor")),
        P(None, None, ("dp", "tensor")),
        P(None, None, ("dp", "tensor")),
    )
    return jax.shard_map(local, mesh=mesh, in_specs=in_specs, out_specs=out_specs, check_vma=False)
```

```python
import functools
import math

import jax
import jax.numpy as jnp
from jax import lax
from jax.experimental import pallas as pl
from jax.experimental.pallas import tpu as pltpu
from jax.sharding import PartitionSpec as P

HD = 64
WIDE = 128
eps = 1e-05
LOG2E = 1.0 / math.log(2.0)
LN2 = math.log(2.0)
MASKED = -1e30
bf16 = jnp.bfloat16
f32 = jnp.float32


def exchange(value, axis, mask):
    count = lax.axis_size(axis)
    return lax.ppermute(value, axis, [(i, i ^ mask) for i in range(count)])


def dp_masks():
    count = lax.axis_size("dp")
    masks = []
    while count > 1:
        count //= 2
        masks.append(count)
    return masks


def relative_mask(position):
    result = 0
    for at, mask in enumerate(dp_masks()):
        result = result + ((position >> at) & 1) * mask
    return result


def together(*values):
    return lax.optimization_barrier(values)


def gather_steps(first, second):
    masks = dp_masks()
    cut = first.shape[1]

    def z_step(mask):
        return (
            lambda state: (exchange(state[0], "dp", mask),),
            lambda state, got: (jnp.concatenate([state[0], got[0]], axis=0),),
        )

    near = (
        lambda state: (exchange(state[0], "dp", masks[-1]), exchange(state[1], "tensor", 2)),
        lambda state, got: (
            jnp.concatenate([state[0], got[0]], axis=0),
            state[1],
            got[1],
        ),
    )
    last = (
        lambda state: (
            exchange(state[0], "tensor", 2),
            exchange(state[1], "dp", masks[-1]),
            exchange(state[2], "dp", masks[-1]),
        ),
        lambda state, got: (
            state[0],
            got[0],
            *[jnp.concatenate([state[1 + i], got[1 + i]], axis=0) for i in range(2)],
        ),
    )

    def split(finish):
        def cut_last(state, got):
            block = finish(state, got)[0]
            return block[:, :cut], block[:, cut:]

        return cut_last

    ahead = [z_step(mask) for mask in masks[:-1]]
    ahead[-1] = (ahead[-1][0], split(ahead[-1][1]))
    return (jnp.concatenate([first, second], axis=1),), ahead, [near, last]


class Gathering:
    def __init__(self, groups):
        made = [gather_steps(*group) for group in groups]
        self.states = [start for start, _, _ in made]
        self.plan = [[(0, step)] for step in made[0][1]]
        for at, (_, _, near) in enumerate(made):
            ahead = made[at + 1][1] if at + 1 < len(made) else []
            late = 1 if at % 2 == 0 and at > 0 else 0
            for i in range(max(len(near), len(ahead) + late)):
                stage = [(at, near[i])] if i < len(near) else []
                j = i - late
                self.plan.append(stage + ([(at + 1, ahead[j])] if 0 <= j < len(ahead) else []))
        self.ends = [
            max(i for i, stage in enumerate(self.plan) for g, _ in stage if g == at)
            for at in range(len(made))
        ]
        self.done = 0
        self.tokens = ()

    def advance(self, *others):
        stage = self.plan[self.done]
        self.done += 1
        flat = [part for g, _ in stage for part in self.states[g]]
        flat = behind(flat, *self.tokens)
        states, received, at = [], [], 0
        for g, (send, _) in stage:
            states.append(flat[at : at + len(self.states[g])])
            at += len(self.states[g])
            received.append(send(states[-1]))
        flat = together(*[part for got in received for part in got], *others)
        at = 0
        for (g, (_, finish)), state, got in zip(stage, states, received):
            self.states[g] = finish(state, flat[at : at + len(got)])
            at += len(got)
        self.tokens = [part for g, _ in stage for part in self.states[g][:1]]
        return flat[at:]

    def until(self, group):
        while self.done <= self.ends[group]:
            self.advance()
        return self.states[group]


def behind(values, *tokens):
    return together(*values, *tokens)[: len(values)]


def add_low(kept, received):
    return (kept.astype(f32) + received.astype(f32)).astype(bf16)


def near_one_sent(first, second):
    return first[1], second[:, second.shape[1] // 2 :]


def near_one(sent):
    return exchange(sent[0], "tensor", 2), exchange(sent[1], "dp", dp_masks()[-1])


def near_one_sum(first, second, got):
    return add_low(first[0], got[0]), add_low(second[:, : second.shape[1] // 2], got[1])


def near_two(first, second):
    half = first.shape[0] // 2
    return exchange(first[half:], "dp", dp_masks()[-1]), exchange(second[1], "tensor", 2)


def near_two_sum(first, second, got):
    return add_low(first[: first.shape[0] // 2], got[0]), add_low(second[0], got[1])


def far(value, masks):
    for mask in masks[:-1]:
        value = far_sum(value, exchange(value[value.shape[0] // 2 :], "dp", mask))
    return value, exchange(value[value.shape[0] // 2 :], "dp", masks[-1])


def far_sum(value, got):
    return add_low(value[: value.shape[0] // 2], got)


class Folding:
    def __init__(self, own, other):
        masks = dp_masks()[-2::-1]
        self.masks = masks[:-1], masks[-1:]
        self.own, self.other = own, other
        self.half = own.shape[1] // 2
        self.attn = None
        self.step = 0

    def send(self):
        step = self.step
        if step == 0:
            return (exchange(self.other, "tensor", 1),)
        if step == 1:
            return near_one(self.feed)
        if step == 2:
            got = near_two(*self.feed)
            return got if self.attn is None else got + near_one(near_one_sent(*self.attn))
        if step == 3:
            self.feed, more = far(self.feed, self.masks[0])
            return *near_two(*self.attn), more
        self.attn, *got = far(self.attn, self.masks[step - 4])
        if step == 4:
            self.feed, more = far(self.feed, self.masks[1])
            got.append(more)
        return got

    def finish(self, got):
        step, half = self.step, self.half
        self.step += 1
        if step == 0:
            own, other = self.own, got[0]
            self.kept = (own[0], other[0], own[2:, :half], other[2:, :half])
            self.feed = together(
                add_low(own[1], other[1]), add_low(own[2:, half:], other[2:, half:])
            )
        elif step == 1:
            first = self.kept[0].astype(f32) + self.kept[1].astype(f32) + got[0].astype(f32)
            second = self.kept[2].astype(f32) + self.kept[3].astype(f32) + got[1].astype(f32)
            self.feed = together(first.astype(bf16), second.astype(bf16))
        elif step == 2:
            self.feed = together(*near_two_sum(*self.feed, got[:2]))
            if self.attn is not None:
                self.feed = jnp.concatenate(self.feed, axis=1)
                self.attn = near_one_sum(*self.attn, got[2:])
                self.feed, *self.attn = together(self.feed, *self.attn)
        elif step == 3:
            self.attn = jnp.concatenate(near_two_sum(*self.attn, got[:2]), axis=1)
            self.feed = far_sum(self.feed, got[2])
            self.attn, self.feed = together(self.attn, self.feed)
        else:
            self.attn = far_sum(self.attn, got[0])
            if step == 4:
                self.feed = far_sum(self.feed, got[1])
            self.attn, self.feed = together(self.attn, self.feed)

    def tokens(self):
        if self.step == 0:
            return []
        parts = self.feed if self.step < 3 and isinstance(self.feed, (list, tuple)) else (self.feed,)
        if self.attn is None:
            return list(parts)
        return [*parts, *(self.attn if isinstance(self.attn, (list, tuple)) else (self.attn,))]

    def result(self):
        half, low = self.attn.shape[1] // 2, self.feed.shape[1] // 2
        parts = self.attn[:, :half], self.attn[:, half:], self.feed[:, :low], self.feed[:, low:]
        return [part.astype(f32) for part in parts]


class LastFolding:
    def __init__(self, attn, up, down):
        self.masks = dp_masks()[-2::-1]
        self.attn = attn
        self.feed = jnp.concatenate([up, down], axis=1)
        self.step = 0

    def send(self):
        first, last = self.masks[:-1], self.masks[-1:]
        self.attn, *got = far(self.attn, (dp_masks()[-1:], first, last)[self.step])
        if self.step < 2:
            self.feed, more = far(self.feed, (first, last)[self.step])
            got.append(more)
        return got

    def finish(self, got):
        self.attn = far_sum(self.attn, got[0])
        if self.step < 2:
            self.feed = far_sum(self.feed, got[1])
        self.attn, self.feed = together(self.attn, self.feed)
        self.step += 1

    result = Folding.result


def advance(folds, *others):
    received = [fold.send() for fold in folds]
    flat = together(*[part for got in received for part in got], *others)
    at = 0
    for fold, got in zip(folds, received):
        fold.finish(flat[at : at + len(got)])
        at += len(got)
    return flat[at:]


def split_low(value):
    high = value.astype(bf16)
    rest = value - high.astype(f32)
    mid = rest.astype(bf16)
    return high, mid, (rest - mid.astype(f32)).astype(bf16)


def lane_at(rows):
    return lax.broadcasted_iota(jnp.int32, (rows, WIDE - HD), 1)


def key_extra(rows, row_count, quarter, ones):
    lane = lane_at(rows)
    row = lax.broadcasted_iota(jnp.int32, (rows, WIDE - HD), 0)
    masked = lax.rem(row, quarter) >= row_count
    bias = jnp.where(masked, MASKED, 0.0).astype(f32)
    value = jnp.where(lane == 0, bias, jnp.where(lane <= ones, 1.0, 0.0))
    return value.astype(bf16)


def ones_extra(rows, ones):
    return jnp.where(lane_at(rows) < ones, 1.0, 0.0).astype(bf16)


def widen(part, extra):
    return jnp.concatenate([part, extra], axis=1)


def nt_dot(left, right):
    return lax.dot_general(left, right, (((1,), (1,)), ((), ())), preferred_element_type=f32)


def nn_dot(left, right):
    return lax.dot_general(left, right, (((1,), (0,)), ((), ())), preferred_element_type=f32)


def tn_dot(left, right):
    return lax.dot_general(left, right, (((0,), (0,)), ((), ())), preferred_element_type=f32)


def whole(shape):
    return pl.BlockSpec(shape, lambda j: (0,) * len(shape))


def single(shape):
    return pl.BlockSpec(shape, lambda j: (0,) * len(shape), pipeline_mode=pl.Buffered(1))


def attend_kernel(row_count, quarter, step, row, first, *refs):
    normed_a, normed_b, w_qk, w_vo, bias = refs[:5]
    if first:
        qkv, o, lse, q_s, k_s, v_s, o_s = refs[5:]
    else:
        o_before, w_before, share_a, share_b, qkv, o, lse, q_s, k_s, v_s, o_s = refs[5:]
    rows = normed_a.shape[0]
    wide = o.shape[1]
    heads = wide // HD
    k_more = key_extra(rows, row_count, quarter, 0)
    one = ones_extra(rows, 1)
    lane = lax.broadcasted_iota(jnp.int32, (1, 2 * wide), 1)
    scale = jnp.where(lane < wide, HD**-0.5 * LOG2E, 1.0)
    for half, normed in enumerate((normed_a, normed_b)):
        at = pl.ds(half * rows, rows)
        qk = nn_dot(normed[...], w_qk[...]) + bias[row : row + 1, : 2 * wide]
        qk = (qk * scale).astype(bf16)
        v = nn_dot(normed[...], w_vo[:, :wide]) + bias[row + 1 : row + 2, :wide]
        v = v.astype(bf16)
        qkv[at, : 2 * wide] = qk
        qkv[at, 2 * wide :] = v
        for h in range(heads):
            low, high = h * HD, (h + 1) * HD
            q_s[h, at, :] = widen(qk[:, low:high], one)
            k_s[h, at, :] = widen(qk[:, wide + low : wide + high], k_more)
            v_s[h, at, :] = widen(v[:, low:high], one)

    def work(h, carry):
        is_total = lax.broadcasted_iota(jnp.int32, (step, WIDE), 1) == HD
        for part in range(2 * rows // step):
            at = pl.ds(part * step, step)
            scores = nt_dot(q_s[h, at, :], k_s[h])
            top = jnp.max(scores, axis=-1, keepdims=True)
            summed = nn_dot(jnp.exp2(scores - top).astype(bf16), v_s[h])
            total = summed[:, HD : HD + 1]
            o_s[h, at, :] = jnp.where(is_total, top + jnp.log2(total), summed / total)
        return carry

    lax.fori_loop(0, heads, work, 0)
    for h in range(heads):
        o[:, h * HD : (h + 1) * HD] = o_s[h][:, :HD].astype(bf16)
        lse[:, h : h + 1] = o_s[h][:, HD : HD + 1]
    if not first:
        for half, share in enumerate((share_a, share_b)):
            at = pl.ds(half * rows, rows)
            value = nt_dot(o_before[at, :], w_before[:, wide:]) + nt_dot(o[at, :], w_vo[:, wide:])
            share[...] = value.astype(share.dtype)


def attend(row_count, quarter, row, normed_a, normed_b, w_qk, w_vo, bias, before):
    rows, width = normed_a.shape
    wide = w_qk.shape[1] // 2
    heads = wide // HD
    operands = (normed_a, normed_b, w_qk, w_vo, bias, *before)
    outs = [
        jax.ShapeDtypeStruct((2 * rows, 3 * wide), bf16),
        jax.ShapeDtypeStruct((2 * rows, wide), bf16),
        jax.ShapeDtypeStruct((2 * rows, 8), f32),
    ]
    if before:
        outs = [jax.ShapeDtypeStruct((rows, width), kind) for kind in (f32, bf16)] + outs
    return pl.pallas_call(
        functools.partial(attend_kernel, row_count, quarter, min(512, 2 * rows), row, not before),
        grid=(1,),
        in_specs=[single(part.shape) for part in operands],
        out_specs=[whole(part.shape) for part in outs],
        out_shape=outs,
        scratch_shapes=[pltpu.VMEM((heads, 2 * rows, WIDE), bf16)] * 3
        + [pltpu.VMEM((heads, 2 * rows, WIDE), f32)],
        compiler_params=pltpu.CompilerParams(vmem_limit_bytes=60 * 2**20),
    )(*operands)


def attend_back_kernel(row_count, quarter, step, first, *refs):
    branch_a, branch_b, w_qk, w_vo, qkv, o, lse = refs[:7]
    if first:
        dqkv, sums, q_s, k_s, kt_s, v_s, do_s, dq_s, dk_s, dv_s = refs[7:]
    else:
        dqkv_before, w_qk_before, w_vo_before, dn_a, dn_b = refs[7:12]
        dqkv, sums, q_s, k_s, kt_s, v_s, do_s, dq_s, dk_s, dv_s = refs[12:]
    rows = branch_a.shape[0]
    wide = o.shape[1]
    heads = wide // HD
    k_more = key_extra(rows, row_count, quarter, 3)
    three = ones_extra(rows, 3)
    lane = lane_at(rows)

    def spread_lanes(first, parts):
        value = jnp.where(lane < first, 1.0, 0.0).astype(f32)
        for at, part in enumerate(parts):
            value = jnp.where(lane == first + at, part.astype(f32), value)
        return value.astype(bf16)

    for half, branch in enumerate((branch_a, branch_b)):
        at = pl.ds(half * rows, rows)
        grad_all = nn_dot(branch[...], w_vo[:, wide:]).astype(bf16)
        for h in range(heads):
            low, high = h * HD, (h + 1) * HD
            minus_lse = split_low(-lse[at, h : h + 1])
            q_s[h, at, :] = widen(qkv[at, low:high], spread_lanes(1, minus_lse))
            keys = widen(qkv[at, wide + low : wide + high], k_more)
            k_s[h, at, :] = keys
            kt_s[h, :, at] = jnp.transpose(keys.astype(f32)).astype(bf16)
            v_s[h, at, :] = widen(qkv[at, 2 * wide + low : 2 * wide + high], three)
            grad = grad_all[:, low:high]
            inner = jnp.sum(grad.astype(f32) * o[at, low:high].astype(f32), axis=1, keepdims=True)
            do_s[h, at, :] = widen(grad, spread_lanes(0, split_low(-inner)))

    def work(h, carry):
        for part in range(2 * rows // step):
            at = pl.ds(part * step, step)
            queries = q_s[h, at, :]
            grad_out = do_s[h, at, :]
            probs = jnp.exp2(nt_dot(k_s[h], queries))
            grad_scores = (probs * nt_dot(v_s[h], grad_out)).astype(bf16)
            grad_values = nn_dot(probs.astype(bf16), grad_out)
            grad_keys = nn_dot(grad_scores, queries)
            if part == 0:
                dv_s[h] = grad_values
                dk_s[h] = grad_keys
            else:
                dv_s[h] += grad_values
                dk_s[h] += grad_keys
            dq_s[h, at, :] = jnp.transpose(nn_dot(kt_s[h], grad_scores))
        return carry

    lax.fori_loop(0, heads, work, 0)
    for h in range(heads):
        low, high = h * HD, (h + 1) * HD
        dqkv[:, low:high] = (dq_s[h][:, :HD] * HD**-0.5).astype(bf16)
        dqkv[:, wide + low : wide + high] = (dk_s[h][:, :HD] * LN2).astype(bf16)
        dqkv[:, 2 * wide + low : 2 * wide + high] = dv_s[h][:, :HD].astype(bf16)
    sums[...] = jnp.zeros_like(sums)
    sums[0:1, :] = jnp.sum(dqkv[...].astype(f32), axis=0, keepdims=True)
    if not first:
        for half, dest in enumerate((dn_a, dn_b)):
            at = pl.ds(half * rows, rows)
            part = nt_dot(dqkv[at, : 2 * wide], w_qk[...])
            part = part + nt_dot(dqkv[at, 2 * wide :], w_vo[:, :wide])
            part = part + nt_dot(dqkv_before[at, : 2 * wide], w_qk_before[...])
            part = part + nt_dot(dqkv_before[at, 2 * wide :], w_vo_before[:, :wide])
            dest[...] = part.astype(dest.dtype)


def attend_back(row_count, quarter, branch_a, branch_b, w_qk, w_vo, qkv, o, lse, before):
    rows, width = branch_a.shape
    wide = o.shape[1]
    heads = wide // HD
    operands = (branch_a, branch_b, w_qk, w_vo, qkv, o, lse, *before)
    outs = [
        jax.ShapeDtypeStruct((2 * rows, 3 * wide), bf16),
        jax.ShapeDtypeStruct((8, 3 * wide), f32),
    ]
    if before:
        outs = [jax.ShapeDtypeStruct((rows, width), kind) for kind in (f32, bf16)] + outs
    return pl.pallas_call(
        functools.partial(attend_back_kernel, row_count, quarter, min(512, 2 * rows), not before),
        grid=(1,),
        in_specs=[single(part.shape) for part in operands],
        out_specs=[whole(part.shape) for part in outs],
        out_shape=outs,
        scratch_shapes=[
            pltpu.VMEM((heads, 2 * rows, WIDE), bf16),
            pltpu.VMEM((heads, 2 * rows, WIDE), bf16),
            pltpu.VMEM((heads, WIDE, 2 * rows), bf16),
            pltpu.VMEM((heads, 2 * rows, WIDE), bf16),
            pltpu.VMEM((heads, 2 * rows, WIDE), bf16),
            pltpu.VMEM((heads, 2 * rows, WIDE), f32),
            pltpu.VMEM((heads, 2 * rows, WIDE), f32),
            pltpu.VMEM((heads, 2 * rows, WIDE), f32),
        ],
        compiler_params=pltpu.CompilerParams(vmem_limit_bytes=62 * 2**20),
    )(*operands)


def normalized(value):
    centred = value - jnp.mean(value, axis=-1, keepdims=True)
    scale = lax.rsqrt(jnp.mean(centred * centred, axis=-1, keepdims=True) + eps)
    return centred * scale, scale


def norm_back(value, gain, grad):
    unit, scale = normalized(value)
    scaled = grad * gain
    result = scale * (
        scaled
        - jnp.mean(scaled, axis=-1, keepdims=True)
        - unit * jnp.mean(scaled * unit, axis=-1, keepdims=True)
    )
    sums = [jnp.sum(part, axis=0, keepdims=True) for part in (grad * unit, grad)]
    return result, *sums


def gelu_both(value):
    share = 0.5 * (1.0 + lax.erf(value * math.sqrt(0.5)))
    density = jnp.exp(-0.5 * value * value) * (1.0 / math.sqrt(2.0 * math.pi))
    return (value * share).astype(bf16), (share + value * density).astype(bf16)


def feed_kernel(at, layers, *refs):
    final = at == layers - 1
    gain, shift, obias = 2 * at, 2 * layers + 2 * at, 4 * layers + 2 * at
    current, share_a, share_b, vectors, bias = refs[:5]
    ups, downs, activated, slopes = [refs[5 + 4 * i : 9 + 4 * i] for i in range(4)]
    middle, normed, total = refs[21:24]
    j = pl.program_id(0)

    @pl.when(j == 0)
    def _():
        value = current[...] + (share_a[...] + share_b[...].astype(f32) + vectors[obias : obias + 1, :])
        middle[...] = value
        unit, _ = normalized(value)
        unit = unit * vectors[gain + 1 : gain + 2, :] + vectors[shift + 1 : shift + 2, :]
        normed[...] = unit.astype(bf16)
        total[...] = value + vectors[obias + 1 : obias + 2, :]

    rows_in = normed[...]
    for t in range(4):
        upward = nn_dot(rows_in, ups[t][...]) + bias[t * layers + at : t * layers + at + 1, :]
        activated[t][...], slopes[t][...] = gelu_both(upward)
    joined = jnp.concatenate([ref[...] for ref in activated], axis=1)
    down = jnp.concatenate([ref[...] for ref in downs], axis=1)
    total[...] += nt_dot(joined, down)
    if not final:
        following = refs[24]

        @pl.when(j == pl.num_programs(0) - 1)
        def _():
            unit, _ = normalized(total[...])
            unit = unit * vectors[gain + 2 : gain + 3, :] + vectors[shift + 2 : shift + 3, :]
            following[...] = unit.astype(bf16)


def column_block(rows, step):
    return pl.BlockSpec((rows, step), lambda j: (0, j))


def feed(at, layers, current, share_a, share_b, vectors, bias, ups, downs):
    rows, width = current.shape
    hidden = ups[0].shape[1]
    step = min(256, hidden)
    rest = [f32, bf16, f32] if at == layers - 1 else [f32, bf16, f32, bf16]
    fronts = (current, share_a, share_b, vectors)
    return pl.pallas_call(
        functools.partial(feed_kernel, at, layers),
        grid=(hidden // step,),
        in_specs=[single(part.shape) for part in fronts]
        + [column_block(bias.shape[0], step)]
        + [column_block(width, step)] * 8,
        out_specs=[column_block(rows, step)] * 8 + [whole((rows, width))] * len(rest),
        out_shape=[jax.ShapeDtypeStruct((rows, hidden), bf16)] * 8
        + [jax.ShapeDtypeStruct((rows, width), kind) for kind in rest],
        compiler_params=pltpu.CompilerParams(vmem_limit_bytes=60 * 2**20),
    )(*fronts, bias, *ups, *downs)


def feed_back_kernel(at, layers, *refs):
    final = at == layers - 1
    gain = 2 * at
    count = 1 if final else 4
    fronts, refs = refs[:count], refs[count:]
    middle, normed, vectors = refs[:3]
    ups, downs, activated, slopes = [refs[3 + 4 * i : 7 + 4 * i] for i in range(4)]
    own, other, bias_grad, grad_out, branch, sums = refs[19:25]
    total, grad, grad_low, normed_t, grad_t = refs[25:]
    j = pl.program_id(0)

    @pl.when(j == 0)
    def _():
        sums[...] = jnp.zeros_like(sums)
        if final:
            value = fronts[0][...].astype(f32)
        else:
            above, layer_out, share_a, share_b = fronts
            grad_normed = share_a[...] + share_b[...].astype(f32)
            value, gain_one, shift_one = norm_back(
                layer_out[...], vectors[gain + 2 : gain + 3, :], grad_normed
            )
            value = value + above[...]
            sums[4:5, :], sums[5:6, :] = gain_one, shift_one
        grad[...] = value
        low = value.astype(bf16)
        grad_low[...] = low
        sums[0:1, :] = jnp.sum(low.astype(f32), axis=0, keepdims=True)
        normed_t[...] = jnp.transpose(normed[...].astype(f32)).astype(bf16)
        grad_t[...] = jnp.transpose(low.astype(f32)).astype(bf16)
        total[...] = jnp.zeros_like(total)

    grad_rows = grad_low[...]
    grad_ups = []
    for t in range(4):
        grad_act = nn_dot(grad_rows, downs[t][...])
        scaled = grad_act * slopes[t][...].astype(f32)
        grad_ups.append(scaled.astype(bf16))
        bias_grad[t : t + 1, :] = jnp.sum(scaled, axis=0, keepdims=True)
        dest = (own, other)[t % 2]
        dest[t // 2] = nn_dot(normed_t[...], grad_ups[t]).astype(bf16)
        dest[2 + t // 2] = nn_dot(grad_t[...], activated[t][...]).astype(bf16)
    joined = jnp.concatenate(grad_ups, axis=1)
    up = jnp.concatenate([ref[...] for ref in ups], axis=1)
    total[...] += nt_dot(joined, up)

    @pl.when(j == pl.num_programs(0) - 1)
    def _():
        value, gain_two, shift_two = norm_back(
            middle[...], vectors[gain + 1 : gain + 2, :], total[...]
        )
        value = value + grad[...]
        grad_out[...] = value
        low = value.astype(bf16)
        branch[...] = low
        sums[1:2, :], sums[2:3, :] = gain_two, shift_two
        sums[3:4, :] = jnp.sum(low.astype(f32), axis=0, keepdims=True)


def feed_back(at, layers, fronts, middle, normed, vectors, ups, downs, activated, slopes):
    rows, width = normed.shape
    hidden = activated[0].shape[1]
    step = min(256, hidden)
    stack = pl.BlockSpec((4, width, step), lambda j: (0, 0, j))
    singles = (*fronts, middle, normed, vectors)
    return pl.pallas_call(
        functools.partial(feed_back_kernel, at, layers),
        grid=(hidden // step,),
        in_specs=[single(part.shape) for part in singles]
        + [column_block(width, step)] * 8
        + [column_block(rows, step)] * 8,
        out_specs=[stack] * 2
        + [column_block(4, step)]
        + [whole((rows, width))] * 2
        + [whole((8, width))],
        out_shape=[jax.ShapeDtypeStruct((4, width, hidden), bf16)] * 2
        + [
            jax.ShapeDtypeStruct((4, hidden), f32),
            jax.ShapeDtypeStruct((rows, width), f32),
            jax.ShapeDtypeStruct((rows, width), bf16),
            jax.ShapeDtypeStruct((8, width), f32),
        ],
        scratch_shapes=[pltpu.VMEM((rows, width), f32)] * 2
        + [pltpu.VMEM((rows, width), bf16)]
        + [pltpu.VMEM((width, rows), bf16)] * 2,
        compiler_params=pltpu.CompilerParams(vmem_limit_bytes=62 * 2**20),
    )(*singles, *ups, *downs, *activated, *slopes)


def local(
    frames,
    cotangent,
    qkv_weight,
    out_weight,
    up_weight,
    down_weight,
    qv_bias,
    up_bias,
    norm_gains,
    norm_shifts,
    out_biases,
):
    layers, block = qkv_weight.shape[:2]
    wide = qkv_weight.shape[3]
    row_count, width = frames.shape[1:]
    hidden = up_weight.shape[2]
    quarter = -(-row_count // 128) * 128
    rows = 2 * quarter
    count_dp = lax.axis_size("dp")
    me = lax.axis_index("dp")
    t_me = lax.axis_index("tensor")
    y_me = t_me // 2
    block_at = relative_mask(jnp.arange(count_dp)) ^ me

    norm_part, up_part, qv_part = norm_gains.shape[2], up_bias.shape[1], qv_bias.shape[2]

    def place(part, size, at):
        room = jnp.zeros((part.shape[0], size), f32)
        return lax.dynamic_update_slice(room, part, (0, at))

    by_width = jnp.stack([norm_gains, norm_shifts, out_biases]).reshape(6 * layers, norm_part)
    by_width = place(by_width, 4 * norm_part, t_me * norm_part)
    by_hidden = jnp.concatenate(
        [
            place(up_bias, width, me * up_part),
            place(qv_bias.reshape(2 * layers, qv_part), width, me * qv_part),
        ]
    )

    source = jnp.repeat(block_at, block) * block + jnp.tile(jnp.arange(block), count_dp)
    to_relative = (jnp.arange(width)[:, None] == source[None, :]).astype(bf16)

    first = y_me == 0

    def other_clip(value):
        return jnp.where(first, value[1], value[0])

    def take_clip(value, theirs):
        mine = jnp.where(first, value[0], value[1])
        padding = ((0, 0), (0, quarter - row_count), (0, 0))
        both = jnp.pad(jnp.stack([mine, theirs]), padding).reshape(rows, width)
        return nn_dot(both, to_relative)

    def give_half(value):
        return exchange(value[quarter:].astype(bf16), "tensor", 2)

    def give_clip(value, theirs):
        mine = value[:quarter]
        theirs = nt_dot(theirs, to_relative)[:row_count]
        high = mine.astype(bf16)
        low = (mine - high.astype(f32)).astype(bf16)
        mine = (nt_dot(high, to_relative) + nt_dot(low, to_relative))[:row_count]
        return jnp.stack([jnp.where(first, mine, theirs), jnp.where(first, theirs, mine)])

    current = take_clip(frames, exchange(other_clip(frames), "tensor", 2))
    clip = other_clip(cotangent)

    groups = []
    for at in range(layers):
        qk = jnp.concatenate([qkv_weight[at, :, 0], qkv_weight[at, :, 1]], axis=1)
        vo = jnp.concatenate([qkv_weight[at, :, 2], out_weight[at].T], axis=1)
        groups += [(qk, vo), (up_weight[at], down_weight[at].T)]
    gathering = Gathering(groups)
    for mask in dp_masks():
        got = exchange(by_width, "dp", mask), exchange(by_hidden, "dp", mask)
        if mask == 2:
            got = gathering.advance(*got)
        else:
            got = together(*got)
        by_width = jnp.concatenate([by_width, got[0]], axis=1)
        by_hidden = by_hidden + got[1]
    cut = 6 * layers
    own = jnp.concatenate([by_width, by_hidden])
    got, clip = gathering.advance(exchange(own[: cut + layers], "tensor", 1), clip)
    own = jnp.concatenate([own[:cut] + got[:cut], own[cut : cut + layers], got[cut:], own[cut + layers :]])
    (got,) = gathering.advance(exchange(own, "tensor", 2))
    vectors = own[:cut] + got[:cut]
    end = cut + 2 * layers
    biases = jnp.concatenate([own[cut:end], got[cut:end], own[end:], got[end:]])
    gain_all, shift_all = vectors[: 2 * layers], vectors[2 * layers : 4 * layers]

    def feed_weights(group):
        parts = gathering.until(group)
        return [
            [parts[2 * i], exchange(parts[2 * i], "tensor", 1), parts[2 * i + 1], exchange(parts[2 * i + 1], "tensor", 1)]
            for i in range(2)
        ]

    weights = []
    saved = []
    unit, _ = normalized(current)
    normed_a = (unit * gain_all[0] + shift_all[0]).astype(bf16)
    (normed_b,) = gathering.advance(exchange(normed_a, "tensor", 1))
    for at in range(layers):
        final = at == layers - 1
        w_qk, w_qk_other, w_vo, w_vo_other = gathering.until(2 * at)
        w_attn = ((w_qk, w_vo), (w_qk_other, w_vo_other))
        heads = []
        for t in range(2):
            before = (heads[0][1], w_attn[0][1]) if t else ()
            ready = behind((normed_a, normed_b), *gathering.tokens, *before[:1])
            row = 4 * layers + 2 * (t * layers + at)
            out = attend(row_count, quarter, row, *ready, *w_attn[t], biases, before)
            *shares, qkv, o, lse = gathering.advance(*out)
            heads.append((qkv, o, lse))
        share_b = exchange(shares[1], "tensor", 1)
        if not final:
            (share_b,) = gathering.advance(share_b)
        w_up, w_down = feed_weights(2 * at + 1)
        fed = feed(at, layers, current, shares[0], share_b, vectors, biases, w_up, w_down)
        if not final:
            fed = gathering.advance(*fed, *([exchange(clip, "tensor", 2)] if at == 0 else []))
            if at == 0:
                *fed, clip = fed
        weights.append((w_attn, w_up, w_down))
        normed = jnp.concatenate([normed_a, normed_b], axis=0)
        saved.append((current, normed, heads, fed[:4], fed[4:8], fed[8], fed[9]))
        current = fed[10]
        if not final:
            normed_a = fed[11]
            (normed_b,) = gathering.advance(exchange(normed_a, "tensor", 1))
    if layers == 1:
        clip = exchange(clip, "tensor", 2)
    small_grads = [None] * layers
    weight_grads = [None] * layers
    folding = None
    fronts = (take_clip(cotangent, clip),)
    for at in reversed(range(layers)):
        final = at == layers - 1
        w_attn, w_up, w_down = weights[at]
        layer_in, normed, heads, activated, slopes, middle, normed_two = saved[at]
        uppers = [] if folding is None else [folding]
        if uppers:
            fronts = behind(fronts, *folding.tokens())
        fed = feed_back(
            at, layers, fronts, middle, normed_two, vectors, w_up, w_down, activated, slopes
        )
        if final:
            *fed, encoded_half = together(*fed, give_half(current))
        own, other, bup, gradient, branch_a, sums = advance(uppers, *fed)
        branch_b = exchange(branch_a, "tensor", 1)
        core = Folding(own, other)

        def weight_grad(t, dqkv):
            dw = tn_dot(normed, dqkv).astype(bf16)
            o = heads[t][1]
            dw_o = (tn_dot(branch_a, o[:rows]) + tn_dot(branch_b, o[rows:])).astype(bf16)
            return dw[:, : 2 * wide], jnp.concatenate([dw[:, 2 * wide :], dw_o], axis=1)

        def state_tokens():
            return [part for fold in (core, *uppers) for part in fold.tokens()]

        if at == 0:
            advance([core, *uppers])
        elif uppers:
            advance(uppers)
        ready = behind((branch_a, branch_b), *state_tokens())
        dqkv_other, sums_other = advance(
            [core, *uppers],
            *attend_back(row_count, quarter, *ready, *w_attn[1], *heads[1], ()),
        )
        if at == 0:
            sent = jnp.concatenate(weight_grad(1, dqkv_other), axis=1)
            got = (exchange(sent, "tensor", 2),)
        else:
            sent, got = dqkv_other, ()
        ready = behind((branch_a, branch_b), sent, *state_tokens())
        *got, share_a, share_b, dqkv_own, sums_own = advance(
            [core, *uppers],
            *got,
            *attend_back(
                row_count, quarter, *ready, *w_attn[0], *heads[0], (dqkv_other, *w_attn[1])
            ),
        )
        if uppers:
            weight_grads[at + 1] = folding.result()
        share_b = exchange(share_b, "tensor", 1)
        dw_own = weight_grad(0, dqkv_own)
        if at == 0:
            dw_own = add_low(jnp.concatenate(dw_own, axis=1), got[0])
            folding = LastFolding(dw_own, *core.feed)
        else:
            dw_other = weight_grad(1, dqkv_other)
            core.attn = together(*[jnp.stack(pair) for pair in zip(dw_own, dw_other)])
            folding = core
        fronts = (gradient, layer_in, share_a, share_b)
        small_grads[at] = (sums, (sums_own, sums_other), bup)
    grad_in, *last_sums = norm_back(
        layer_in, gain_all[0], share_a + share_b.astype(f32)
    )
    gradient = gradient + grad_in
    lane = jnp.arange(width)
    head_source = block_at[lane // block] * qv_part + lane % block
    to_blocks = (jnp.arange(wide)[:, None] == head_source[None, :]) & (lane % block < qv_part)
    up_source = block_at[lane // block] * up_part + lane % block
    up_blocks = (jnp.arange(hidden)[:, None] == up_source[None, :]) & (lane % block < up_part)

    def reorder(part, matrix):
        return lax.dot_general(
            part,
            matrix.astype(f32),
            (((1,), (0,)), ((), ())),
            precision=lax.Precision.HIGHEST,
            preferred_element_type=f32,
        )

    bups = reorder(
        jnp.concatenate([small_grads[at][2][t : t + 1] for t in range(4) for at in range(layers)]),
        up_blocks,
    )
    bqv = reorder(
        jnp.concatenate(
            [
                small_grads[at][1][t][:1, i * wide : (i + 1) * wide]
                for t in range(2)
                for at in range(layers)
                for i in (0, 2)
            ]
        ),
        to_blocks,
    )
    last_sums = jnp.concatenate([*last_sums, jnp.zeros((6, width), f32)])
    by_width = jnp.concatenate([small_grads[at][0] for at in range(layers)] + [last_sums])
    small = [
        jnp.concatenate(
            [by_width, bups[t * layers : (t + 1) * layers]]
            + ([bqv[t * layers : (t + 2) * layers]] if t % 2 == 0 else [])
        )
        for t in range(4)
    ]
    advance([folding])
    gradient, *small, folding.attn, folding.feed = together(
        gradient, *small, folding.attn, folding.feed
    )
    half, *got = advance(
        [folding],
        give_half(gradient),
        *[exchange(small[t], "tensor", t) for t in range(1, 4)],
    )
    cut = 8 * layers + 8
    small, more = small[0] + got[1], got[0] + got[2]
    small = jnp.concatenate([small[: cut + layers] + more, small[cut + layers :]])
    frames_grad = give_clip(gradient, half)
    for mask in reversed(dp_masks()):
        got = exchange(small[:, small.shape[1] // 2 :], "dp", mask)
        if folding.step < 3:
            (got,) = advance([folding], got)
        small = small[:, : small.shape[1] // 2] + got
        if folding.step == 3 and mask == 1:
            small, current, encoded_half = together(small, current, encoded_half)
    encoded = give_clip(current, encoded_half)
    weight_grads[0] = folding.result()
    by_width = lax.dynamic_slice(small, (0, t_me * norm_part), (cut, norm_part))
    rows_of = [by_width[8 * at : 8 * at + 8] for at in range(layers + 1)]
    one = [rows_of[at][4:6] for at in range(layers - 1)]
    one = [rows_of[layers][0:2]] + one

    def pair(make):
        return jnp.stack([jnp.stack(make(at)) for at in range(layers)])

    gains = pair(lambda at: [one[at][0], rows_of[at][1]])
    shifts = pair(lambda at: [one[at][1], rows_of[at][2]])
    obiases = pair(lambda at: [rows_of[at][3], rows_of[at][0]])
    bups = small[cut : cut + layers, :up_part]
    bqv = small[cut + layers :, :qv_part].reshape(layers, 2, qv_part)

    def stacked(make):
        return jnp.stack([make(*weight_grads[at]) for at in range(layers)])

    return (
        encoded,
        frames_grad,
        stacked(lambda qk, vo, up, down: jnp.stack([qk[:, :wide], qk[:, wide:], vo[:, :wide]], axis=1)),
        stacked(lambda qk, vo, up, down: vo[:, wide:].T),
        stacked(lambda qk, vo, up, down: up),
        stacked(lambda qk, vo, up, down: down.T),
        bqv,
        bups,
        gains,
        shifts,
        obiases,
    )


def solution(mesh):
    in_specs = (
        P("dp", "tensor", None),
        P("dp", "tensor", None),
        P(None, "dp", None, "tensor"),
        P(None, "tensor", "dp"),
        P(None, "dp", "tensor"),
        P(None, "tensor", "dp"),
        P(None, None, ("tensor", "dp")),
        P(None, ("tensor", "dp")),
        P(None, None, ("dp", "tensor")),
        P(None, None, ("dp", "tensor")),
        P(None, None, ("dp", "tensor")),
    )
    out_specs = (
        P("dp", "tensor", None),
        P("dp", "tensor", None),
        P(None, "dp", None, "tensor"),
        P(None, "tensor", "dp"),
        P(None, "dp", "tensor"),
        P(None, "tensor", "dp"),
        P(None, None, ("tensor", "dp")),
        P(None, ("tensor", "dp")),
        P(None, None, ("dp", "tensor")),
        P(None, None, ("dp", "tensor")),
        P(None, None, ("dp", "tensor")),
    )
    return jax.shard_map(local, mesh=mesh, in_specs=in_specs, out_specs=out_specs, check_vma=False)
```

```python
import functools
import math

import jax
import jax.numpy as jnp
from jax import lax
from jax.experimental import pallas as pl
from jax.experimental.pallas import tpu as pltpu
from jax.sharding import PartitionSpec as P

HD = 64
WIDE = 128
eps = 1e-05
LOG2E = 1.0 / math.log(2.0)
LN2 = math.log(2.0)
MASKED = -1e30
bf16 = jnp.bfloat16
f32 = jnp.float32


def exchange(value, axis, mask):
    count = lax.axis_size(axis)
    return lax.ppermute(value, axis, [(i, i ^ mask) for i in range(count)])


def dp_masks():
    count = lax.axis_size("dp")
    masks = []
    while count > 1:
        count //= 2
        masks.append(count)
    return masks


def relative_mask(position):
    result = 0
    for at, mask in enumerate(dp_masks()):
        result = result + ((position >> at) & 1) * mask
    return result


def together(*values):
    return lax.optimization_barrier(values)


def gather_steps(first, second):
    masks = dp_masks()
    cut = first.shape[1]

    def z_step(mask):
        return (
            lambda state: (exchange(state[0], "dp", mask),),
            lambda state, got: (jnp.concatenate([state[0], got[0]], axis=0),),
        )

    near = (
        lambda state: (exchange(state[0], "dp", masks[-1]), exchange(state[1], "tensor", 2)),
        lambda state, got: (
            jnp.concatenate([state[0], got[0]], axis=0),
            state[1],
            got[1],
        ),
    )
    last = (
        lambda state: (
            exchange(state[0], "tensor", 2),
            exchange(state[1], "dp", masks[-1]),
            exchange(state[2], "dp", masks[-1]),
        ),
        lambda state, got: (
            state[0],
            got[0],
            *[jnp.concatenate([state[1 + i], got[1 + i]], axis=0) for i in range(2)],
        ),
    )

    def split(finish):
        def cut_last(state, got):
            block = finish(state, got)[0]
            return block[:, :cut], block[:, cut:]

        return cut_last

    ahead = [z_step(mask) for mask in masks[:-1]]
    ahead[-1] = (ahead[-1][0], split(ahead[-1][1]))
    return (jnp.concatenate([first, second], axis=1),), ahead, [near, last]


class Gathering:
    def __init__(self, groups):
        made = [gather_steps(*group) for group in groups]
        self.states = [start for start, _, _ in made]
        self.plan = [[(0, step)] for step in made[0][1]]
        for at, (_, _, near) in enumerate(made):
            ahead = made[at + 1][1] if at + 1 < len(made) else []
            for i in range(max(len(near), len(ahead))):
                stage = [(at, near[i])] if i < len(near) else []
                self.plan.append(stage + ([(at + 1, ahead[i])] if i < len(ahead) else []))
        self.ends = [
            max(i for i, stage in enumerate(self.plan) for g, _ in stage if g == at)
            for at in range(len(made))
        ]
        self.done = 0
        self.tokens = ()

    def advance(self, *others):
        stage = self.plan[self.done]
        self.done += 1
        flat = [part for g, _ in stage for part in self.states[g]]
        flat = behind(flat, *self.tokens)
        states, received, at = [], [], 0
        for g, (send, _) in stage:
            states.append(flat[at : at + len(self.states[g])])
            at += len(self.states[g])
            received.append(send(states[-1]))
        flat = together(*[part for got in received for part in got], *others)
        at = 0
        for (g, (_, finish)), state, got in zip(stage, states, received):
            self.states[g] = finish(state, flat[at : at + len(got)])
            at += len(got)
        self.tokens = [part for g, _ in stage for part in self.states[g][:1]]
        return flat[at:]

    def until(self, group):
        while self.done <= self.ends[group]:
            self.advance()
        return self.states[group]


def behind(values, *tokens):
    return together(*values, *tokens)[: len(values)]


def add_low(kept, received):
    return (kept.astype(f32) + received.astype(f32)).astype(bf16)


def near_one_sent(first, second):
    return first[1], second[:, second.shape[1] // 2 :]


def near_one(sent):
    return exchange(sent[0], "tensor", 2), exchange(sent[1], "dp", dp_masks()[-1])


def near_one_sum(first, second, got):
    return add_low(first[0], got[0]), add_low(second[:, : second.shape[1] // 2], got[1])


def near_two(first, second):
    half = first.shape[0] // 2
    return exchange(first[half:], "dp", dp_masks()[-1]), exchange(second[1], "tensor", 2)


def near_two_sum(first, second, got):
    return add_low(first[: first.shape[0] // 2], got[0]), add_low(second[0], got[1])


def far(value, masks):
    for mask in masks[:-1]:
        value = far_sum(value, exchange(value[value.shape[0] // 2 :], "dp", mask))
    return value, exchange(value[value.shape[0] // 2 :], "dp", masks[-1])


def far_sum(value, got):
    return add_low(value[: value.shape[0] // 2], got)


class Folding:
    def __init__(self, own, other):
        masks = dp_masks()[-2::-1]
        self.masks = masks[:-1], masks[-1:]
        self.own, self.other = own, other
        self.half = own.shape[1] // 2
        self.attn = None
        self.step = 0

    def send(self):
        step = self.step
        if step == 0:
            return (exchange(self.other, "tensor", 1),)
        if step == 1:
            return near_one(self.feed)
        if step == 2:
            got = near_two(*self.feed)
            return got if self.attn is None else got + near_one(near_one_sent(*self.attn))
        if step == 3:
            self.feed, more = far(self.feed, self.masks[0])
            return *near_two(*self.attn), more
        self.attn, *got = far(self.attn, self.masks[step - 4])
        if step == 4:
            self.feed, more = far(self.feed, self.masks[1])
            got.append(more)
        return got

    def finish(self, got):
        step, half = self.step, self.half
        self.step += 1
        if step == 0:
            own, other = self.own, got[0]
            self.kept = (own[0], other[0], own[2:, :half], other[2:, :half])
            self.feed = together(
                add_low(own[1], other[1]), add_low(own[2:, half:], other[2:, half:])
            )
        elif step == 1:
            first = self.kept[0].astype(f32) + self.kept[1].astype(f32) + got[0].astype(f32)
            second = self.kept[2].astype(f32) + self.kept[3].astype(f32) + got[1].astype(f32)
            self.feed = together(first.astype(bf16), second.astype(bf16))
        elif step == 2:
            self.feed = together(*near_two_sum(*self.feed, got[:2]))
            if self.attn is not None:
                self.feed = jnp.concatenate(self.feed, axis=1)
                self.attn = near_one_sum(*self.attn, got[2:])
                self.feed, *self.attn = together(self.feed, *self.attn)
        elif step == 3:
            self.attn = jnp.concatenate(near_two_sum(*self.attn, got[:2]), axis=1)
            self.feed = far_sum(self.feed, got[2])
            self.attn, self.feed = together(self.attn, self.feed)
        else:
            self.attn = far_sum(self.attn, got[0])
            if step == 4:
                self.feed = far_sum(self.feed, got[1])
            self.attn, self.feed = together(self.attn, self.feed)

    def tokens(self):
        if self.step == 0:
            return []
        parts = self.feed if self.step < 3 and isinstance(self.feed, (list, tuple)) else (self.feed,)
        if self.attn is None:
            return list(parts)
        return [*parts, *(self.attn if isinstance(self.attn, (list, tuple)) else (self.attn,))]

    def result(self):
        half, low = self.attn.shape[1] // 2, self.feed.shape[1] // 2
        parts = self.attn[:, :half], self.attn[:, half:], self.feed[:, :low], self.feed[:, low:]
        return [part.astype(f32) for part in parts]


class LastFolding:
    def __init__(self, attn, up, down):
        self.masks = dp_masks()[-2::-1]
        self.attn = attn
        self.feed = jnp.concatenate([up, down], axis=1)
        self.step = 0

    def send(self):
        first, last = self.masks[:-1], self.masks[-1:]
        self.attn, *got = far(self.attn, (dp_masks()[-1:], first, last)[self.step])
        if self.step < 2:
            self.feed, more = far(self.feed, (first, last)[self.step])
            got.append(more)
        return got

    def finish(self, got):
        self.attn = far_sum(self.attn, got[0])
        if self.step < 2:
            self.feed = far_sum(self.feed, got[1])
        self.attn, self.feed = together(self.attn, self.feed)
        self.step += 1

    result = Folding.result


def advance(folds, *others):
    received = [fold.send() for fold in folds]
    flat = together(*[part for got in received for part in got], *others)
    at = 0
    for fold, got in zip(folds, received):
        fold.finish(flat[at : at + len(got)])
        at += len(got)
    return flat[at:]


def split_low(value):
    high = value.astype(bf16)
    rest = value - high.astype(f32)
    mid = rest.astype(bf16)
    return high, mid, (rest - mid.astype(f32)).astype(bf16)


def lane_at(rows):
    return lax.broadcasted_iota(jnp.int32, (rows, WIDE - HD), 1)


def key_extra(rows, row_count, quarter, ones):
    lane = lane_at(rows)
    row = lax.broadcasted_iota(jnp.int32, (rows, WIDE - HD), 0)
    masked = lax.rem(row, quarter) >= row_count
    bias = jnp.where(masked, MASKED, 0.0).astype(f32)
    value = jnp.where(lane == 0, bias, jnp.where(lane <= ones, 1.0, 0.0))
    return value.astype(bf16)


def ones_extra(rows, ones):
    return jnp.where(lane_at(rows) < ones, 1.0, 0.0).astype(bf16)


def widen(part, extra):
    return jnp.concatenate([part, extra], axis=1)


def nt_dot(left, right):
    return lax.dot_general(left, right, (((1,), (1,)), ((), ())), preferred_element_type=f32)


def nn_dot(left, right):
    return lax.dot_general(left, right, (((1,), (0,)), ((), ())), preferred_element_type=f32)


def tn_dot(left, right):
    return lax.dot_general(left, right, (((0,), (0,)), ((), ())), preferred_element_type=f32)


def whole(shape):
    return pl.BlockSpec(shape, lambda j: (0,) * len(shape))


def single(shape):
    return pl.BlockSpec(shape, lambda j: (0,) * len(shape), pipeline_mode=pl.Buffered(1))


def attend_kernel(row_count, quarter, step, row, first, *refs):
    normed_a, normed_b, w_qk, w_vo, bias = refs[:5]
    if first:
        qkv, o, lse, q_s, k_s, v_s, o_s = refs[5:]
    else:
        o_before, w_before, share_a, share_b, qkv, o, lse, q_s, k_s, v_s, o_s = refs[5:]
    rows = normed_a.shape[0]
    wide = o.shape[1]
    heads = wide // HD
    k_more = key_extra(rows, row_count, quarter, 0)
    one = ones_extra(rows, 1)
    lane = lax.broadcasted_iota(jnp.int32, (1, 2 * wide), 1)
    scale = jnp.where(lane < wide, HD**-0.5 * LOG2E, 1.0)
    for half, normed in enumerate((normed_a, normed_b)):
        at = pl.ds(half * rows, rows)
        qk = nn_dot(normed[...], w_qk[...]) + bias[row : row + 1, : 2 * wide]
        qk = (qk * scale).astype(bf16)
        v = nn_dot(normed[...], w_vo[:, :wide]) + bias[row + 1 : row + 2, :wide]
        v = v.astype(bf16)
        qkv[at, : 2 * wide] = qk
        qkv[at, 2 * wide :] = v
        for h in range(heads):
            low, high = h * HD, (h + 1) * HD
            q_s[h, at, :] = widen(qk[:, low:high], one)
            k_s[h, at, :] = widen(qk[:, wide + low : wide + high], k_more)
            v_s[h, at, :] = widen(v[:, low:high], one)

    def work(h, carry):
        is_total = lax.broadcasted_iota(jnp.int32, (step, WIDE), 1) == HD
        for part in range(2 * rows // step):
            at = pl.ds(part * step, step)
            scores = nt_dot(q_s[h, at, :], k_s[h])
            top = jnp.max(scores, axis=-1, keepdims=True)
            summed = nn_dot(jnp.exp2(scores - top).astype(bf16), v_s[h])
            total = summed[:, HD : HD + 1]
            o_s[h, at, :] = jnp.where(is_total, top + jnp.log2(total), summed / total)
        return carry

    lax.fori_loop(0, heads, work, 0)
    for h in range(heads):
        o[:, h * HD : (h + 1) * HD] = o_s[h][:, :HD].astype(bf16)
        lse[:, h : h + 1] = o_s[h][:, HD : HD + 1]
    if not first:
        for half, share in enumerate((share_a, share_b)):
            at = pl.ds(half * rows, rows)
            value = nt_dot(o_before[at, :], w_before[:, wide:]) + nt_dot(o[at, :], w_vo[:, wide:])
            share[...] = value.astype(share.dtype)


def attend(row_count, quarter, row, normed_a, normed_b, w_qk, w_vo, bias, before):
    rows, width = normed_a.shape
    wide = w_qk.shape[1] // 2
    heads = wide // HD
    operands = (normed_a, normed_b, w_qk, w_vo, bias, *before)
    outs = [
        jax.ShapeDtypeStruct((2 * rows, 3 * wide), bf16),
        jax.ShapeDtypeStruct((2 * rows, wide), bf16),
        jax.ShapeDtypeStruct((2 * rows, 8), f32),
    ]
    if before:
        outs = [jax.ShapeDtypeStruct((rows, width), kind) for kind in (f32, bf16)] + outs
    return pl.pallas_call(
        functools.partial(attend_kernel, row_count, quarter, min(512, 2 * rows), row, not before),
        grid=(1,),
        in_specs=[single(part.shape) for part in operands],
        out_specs=[whole(part.shape) for part in outs],
        out_shape=outs,
        scratch_shapes=[pltpu.VMEM((heads, 2 * rows, WIDE), bf16)] * 3
        + [pltpu.VMEM((heads, 2 * rows, WIDE), f32)],
        compiler_params=pltpu.CompilerParams(vmem_limit_bytes=60 * 2**20),
    )(*operands)


def attend_back_kernel(row_count, quarter, step, first, *refs):
    branch_a, branch_b, w_qk, w_vo, qkv, o, lse = refs[:7]
    if first:
        dqkv, sums, q_s, k_s, kt_s, v_s, do_s, dq_s, dk_s, dv_s = refs[7:]
    else:
        dqkv_before, w_qk_before, w_vo_before, dn_a, dn_b = refs[7:12]
        dqkv, sums, q_s, k_s, kt_s, v_s, do_s, dq_s, dk_s, dv_s = refs[12:]
    rows = branch_a.shape[0]
    wide = o.shape[1]
    heads = wide // HD
    k_more = key_extra(rows, row_count, quarter, 3)
    three = ones_extra(rows, 3)
    lane = lane_at(rows)

    def spread_lanes(first, parts):
        value = jnp.where(lane < first, 1.0, 0.0).astype(f32)
        for at, part in enumerate(parts):
            value = jnp.where(lane == first + at, part.astype(f32), value)
        return value.astype(bf16)

    for half, branch in enumerate((branch_a, branch_b)):
        at = pl.ds(half * rows, rows)
        grad_all = nn_dot(branch[...], w_vo[:, wide:]).astype(bf16)
        for h in range(heads):
            low, high = h * HD, (h + 1) * HD
            minus_lse = split_low(-lse[at, h : h + 1])
            q_s[h, at, :] = widen(qkv[at, low:high], spread_lanes(1, minus_lse))
            keys = widen(qkv[at, wide + low : wide + high], k_more)
            k_s[h, at, :] = keys
            kt_s[h, :, at] = jnp.transpose(keys.astype(f32)).astype(bf16)
            v_s[h, at, :] = widen(qkv[at, 2 * wide + low : 2 * wide + high], three)
            grad = grad_all[:, low:high]
            inner = jnp.sum(grad.astype(f32) * o[at, low:high].astype(f32), axis=1, keepdims=True)
            do_s[h, at, :] = widen(grad, spread_lanes(0, split_low(-inner)))

    def work(h, carry):
        for part in range(2 * rows // step):
            at = pl.ds(part * step, step)
            queries = q_s[h, at, :]
            grad_out = do_s[h, at, :]
            probs = jnp.exp2(nt_dot(k_s[h], queries))
            grad_scores = (probs * nt_dot(v_s[h], grad_out)).astype(bf16)
            grad_values = nn_dot(probs.astype(bf16), grad_out)
            grad_keys = nn_dot(grad_scores, queries)
            if part == 0:
                dv_s[h] = grad_values
                dk_s[h] = grad_keys
            else:
                dv_s[h] += grad_values
                dk_s[h] += grad_keys
            dq_s[h, at, :] = jnp.transpose(nn_dot(kt_s[h], grad_scores))
        return carry

    lax.fori_loop(0, heads, work, 0)
    for h in range(heads):
        low, high = h * HD, (h + 1) * HD
        dqkv[:, low:high] = (dq_s[h][:, :HD] * HD**-0.5).astype(bf16)
        dqkv[:, wide + low : wide + high] = (dk_s[h][:, :HD] * LN2).astype(bf16)
        dqkv[:, 2 * wide + low : 2 * wide + high] = dv_s[h][:, :HD].astype(bf16)
    sums[...] = jnp.zeros_like(sums)
    sums[0:1, :] = jnp.sum(dqkv[...].astype(f32), axis=0, keepdims=True)
    if not first:
        for half, dest in enumerate((dn_a, dn_b)):
            at = pl.ds(half * rows, rows)
            part = nt_dot(dqkv[at, : 2 * wide], w_qk[...])
            part = part + nt_dot(dqkv[at, 2 * wide :], w_vo[:, :wide])
            part = part + nt_dot(dqkv_before[at, : 2 * wide], w_qk_before[...])
            part = part + nt_dot(dqkv_before[at, 2 * wide :], w_vo_before[:, :wide])
            dest[...] = part.astype(dest.dtype)


def attend_back(row_count, quarter, branch_a, branch_b, w_qk, w_vo, qkv, o, lse, before):
    rows, width = branch_a.shape
    wide = o.shape[1]
    heads = wide // HD
    operands = (branch_a, branch_b, w_qk, w_vo, qkv, o, lse, *before)
    outs = [
        jax.ShapeDtypeStruct((2 * rows, 3 * wide), bf16),
        jax.ShapeDtypeStruct((8, 3 * wide), f32),
    ]
    if before:
        outs = [jax.ShapeDtypeStruct((rows, width), kind) for kind in (f32, bf16)] + outs
    return pl.pallas_call(
        functools.partial(attend_back_kernel, row_count, quarter, min(512, 2 * rows), not before),
        grid=(1,),
        in_specs=[single(part.shape) for part in operands],
        out_specs=[whole(part.shape) for part in outs],
        out_shape=outs,
        scratch_shapes=[
            pltpu.VMEM((heads, 2 * rows, WIDE), bf16),
            pltpu.VMEM((heads, 2 * rows, WIDE), bf16),
            pltpu.VMEM((heads, WIDE, 2 * rows), bf16),
            pltpu.VMEM((heads, 2 * rows, WIDE), bf16),
            pltpu.VMEM((heads, 2 * rows, WIDE), bf16),
            pltpu.VMEM((heads, 2 * rows, WIDE), f32),
            pltpu.VMEM((heads, 2 * rows, WIDE), f32),
            pltpu.VMEM((heads, 2 * rows, WIDE), f32),
        ],
        compiler_params=pltpu.CompilerParams(vmem_limit_bytes=62 * 2**20),
    )(*operands)


def normalized(value):
    centred = value - jnp.mean(value, axis=-1, keepdims=True)
    scale = lax.rsqrt(jnp.mean(centred * centred, axis=-1, keepdims=True) + eps)
    return centred * scale, scale


def norm_back(value, gain, grad):
    unit, scale = normalized(value)
    scaled = grad * gain
    result = scale * (
        scaled
        - jnp.mean(scaled, axis=-1, keepdims=True)
        - unit * jnp.mean(scaled * unit, axis=-1, keepdims=True)
    )
    sums = [jnp.sum(part, axis=0, keepdims=True) for part in (grad * unit, grad)]
    return result, *sums


def gelu_both(value):
    share = 0.5 * (1.0 + lax.erf(value * math.sqrt(0.5)))
    density = jnp.exp(-0.5 * value * value) * (1.0 / math.sqrt(2.0 * math.pi))
    return (value * share).astype(bf16), (share + value * density).astype(bf16)


def feed_kernel(at, layers, *refs):
    final = at == layers - 1
    gain, shift, obias = 2 * at, 2 * layers + 2 * at, 4 * layers + 2 * at
    current, share_a, share_b, vectors, bias = refs[:5]
    ups, downs, activated, slopes = [refs[5 + 4 * i : 9 + 4 * i] for i in range(4)]
    middle, normed, total = refs[21:24]
    j = pl.program_id(0)

    @pl.when(j == 0)
    def _():
        value = current[...] + (share_a[...] + share_b[...].astype(f32) + vectors[obias : obias + 1, :])
        middle[...] = value
        unit, _ = normalized(value)
        unit = unit * vectors[gain + 1 : gain + 2, :] + vectors[shift + 1 : shift + 2, :]
        normed[...] = unit.astype(bf16)
        total[...] = value + vectors[obias + 1 : obias + 2, :]

    rows_in = normed[...]
    for t in range(4):
        upward = nn_dot(rows_in, ups[t][...]) + bias[t * layers + at : t * layers + at + 1, :]
        activated[t][...], slopes[t][...] = gelu_both(upward)
    joined = jnp.concatenate([ref[...] for ref in activated], axis=1)
    down = jnp.concatenate([ref[...] for ref in downs], axis=1)
    total[...] += nt_dot(joined, down)
    if not final:
        following = refs[24]

        @pl.when(j == pl.num_programs(0) - 1)
        def _():
            unit, _ = normalized(total[...])
            unit = unit * vectors[gain + 2 : gain + 3, :] + vectors[shift + 2 : shift + 3, :]
            following[...] = unit.astype(bf16)


def column_block(rows, step):
    return pl.BlockSpec((rows, step), lambda j: (0, j))


def feed(at, layers, current, share_a, share_b, vectors, bias, ups, downs):
    rows, width = current.shape
    hidden = ups[0].shape[1]
    step = min(256, hidden)
    rest = [f32, bf16, f32] if at == layers - 1 else [f32, bf16, f32, bf16]
    fronts = (current, share_a, share_b, vectors)
    return pl.pallas_call(
        functools.partial(feed_kernel, at, layers),
        grid=(hidden // step,),
        in_specs=[single(part.shape) for part in fronts]
        + [column_block(bias.shape[0], step)]
        + [column_block(width, step)] * 8,
        out_specs=[column_block(rows, step)] * 8 + [whole((rows, width))] * len(rest),
        out_shape=[jax.ShapeDtypeStruct((rows, hidden), bf16)] * 8
        + [jax.ShapeDtypeStruct((rows, width), kind) for kind in rest],
        compiler_params=pltpu.CompilerParams(vmem_limit_bytes=60 * 2**20),
    )(*fronts, bias, *ups, *downs)


def feed_back_kernel(at, layers, *refs):
    final = at == layers - 1
    gain = 2 * at
    count = 1 if final else 4
    fronts, refs = refs[:count], refs[count:]
    middle, normed, vectors = refs[:3]
    ups, downs, activated, slopes = [refs[3 + 4 * i : 7 + 4 * i] for i in range(4)]
    own, other, bias_grad, grad_out, branch, sums = refs[19:25]
    total, grad, grad_low, normed_t, grad_t = refs[25:]
    j = pl.program_id(0)

    @pl.when(j == 0)
    def _():
        sums[...] = jnp.zeros_like(sums)
        if final:
            value = fronts[0][...].astype(f32)
        else:
            above, layer_out, share_a, share_b = fronts
            grad_normed = share_a[...] + share_b[...].astype(f32)
            value, gain_one, shift_one = norm_back(
                layer_out[...], vectors[gain + 2 : gain + 3, :], grad_normed
            )
            value = value + above[...]
            sums[4:5, :], sums[5:6, :] = gain_one, shift_one
        grad[...] = value
        low = value.astype(bf16)
        grad_low[...] = low
        sums[0:1, :] = jnp.sum(low.astype(f32), axis=0, keepdims=True)
        normed_t[...] = jnp.transpose(normed[...].astype(f32)).astype(bf16)
        grad_t[...] = jnp.transpose(low.astype(f32)).astype(bf16)
        total[...] = jnp.zeros_like(total)

    grad_rows = grad_low[...]
    grad_ups = []
    for t in range(4):
        grad_act = nn_dot(grad_rows, downs[t][...])
        scaled = grad_act * slopes[t][...].astype(f32)
        grad_ups.append(scaled.astype(bf16))
        bias_grad[t : t + 1, :] = jnp.sum(scaled, axis=0, keepdims=True)
        dest = (own, other)[t % 2]
        dest[t // 2] = nn_dot(normed_t[...], grad_ups[t]).astype(bf16)
        dest[2 + t // 2] = nn_dot(grad_t[...], activated[t][...]).astype(bf16)
    joined = jnp.concatenate(grad_ups, axis=1)
    up = jnp.concatenate([ref[...] for ref in ups], axis=1)
    total[...] += nt_dot(joined, up)

    @pl.when(j == pl.num_programs(0) - 1)
    def _():
        value, gain_two, shift_two = norm_back(
            middle[...], vectors[gain + 1 : gain + 2, :], total[...]
        )
        value = value + grad[...]
        grad_out[...] = value
        low = value.astype(bf16)
        branch[...] = low
        sums[1:2, :], sums[2:3, :] = gain_two, shift_two
        sums[3:4, :] = jnp.sum(low.astype(f32), axis=0, keepdims=True)


def feed_back(at, layers, fronts, middle, normed, vectors, ups, downs, activated, slopes):
    rows, width = normed.shape
    hidden = activated[0].shape[1]
    step = min(256, hidden)
    stack = pl.BlockSpec((4, width, step), lambda j: (0, 0, j))
    singles = (*fronts, middle, normed, vectors)
    return pl.pallas_call(
        functools.partial(feed_back_kernel, at, layers),
        grid=(hidden // step,),
        in_specs=[single(part.shape) for part in singles]
        + [column_block(width, step)] * 8
        + [column_block(rows, step)] * 8,
        out_specs=[stack] * 2
        + [column_block(4, step)]
        + [whole((rows, width))] * 2
        + [whole((8, width))],
        out_shape=[jax.ShapeDtypeStruct((4, width, hidden), bf16)] * 2
        + [
            jax.ShapeDtypeStruct((4, hidden), f32),
            jax.ShapeDtypeStruct((rows, width), f32),
            jax.ShapeDtypeStruct((rows, width), bf16),
            jax.ShapeDtypeStruct((8, width), f32),
        ],
        scratch_shapes=[pltpu.VMEM((rows, width), f32)] * 2
        + [pltpu.VMEM((rows, width), bf16)]
        + [pltpu.VMEM((width, rows), bf16)] * 2,
        compiler_params=pltpu.CompilerParams(vmem_limit_bytes=62 * 2**20),
    )(*singles, *ups, *downs, *activated, *slopes)


def finish_kernel(layers, wide, *refs):
    layer_in, above, share_a, share_b, gain, up_blocks, head_blocks = refs[:7]
    sums, biases, heads = refs[7 : 7 + layers], refs[7 + layers : 7 + 2 * layers], refs[7 + 2 * layers : 7 + 4 * layers]
    grad, low, *small = refs[7 + 4 * layers :]
    grad_normed = share_a[...] + share_b[...].astype(f32)
    value, gain_one, shift_one = norm_back(layer_in[...], gain[0:1, :], grad_normed)
    value = value + above[...]
    grad[...] = value
    low[...] = value[low.shape[0] :, :].astype(bf16)

    def reorder(part, blocks):
        return sum(nn_dot(piece, blocks[...]) for piece in split_low(part))

    for t in range(4):
        small[t][...] = jnp.zeros_like(small[t])
        small[t][0:1, :] = gain_one
        small[t][2 * layers : 2 * layers + 1, :] = shift_one
    for at in range(layers):
        rows = [(2 * at + 1, 1), (2 * (layers + at) + 1, 2)]
        rows += [(4 * layers + 2 * at, 3), (4 * layers + 2 * at + 1, 0)]
        if at + 1 < layers:
            rows += [(2 * (at + 1), 4), (2 * (layers + at + 1), 5)]
        bias = reorder(biases[at][...], up_blocks)
        for t in range(4):
            for dest, source in rows:
                small[t][dest : dest + 1, :] = sums[at][source : source + 1, :]
            small[t][6 * layers + at : 6 * layers + at + 1, :] = bias[t : t + 1, :]
        for group in range(2):
            both = heads[2 * at + group]
            for i, first in enumerate((0, 2 * wide)):
                dest = 7 * layers + 2 * at + i
                row = reorder(both[:, first : first + wide], head_blocks)
                small[2 * group][dest : dest + 1, :] = row[0:1, :]


def finish(layers, quarter, wide, fronts, sums, biases, heads):
    rows, width = fronts[0].shape
    operands = (*fronts, *sums, *biases, *heads)
    count = -(-9 * layers // 8) * 8
    outs = [jax.ShapeDtypeStruct((rows, width), f32), jax.ShapeDtypeStruct((rows - quarter, width), bf16)]
    outs += [jax.ShapeDtypeStruct((count, width), f32)] * 4
    return pl.pallas_call(
        functools.partial(finish_kernel, layers, wide),
        grid=(1,),
        in_specs=[single(part.shape) for part in operands],
        out_specs=[whole(part.shape) for part in outs],
        out_shape=outs,
        compiler_params=pltpu.CompilerParams(vmem_limit_bytes=56 * 2**20),
    )(*operands)


def local(
    frames,
    cotangent,
    qkv_weight,
    out_weight,
    up_weight,
    down_weight,
    qv_bias,
    up_bias,
    norm_gains,
    norm_shifts,
    out_biases,
):
    layers, block = qkv_weight.shape[:2]
    wide = qkv_weight.shape[3]
    row_count, width = frames.shape[1:]
    hidden = up_weight.shape[2]
    quarter = -(-row_count // 128) * 128
    rows = 2 * quarter
    me = lax.axis_index("dp")
    t_me = lax.axis_index("tensor")
    y_me = t_me // 2

    def blocks_of(size, part):
        lane = jnp.arange(width)
        source = (relative_mask(lane // block) ^ me) * part + lane % block
        return (
            (jnp.arange(size)[:, None] == source[None, :]) & (lane % block < part)[None, :]
        ).astype(bf16)

    norm_part, up_part, qv_part = norm_gains.shape[2], up_bias.shape[1], qv_bias.shape[2]

    def place(part, size, at):
        room = jnp.zeros((part.shape[0], size), f32)
        return lax.dynamic_update_slice(room, part, (0, at))

    groups = []
    for at in range(layers):
        qk = jnp.concatenate([qkv_weight[at, :, 0], qkv_weight[at, :, 1]], axis=1)
        vo = jnp.concatenate([qkv_weight[at, :, 2], out_weight[at].T], axis=1)
        groups += [(qk, vo), (up_weight[at], down_weight[at].T)]
    gathering = Gathering(groups)
    norm_gains, up_bias, frames, cotangent = behind(
        (norm_gains, up_bias, frames, cotangent), *gathering.states[0]
    )
    by_width = jnp.stack([norm_gains, norm_shifts, out_biases]).reshape(6 * layers, norm_part)
    by_width = place(by_width, 4 * norm_part, t_me * norm_part)
    by_hidden = jnp.concatenate(
        [
            place(up_bias, width, me * up_part),
            place(qv_bias.reshape(2 * layers, qv_part), width, me * qv_part),
        ]
    )

    to_relative = blocks_of(width, block)
    first = y_me == 0

    def other_clip(value):
        return jnp.where(first, value[1], value[0])

    def take_clip(value, theirs):
        mine = jnp.where(first, value[0], value[1])
        padding = ((0, 0), (0, quarter - row_count), (0, 0))
        both = jnp.pad(jnp.stack([mine, theirs]), padding).reshape(rows, width)
        return nn_dot(both, to_relative)

    def give_half(value):
        return exchange(value[quarter:].astype(bf16), "tensor", 2)

    def give_clip(value, theirs):
        mine = value[:quarter]
        theirs = nt_dot(theirs, to_relative)[:row_count]
        high = mine.astype(bf16)
        low = (mine - high.astype(f32)).astype(bf16)
        mine = (nt_dot(high, to_relative) + nt_dot(low, to_relative))[:row_count]
        return jnp.stack([jnp.where(first, mine, theirs), jnp.where(first, theirs, mine)])

    current = take_clip(frames, exchange(other_clip(frames), "tensor", 2))
    clip = other_clip(cotangent)

    for mask in dp_masks():
        got = exchange(by_width, "dp", mask), exchange(by_hidden, "dp", mask)
        if mask == 2:
            got = gathering.advance(*got)
        else:
            got = together(*got)
        by_width = jnp.concatenate([by_width, got[0]], axis=1)
        by_hidden = by_hidden + got[1]
    cut = 6 * layers
    own = jnp.concatenate([by_width, by_hidden])
    got, clip = gathering.advance(exchange(own[: cut + layers], "tensor", 1), clip)
    own = jnp.concatenate([own[:cut] + got[:cut], own[cut : cut + layers], got[cut:], own[cut + layers :]])
    (got,) = gathering.advance(exchange(own, "tensor", 2))
    vectors = own[:cut] + got[:cut]
    end = cut + 2 * layers
    biases = jnp.concatenate([own[cut:end], got[cut:end], own[end:], got[end:]])
    gain_all, shift_all = vectors[: 2 * layers], vectors[2 * layers : 4 * layers]

    def feed_weights(group):
        parts = gathering.until(group)
        return [
            [parts[2 * i], exchange(parts[2 * i], "tensor", 1), parts[2 * i + 1], exchange(parts[2 * i + 1], "tensor", 1)]
            for i in range(2)
        ]

    weights = []
    saved = []
    unit, _ = normalized(current)
    normed_a = (unit * gain_all[0] + shift_all[0]).astype(bf16)
    (normed_b,) = gathering.advance(exchange(normed_a, "tensor", 1))
    for at in range(layers):
        final = at == layers - 1
        w_qk, w_qk_other, w_vo, w_vo_other = gathering.until(2 * at)
        w_attn = ((w_qk, w_vo), (w_qk_other, w_vo_other))
        heads = []
        for t in range(2):
            before = (heads[0][1], w_attn[0][1]) if t else ()
            ready = behind((normed_a, normed_b), *gathering.tokens, *before[:1])
            row = 4 * layers + 2 * (t * layers + at)
            out = attend(row_count, quarter, row, *ready, *w_attn[t], biases, before)
            *shares, qkv, o, lse = gathering.advance(*out)
            heads.append((qkv, o, lse))
        share_b = exchange(shares[1], "tensor", 1)
        if not final:
            (share_b,) = gathering.advance(share_b)
        w_up, w_down = feed_weights(2 * at + 1)
        fed = feed(at, layers, current, shares[0], share_b, vectors, biases, w_up, w_down)
        if not final:
            fed = gathering.advance(*fed, *([exchange(clip, "tensor", 2)] if at == 0 else []))
            if at == 0:
                *fed, clip = fed
        weights.append((w_attn, w_up, w_down))
        normed = jnp.concatenate([normed_a, normed_b], axis=0)
        saved.append((current, normed, heads, fed[:4], fed[4:8], fed[8], fed[9]))
        current = fed[10]
        if not final:
            normed_a = fed[11]
            normed_b = exchange(normed_a, "tensor", 1)
    if layers == 1:
        clip = exchange(clip, "tensor", 2)
    small_grads = [None] * layers
    weight_grads = [None] * layers
    folding = None
    fronts = (take_clip(cotangent, clip),)
    for at in reversed(range(layers)):
        final = at == layers - 1
        w_attn, w_up, w_down = weights[at]
        layer_in, normed, heads, activated, slopes, middle, normed_two = saved[at]
        uppers = [] if folding is None else [folding]
        if uppers:
            fronts = behind(fronts, *folding.tokens())
        fed = feed_back(
            at, layers, fronts, middle, normed_two, vectors, w_up, w_down, activated, slopes
        )
        if final:
            *fed, encoded_half = together(*fed, give_half(current))
        own, other, bup, gradient, branch_a, sums = advance(uppers, *fed)
        branch_b = exchange(branch_a, "tensor", 1)
        core = Folding(own, other)

        def weight_grad(t, dqkv):
            dw = tn_dot(normed, dqkv).astype(bf16)
            o = heads[t][1]
            dw_o = (tn_dot(branch_a, o[:rows]) + tn_dot(branch_b, o[rows:])).astype(bf16)
            return dw[:, : 2 * wide], jnp.concatenate([dw[:, 2 * wide :], dw_o], axis=1)

        def state_tokens():
            return [part for fold in (core, *uppers) for part in fold.tokens()]

        if at == 0:
            advance([core, *uppers])
        elif uppers:
            advance(uppers)
        ready = behind((branch_a, branch_b), *state_tokens())
        dqkv_other, sums_other = advance(
            [core, *uppers],
            *attend_back(row_count, quarter, *ready, *w_attn[1], *heads[1], ()),
        )
        if at == 0:
            sent = jnp.concatenate(weight_grad(1, dqkv_other), axis=1)
            got = (exchange(sent, "tensor", 2),)
        else:
            sent, got = dqkv_other, ()
        ready = behind((branch_a, branch_b), sent, *state_tokens())
        *got, share_a, share_b, dqkv_own, sums_own = advance(
            [core, *uppers],
            *got,
            *attend_back(
                row_count, quarter, *ready, *w_attn[0], *heads[0], (dqkv_other, *w_attn[1])
            ),
        )
        if uppers:
            weight_grads[at + 1] = folding.result()
        share_b = exchange(share_b, "tensor", 1)
        dw_own = weight_grad(0, dqkv_own)
        if at == 0:
            dw_own = add_low(jnp.concatenate(dw_own, axis=1), got[0])
            folding = LastFolding(dw_own, *core.feed)
        else:
            dw_other = weight_grad(1, dqkv_other)
            core.attn = together(*[jnp.stack(pair) for pair in zip(dw_own, dw_other)])
            folding = core
        fronts = (gradient, layer_in, share_a, share_b)
        small_grads[at] = (sums, (sums_own, sums_other), bup)
    gradient, half, *small = finish(
        layers,
        quarter,
        wide,
        (
            layer_in,
            gradient,
            share_a,
            share_b,
            vectors,
            blocks_of(hidden, up_part),
            blocks_of(wide, qv_part),
        ),
        [small_grads[at][0] for at in range(layers)],
        [small_grads[at][2] for at in range(layers)],
        [part for at in range(layers) for part in small_grads[at][1]],
    )
    advance([folding])
    half, *small, folding.attn, folding.feed = together(
        half, *small, folding.attn, folding.feed
    )
    half, *got = advance(
        [folding],
        exchange(half, "tensor", 2),
        *[exchange(small[t], "tensor", t) for t in range(1, 4)],
    )
    small = small[0] + got[0] + got[1] + got[2]
    frames_grad = give_clip(gradient, half)
    for mask in reversed(dp_masks()):
        got = exchange(small[:, small.shape[1] // 2 :], "dp", mask)
        if folding.step < 3:
            (got,) = advance([folding], got)
        small = small[:, : small.shape[1] // 2] + got
        if folding.step == 3 and mask == 1:
            small, current, encoded_half = together(small, current, encoded_half)
    encoded = give_clip(current, encoded_half)
    weight_grads[0] = folding.result()
    by_width = lax.dynamic_slice(small, (0, t_me * norm_part), (6 * layers, norm_part))
    gains, shifts, obiases = by_width.reshape(3, layers, 2, norm_part)
    bups = small[6 * layers : 7 * layers, :up_part]
    bqv = small[7 * layers : 9 * layers, :qv_part].reshape(layers, 2, qv_part)

    def stacked(make):
        return jnp.stack([make(*weight_grads[at]) for at in range(layers)])

    return (
        encoded,
        frames_grad,
        stacked(lambda qk, vo, up, down: jnp.stack([qk[:, :wide], qk[:, wide:], vo[:, :wide]], axis=1)),
        stacked(lambda qk, vo, up, down: vo[:, wide:].T),
        stacked(lambda qk, vo, up, down: up),
        stacked(lambda qk, vo, up, down: down.T),
        bqv,
        bups,
        gains,
        shifts,
        obiases,
    )


def solution(mesh):
    in_specs = (
        P("dp", "tensor", None),
        P("dp", "tensor", None),
        P(None, "dp", None, "tensor"),
        P(None, "tensor", "dp"),
        P(None, "dp", "tensor"),
        P(None, "tensor", "dp"),
        P(None, None, ("tensor", "dp")),
        P(None, ("tensor", "dp")),
        P(None, None, ("dp", "tensor")),
        P(None, None, ("dp", "tensor")),
        P(None, None, ("dp", "tensor")),
    )
    out_specs = (
        P("dp", "tensor", None),
        P("dp", "tensor", None),
        P(None, "dp", None, "tensor"),
        P(None, "tensor", "dp"),
        P(None, "dp", "tensor"),
        P(None, "tensor", "dp"),
        P(None, None, ("tensor", "dp")),
        P(None, ("tensor", "dp")),
        P(None, None, ("dp", "tensor")),
        P(None, None, ("dp", "tensor")),
        P(None, None, ("dp", "tensor")),
    )
    return jax.shard_map(local, mesh=mesh, in_specs=in_specs, out_specs=out_specs, check_vma=False)
```

```python
import functools
import math

import jax
import jax.numpy as jnp
from jax import lax
from jax.experimental import pallas as pl
from jax.experimental.pallas import tpu as pltpu
from jax.sharding import PartitionSpec as P

HD = 64
WIDE = 128
eps = 1e-05
LOG2E = 1.0 / math.log(2.0)
LN2 = math.log(2.0)
MASKED = -1e30
bf16 = jnp.bfloat16
f32 = jnp.float32


def exchange(value, axis, mask):
    count = lax.axis_size(axis)
    return lax.ppermute(value, axis, [(i, i ^ mask) for i in range(count)])


def dp_masks():
    count = lax.axis_size("dp")
    masks = []
    while count > 1:
        count //= 2
        masks.append(count)
    return masks


def relative_mask(position):
    result = 0
    for at, mask in enumerate(dp_masks()):
        result = result + ((position >> at) & 1) * mask
    return result


def together(*values):
    return lax.optimization_barrier(values)


def gather_steps(first, second):
    masks = dp_masks()
    cut = first.shape[1]

    def z_step(mask):
        return (
            lambda state: (exchange(state[0], "dp", mask),),
            lambda state, got: (jnp.concatenate([state[0], got[0]], axis=0),),
        )

    near = (
        lambda state: (exchange(state[0], "dp", masks[-1]), exchange(state[1], "tensor", 2)),
        lambda state, got: (
            jnp.concatenate([state[0], got[0]], axis=0),
            state[1],
            got[1],
        ),
    )
    last = (
        lambda state: (
            exchange(state[0], "tensor", 2),
            exchange(state[1], "dp", masks[-1]),
            exchange(state[2], "dp", masks[-1]),
        ),
        lambda state, got: (
            state[0],
            got[0],
            *[jnp.concatenate([state[1 + i], got[1 + i]], axis=0) for i in range(2)],
        ),
    )

    def split(finish):
        def cut_last(state, got):
            block = finish(state, got)[0]
            return block[:, :cut], block[:, cut:]

        return cut_last

    ahead = [z_step(mask) for mask in masks[:-1]]
    ahead[-1] = (ahead[-1][0], split(ahead[-1][1]))
    return (jnp.concatenate([first, second], axis=1),), ahead, [near, last]


class Gathering:
    def __init__(self, groups):
        made = [gather_steps(*group) for group in groups]
        self.states = [start for start, _, _ in made]
        self.plan = [[(0, step)] for step in made[0][1]]
        for at, (_, _, near) in enumerate(made):
            ahead = [1] if at == 0 else [at + 1, at + 2] if at % 2 else []
            ahead = [(g, made[g][1]) for g in ahead if g < len(made)]
            for i in range(max([len(near)] + [len(steps) for _, steps in ahead])):
                stage = [(at, near[i])] if i < len(near) else []
                self.plan.append(stage + [(g, steps[i]) for g, steps in ahead if i < len(steps)])
        self.ends = [
            max(i for i, stage in enumerate(self.plan) for g, _ in stage if g == at)
            for at in range(len(made))
        ]
        self.done = 0
        self.tokens = ()

    def advance(self, *others):
        stage = self.plan[self.done]
        self.done += 1
        if stage[0][0] == 0 and len(stage) > 1:
            return self.start(stage, others)
        flat = [part for g, _ in stage for part in self.states[g]]
        flat = behind(flat, *self.tokens)
        states, received, at = [], [], 0
        for g, (send, _) in stage:
            states.append(flat[at : at + len(self.states[g])])
            at += len(self.states[g])
            received.append(send(states[-1]))
        flat = together(*[part for got in received for part in got], *others)
        at = 0
        for (g, (_, finish)), state, got in zip(stage, states, received):
            self.states[g] = finish(state, flat[at : at + len(got)])
            at += len(got)
        self.tokens = [part for g, _ in stage for part in self.states[g][:1]]
        return flat[at:]

    def start(self, stage, others):
        (first, (send, finish)), (second, (send_more, finish_more)) = stage
        state = behind(self.states[first], *self.tokens[:1])
        more = behind(self.states[second], state[0])
        got, got_more = send(state), send_more(more)
        flat = together(*got, *others)
        self.states[first] = finish(state, flat[: len(got)])
        self.states[second] = finish_more(more, got_more)
        self.tokens = [self.states[first][0], self.states[second][0]]
        return flat[len(got) :]

    def until(self, group):
        while self.done <= self.ends[group]:
            self.advance()
        return self.states[group]


def behind(values, *tokens):
    return together(*values, *tokens)[: len(values)]


def add_low(kept, received):
    return (kept.astype(f32) + received.astype(f32)).astype(bf16)


def near_one_sent(first, second):
    return first[1], second[:, second.shape[1] // 2 :]


def near_one(sent):
    return exchange(sent[0], "tensor", 2), exchange(sent[1], "dp", dp_masks()[-1])


def near_one_sum(first, second, got):
    return add_low(first[0], got[0]), add_low(second[:, : second.shape[1] // 2], got[1])


def near_two(first, second):
    half = first.shape[0] // 2
    return exchange(first[half:], "dp", dp_masks()[-1]), exchange(second[1], "tensor", 2)


def near_two_sum(first, second, got):
    return add_low(first[: first.shape[0] // 2], got[0]), add_low(second[0], got[1])


def far(value, masks):
    for mask in masks[:-1]:
        value = far_sum(value, exchange(value[value.shape[0] // 2 :], "dp", mask))
    return value, exchange(value[value.shape[0] // 2 :], "dp", masks[-1])


def far_sum(value, got):
    return add_low(value[: value.shape[0] // 2], got)


class Folding:
    def __init__(self, own, other):
        masks = dp_masks()[-2::-1]
        self.masks = masks[:-1], masks[-1:]
        self.own, self.other = own, other
        self.half = own.shape[1] // 2
        self.attn = None
        self.step = 0

    def send(self):
        step = self.step
        if step == 0:
            return (exchange(self.other, "tensor", 1),)
        if step == 1:
            return near_one(self.feed)
        if step == 2:
            got = near_two(*self.feed)
            return got if self.attn is None else got + near_one(near_one_sent(*self.attn))
        if step == 3:
            self.feed, more = far(self.feed, self.masks[0])
            return *near_two(*self.attn), more
        self.attn, *got = far(self.attn, self.masks[step - 4])
        if step == 4:
            self.feed, more = far(self.feed, self.masks[1])
            got.append(more)
        return got

    def finish(self, got):
        step, half = self.step, self.half
        self.step += 1
        if step == 0:
            own, other = self.own, got[0]
            self.kept = (own[0], other[0], own[2:, :half], other[2:, :half])
            self.feed = together(
                add_low(own[1], other[1]), add_low(own[2:, half:], other[2:, half:])
            )
        elif step == 1:
            first = self.kept[0].astype(f32) + self.kept[1].astype(f32) + got[0].astype(f32)
            second = self.kept[2].astype(f32) + self.kept[3].astype(f32) + got[1].astype(f32)
            self.feed = together(first.astype(bf16), second.astype(bf16))
        elif step == 2:
            self.feed = together(*near_two_sum(*self.feed, got[:2]))
            if self.attn is not None:
                self.feed = jnp.concatenate(self.feed, axis=1)
                self.attn = near_one_sum(*self.attn, got[2:])
                self.feed, *self.attn = together(self.feed, *self.attn)
        elif step == 3:
            self.attn = jnp.concatenate(near_two_sum(*self.attn, got[:2]), axis=1)
            self.feed = far_sum(self.feed, got[2])
            self.attn, self.feed = together(self.attn, self.feed)
        else:
            self.attn = far_sum(self.attn, got[0])
            if step == 4:
                self.feed = far_sum(self.feed, got[1])
            self.attn, self.feed = together(self.attn, self.feed)

    def tokens(self):
        if self.step == 0:
            return []
        parts = self.feed if self.step < 3 and isinstance(self.feed, (list, tuple)) else (self.feed,)
        if self.attn is None:
            return list(parts)
        return [*parts, *(self.attn if isinstance(self.attn, (list, tuple)) else (self.attn,))]

    def result(self):
        half, low = self.attn.shape[1] // 2, self.feed.shape[1] // 2
        parts = self.attn[:, :half], self.attn[:, half:], self.feed[:, :low], self.feed[:, low:]
        return [part.astype(f32) for part in parts]


class LastFolding:
    def __init__(self, attn, up, down):
        self.masks = dp_masks()[-2::-1]
        self.attn = attn
        self.feed = jnp.concatenate([up, down], axis=1)
        self.step = 0

    def send(self):
        first, last = self.masks[:-1], self.masks[-1:]
        self.attn, *got = far(self.attn, (dp_masks()[-1:], first, last)[self.step])
        if self.step < 2:
            self.feed, more = far(self.feed, (first, last)[self.step])
            got.append(more)
        return got

    def finish(self, got):
        self.attn = far_sum(self.attn, got[0])
        if self.step < 2:
            self.feed = far_sum(self.feed, got[1])
        self.attn, self.feed = together(self.attn, self.feed)
        self.step += 1

    result = Folding.result


def advance(folds, *others):
    received = [fold.send() for fold in folds]
    flat = together(*[part for got in received for part in got], *others)
    at = 0
    for fold, got in zip(folds, received):
        fold.finish(flat[at : at + len(got)])
        at += len(got)
    return flat[at:]


def split_low(value):
    high = value.astype(bf16)
    rest = value - high.astype(f32)
    mid = rest.astype(bf16)
    return high, mid, (rest - mid.astype(f32)).astype(bf16)


def lane_at(rows):
    return lax.broadcasted_iota(jnp.int32, (rows, WIDE - HD), 1)


def key_extra(rows, row_count, quarter, ones):
    lane = lane_at(rows)
    row = lax.broadcasted_iota(jnp.int32, (rows, WIDE - HD), 0)
    masked = lax.rem(row, quarter) >= row_count
    bias = jnp.where(masked, MASKED, 0.0).astype(f32)
    value = jnp.where(lane == 0, bias, jnp.where(lane <= ones, 1.0, 0.0))
    return value.astype(bf16)


def ones_extra(rows, ones):
    return jnp.where(lane_at(rows) < ones, 1.0, 0.0).astype(bf16)


def widen(part, extra):
    return jnp.concatenate([part, extra], axis=1)


def nt_dot(left, right):
    return lax.dot_general(left, right, (((1,), (1,)), ((), ())), preferred_element_type=f32)


def nn_dot(left, right):
    return lax.dot_general(left, right, (((1,), (0,)), ((), ())), preferred_element_type=f32)


def tn_dot(left, right):
    return lax.dot_general(left, right, (((0,), (0,)), ((), ())), preferred_element_type=f32)


def whole(shape):
    return pl.BlockSpec(shape, lambda j: (0,) * len(shape))


def single(shape):
    return pl.BlockSpec(shape, lambda j: (0,) * len(shape), pipeline_mode=pl.Buffered(1))


def attend_kernel(row_count, quarter, step, row, first, *refs):
    normed_a, normed_b, w_qk, w_vo, bias = refs[:5]
    if first:
        qkv, o, lse, q_s, k_s, v_s, o_s = refs[5:]
    else:
        o_before, w_before, share_a, share_b, qkv, o, lse, q_s, k_s, v_s, o_s = refs[5:]
    rows = normed_a.shape[0]
    wide = o.shape[1]
    heads = wide // HD
    k_more = key_extra(rows, row_count, quarter, 0)
    one = ones_extra(rows, 1)
    lane = lax.broadcasted_iota(jnp.int32, (1, 2 * wide), 1)
    scale = jnp.where(lane < wide, HD**-0.5 * LOG2E, 1.0)
    for half, normed in enumerate((normed_a, normed_b)):
        at = pl.ds(half * rows, rows)
        qk = nn_dot(normed[...], w_qk[...]) + bias[row : row + 1, : 2 * wide]
        qk = (qk * scale).astype(bf16)
        v = nn_dot(normed[...], w_vo[:, :wide]) + bias[row + 1 : row + 2, :wide]
        v = v.astype(bf16)
        qkv[at, : 2 * wide] = qk
        qkv[at, 2 * wide :] = v
        for h in range(heads):
            low, high = h * HD, (h + 1) * HD
            q_s[h, at, :] = widen(qk[:, low:high], one)
            k_s[h, at, :] = widen(qk[:, wide + low : wide + high], k_more)
            v_s[h, at, :] = widen(v[:, low:high], one)

    def work(h, carry):
        is_total = lax.broadcasted_iota(jnp.int32, (step, WIDE), 1) == HD
        for part in range(2 * rows // step):
            at = pl.ds(part * step, step)
            scores = nt_dot(q_s[h, at, :], k_s[h])
            top = jnp.max(scores, axis=-1, keepdims=True)
            summed = nn_dot(jnp.exp2(scores - top).astype(bf16), v_s[h])
            total = summed[:, HD : HD + 1]
            o_s[h, at, :] = jnp.where(is_total, top + jnp.log2(total), summed / total)
        return carry

    lax.fori_loop(0, heads, work, 0)
    for h in range(heads):
        o[:, h * HD : (h + 1) * HD] = o_s[h][:, :HD].astype(bf16)
        lse[:, h : h + 1] = o_s[h][:, HD : HD + 1]
    if not first:
        for half, share in enumerate((share_a, share_b)):
            at = pl.ds(half * rows, rows)
            value = nt_dot(o_before[at, :], w_before[:, wide:]) + nt_dot(o[at, :], w_vo[:, wide:])
            share[...] = value.astype(share.dtype)


def attend(row_count, quarter, row, normed_a, normed_b, w_qk, w_vo, bias, before):
    rows, width = normed_a.shape
    wide = w_qk.shape[1] // 2
    heads = wide // HD
    operands = (normed_a, normed_b, w_qk, w_vo, bias, *before)
    outs = [
        jax.ShapeDtypeStruct((2 * rows, 3 * wide), bf16),
        jax.ShapeDtypeStruct((2 * rows, wide), bf16),
        jax.ShapeDtypeStruct((2 * rows, 8), f32),
    ]
    if before:
        outs = [jax.ShapeDtypeStruct((rows, width), kind) for kind in (f32, bf16)] + outs
    return pl.pallas_call(
        functools.partial(attend_kernel, row_count, quarter, min(512, 2 * rows), row, not before),
        grid=(1,),
        in_specs=[single(part.shape) for part in operands],
        out_specs=[whole(part.shape) for part in outs],
        out_shape=outs,
        scratch_shapes=[pltpu.VMEM((heads, 2 * rows, WIDE), bf16)] * 3
        + [pltpu.VMEM((heads, 2 * rows, WIDE), f32)],
        compiler_params=pltpu.CompilerParams(vmem_limit_bytes=60 * 2**20),
    )(*operands)


def attend_back_kernel(row_count, quarter, step, first, *refs):
    branch_a, branch_b, w_qk, w_vo, qkv, o, lse = refs[:7]
    if first:
        dqkv, sums, q_s, k_s, kt_s, v_s, do_s, dq_s, dk_s, dv_s = refs[7:]
    else:
        dqkv_before, w_qk_before, w_vo_before, dn_a, dn_b = refs[7:12]
        dqkv, sums, q_s, k_s, kt_s, v_s, do_s, dq_s, dk_s, dv_s = refs[12:]
    rows = branch_a.shape[0]
    wide = o.shape[1]
    heads = wide // HD
    k_more = key_extra(rows, row_count, quarter, 3)
    three = ones_extra(rows, 3)
    lane = lane_at(rows)

    def spread_lanes(first, parts):
        value = jnp.where(lane < first, 1.0, 0.0).astype(f32)
        for at, part in enumerate(parts):
            value = jnp.where(lane == first + at, part.astype(f32), value)
        return value.astype(bf16)

    for half, branch in enumerate((branch_a, branch_b)):
        at = pl.ds(half * rows, rows)
        grad_all = nn_dot(branch[...], w_vo[:, wide:]).astype(bf16)
        for h in range(heads):
            low, high = h * HD, (h + 1) * HD
            minus_lse = split_low(-lse[at, h : h + 1])
            q_s[h, at, :] = widen(qkv[at, low:high], spread_lanes(1, minus_lse))
            keys = widen(qkv[at, wide + low : wide + high], k_more)
            k_s[h, at, :] = keys
            kt_s[h, :, at] = jnp.transpose(keys.astype(f32)).astype(bf16)
            v_s[h, at, :] = widen(qkv[at, 2 * wide + low : 2 * wide + high], three)
            grad = grad_all[:, low:high]
            inner = jnp.sum(grad.astype(f32) * o[at, low:high].astype(f32), axis=1, keepdims=True)
            do_s[h, at, :] = widen(grad, spread_lanes(0, split_low(-inner)))

    def work(h, carry):
        for part in range(2 * rows // step):
            at = pl.ds(part * step, step)
            queries = q_s[h, at, :]
            grad_out = do_s[h, at, :]
            probs = jnp.exp2(nt_dot(k_s[h], queries))
            grad_scores = (probs * nt_dot(v_s[h], grad_out)).astype(bf16)
            grad_values = nn_dot(probs.astype(bf16), grad_out)
            grad_keys = nn_dot(grad_scores, queries)
            if part == 0:
                dv_s[h] = grad_values
                dk_s[h] = grad_keys
            else:
                dv_s[h] += grad_values
                dk_s[h] += grad_keys
            dq_s[h, at, :] = jnp.transpose(nn_dot(kt_s[h], grad_scores))
        return carry

    lax.fori_loop(0, heads, work, 0)
    for h in range(heads):
        low, high = h * HD, (h + 1) * HD
        dqkv[:, low:high] = (dq_s[h][:, :HD] * HD**-0.5).astype(bf16)
        dqkv[:, wide + low : wide + high] = (dk_s[h][:, :HD] * LN2).astype(bf16)
        dqkv[:, 2 * wide + low : 2 * wide + high] = dv_s[h][:, :HD].astype(bf16)
    sums[...] = jnp.zeros_like(sums)
    sums[0:1, :] = jnp.sum(dqkv[...].astype(f32), axis=0, keepdims=True)
    if not first:
        for half, dest in enumerate((dn_a, dn_b)):
            at = pl.ds(half * rows, rows)
            part = nt_dot(dqkv[at, : 2 * wide], w_qk[...])
            part = part + nt_dot(dqkv[at, 2 * wide :], w_vo[:, :wide])
            part = part + nt_dot(dqkv_before[at, : 2 * wide], w_qk_before[...])
            part = part + nt_dot(dqkv_before[at, 2 * wide :], w_vo_before[:, :wide])
            dest[...] = part.astype(dest.dtype)


def attend_back(row_count, quarter, branch_a, branch_b, w_qk, w_vo, qkv, o, lse, before):
    rows, width = branch_a.shape
    wide = o.shape[1]
    heads = wide // HD
    operands = (branch_a, branch_b, w_qk, w_vo, qkv, o, lse, *before)
    outs = [
        jax.ShapeDtypeStruct((2 * rows, 3 * wide), bf16),
        jax.ShapeDtypeStruct((8, 3 * wide), f32),
    ]
    if before:
        outs = [jax.ShapeDtypeStruct((rows, width), kind) for kind in (f32, bf16)] + outs
    return pl.pallas_call(
        functools.partial(attend_back_kernel, row_count, quarter, min(512, 2 * rows), not before),
        grid=(1,),
        in_specs=[single(part.shape) for part in operands],
        out_specs=[whole(part.shape) for part in outs],
        out_shape=outs,
        scratch_shapes=[
            pltpu.VMEM((heads, 2 * rows, WIDE), bf16),
            pltpu.VMEM((heads, 2 * rows, WIDE), bf16),
            pltpu.VMEM((heads, WIDE, 2 * rows), bf16),
            pltpu.VMEM((heads, 2 * rows, WIDE), bf16),
            pltpu.VMEM((heads, 2 * rows, WIDE), bf16),
            pltpu.VMEM((heads, 2 * rows, WIDE), f32),
            pltpu.VMEM((heads, 2 * rows, WIDE), f32),
            pltpu.VMEM((heads, 2 * rows, WIDE), f32),
        ],
        compiler_params=pltpu.CompilerParams(vmem_limit_bytes=62 * 2**20),
    )(*operands)


def normalized(value):
    centred = value - jnp.mean(value, axis=-1, keepdims=True)
    scale = lax.rsqrt(jnp.mean(centred * centred, axis=-1, keepdims=True) + eps)
    return centred * scale, scale


def norm_back(value, gain, grad):
    unit, scale = normalized(value)
    scaled = grad * gain
    result = scale * (
        scaled
        - jnp.mean(scaled, axis=-1, keepdims=True)
        - unit * jnp.mean(scaled * unit, axis=-1, keepdims=True)
    )
    sums = [jnp.sum(part, axis=0, keepdims=True) for part in (grad * unit, grad)]
    return result, *sums


def gelu_both(value):
    share = 0.5 * (1.0 + lax.erf(value * math.sqrt(0.5)))
    density = jnp.exp(-0.5 * value * value) * (1.0 / math.sqrt(2.0 * math.pi))
    return (value * share).astype(bf16), (share + value * density).astype(bf16)


def feed_kernel(at, layers, *refs):
    final = at == layers - 1
    gain, shift, obias = 2 * at, 2 * layers + 2 * at, 4 * layers + 2 * at
    current, share_a, share_b, vectors, bias = refs[:5]
    ups, downs, activated, slopes = [refs[5 + 4 * i : 9 + 4 * i] for i in range(4)]
    middle, normed, total = refs[21:24]
    j = pl.program_id(0)

    @pl.when(j == 0)
    def _():
        value = current[...] + (share_a[...] + share_b[...].astype(f32) + vectors[obias : obias + 1, :])
        middle[...] = value
        unit, _ = normalized(value)
        unit = unit * vectors[gain + 1 : gain + 2, :] + vectors[shift + 1 : shift + 2, :]
        normed[...] = unit.astype(bf16)
        total[...] = value + vectors[obias + 1 : obias + 2, :]

    rows_in = normed[...]
    for t in range(4):
        upward = nn_dot(rows_in, ups[t][...]) + bias[t * layers + at : t * layers + at + 1, :]
        activated[t][...], slopes[t][...] = gelu_both(upward)
    joined = jnp.concatenate([ref[...] for ref in activated], axis=1)
    down = jnp.concatenate([ref[...] for ref in downs], axis=1)
    total[...] += nt_dot(joined, down)
    if not final:
        following = refs[24]

        @pl.when(j == pl.num_programs(0) - 1)
        def _():
            unit, _ = normalized(total[...])
            unit = unit * vectors[gain + 2 : gain + 3, :] + vectors[shift + 2 : shift + 3, :]
            following[...] = unit.astype(bf16)


def column_block(rows, step):
    return pl.BlockSpec((rows, step), lambda j: (0, j))


def feed(at, layers, current, share_a, share_b, vectors, bias, ups, downs):
    rows, width = current.shape
    hidden = ups[0].shape[1]
    step = min(256, hidden)
    rest = [f32, bf16, f32] if at == layers - 1 else [f32, bf16, f32, bf16]
    fronts = (current, share_a, share_b, vectors)
    return pl.pallas_call(
        functools.partial(feed_kernel, at, layers),
        grid=(hidden // step,),
        in_specs=[single(part.shape) for part in fronts]
        + [column_block(bias.shape[0], step)]
        + [column_block(width, step)] * 8,
        out_specs=[column_block(rows, step)] * 8 + [whole((rows, width))] * len(rest),
        out_shape=[jax.ShapeDtypeStruct((rows, hidden), bf16)] * 8
        + [jax.ShapeDtypeStruct((rows, width), kind) for kind in rest],
        compiler_params=pltpu.CompilerParams(vmem_limit_bytes=60 * 2**20),
    )(*fronts, bias, *ups, *downs)


def feed_back_kernel(at, layers, *refs):
    final = at == layers - 1
    gain = 2 * at
    count = 1 if final else 4
    fronts, refs = refs[:count], refs[count:]
    middle, normed, vectors = refs[:3]
    ups, downs, activated, slopes = [refs[3 + 4 * i : 7 + 4 * i] for i in range(4)]
    own, other, bias_grad, grad_out, branch, sums = refs[19:25]
    total, grad, grad_low, normed_t, grad_t = refs[25:]
    j = pl.program_id(0)

    @pl.when(j == 0)
    def _():
        sums[...] = jnp.zeros_like(sums)
        if final:
            value = fronts[0][...].astype(f32)
        else:
            above, layer_out, share_a, share_b = fronts
            grad_normed = share_a[...] + share_b[...].astype(f32)
            value, gain_one, shift_one = norm_back(
                layer_out[...], vectors[gain + 2 : gain + 3, :], grad_normed
            )
            value = value + above[...]
            sums[4:5, :], sums[5:6, :] = gain_one, shift_one
        grad[...] = value
        low = value.astype(bf16)
        grad_low[...] = low
        sums[0:1, :] = jnp.sum(low.astype(f32), axis=0, keepdims=True)
        normed_t[...] = jnp.transpose(normed[...].astype(f32)).astype(bf16)
        grad_t[...] = jnp.transpose(low.astype(f32)).astype(bf16)
        total[...] = jnp.zeros_like(total)

    grad_rows = grad_low[...]
    grad_ups = []
    for t in range(4):
        grad_act = nn_dot(grad_rows, downs[t][...])
        scaled = grad_act * slopes[t][...].astype(f32)
        grad_ups.append(scaled.astype(bf16))
        bias_grad[t : t + 1, :] = jnp.sum(scaled, axis=0, keepdims=True)
        dest = (own, other)[t % 2]
        dest[t // 2] = nn_dot(normed_t[...], grad_ups[t]).astype(bf16)
        dest[2 + t // 2] = nn_dot(grad_t[...], activated[t][...]).astype(bf16)
    joined = jnp.concatenate(grad_ups, axis=1)
    up = jnp.concatenate([ref[...] for ref in ups], axis=1)
    total[...] += nt_dot(joined, up)

    @pl.when(j == pl.num_programs(0) - 1)
    def _():
        value, gain_two, shift_two = norm_back(
            middle[...], vectors[gain + 1 : gain + 2, :], total[...]
        )
        value = value + grad[...]
        grad_out[...] = value
        low = value.astype(bf16)
        branch[...] = low
        sums[1:2, :], sums[2:3, :] = gain_two, shift_two
        sums[3:4, :] = jnp.sum(low.astype(f32), axis=0, keepdims=True)


def feed_back(at, layers, fronts, middle, normed, vectors, ups, downs, activated, slopes):
    rows, width = normed.shape
    hidden = activated[0].shape[1]
    step = min(256, hidden)
    stack = pl.BlockSpec((4, width, step), lambda j: (0, 0, j))
    singles = (*fronts, middle, normed, vectors)
    return pl.pallas_call(
        functools.partial(feed_back_kernel, at, layers),
        grid=(hidden // step,),
        in_specs=[single(part.shape) for part in singles]
        + [column_block(width, step)] * 8
        + [column_block(rows, step)] * 8,
        out_specs=[stack] * 2
        + [column_block(4, step)]
        + [whole((rows, width))] * 2
        + [whole((8, width))],
        out_shape=[jax.ShapeDtypeStruct((4, width, hidden), bf16)] * 2
        + [
            jax.ShapeDtypeStruct((4, hidden), f32),
            jax.ShapeDtypeStruct((rows, width), f32),
            jax.ShapeDtypeStruct((rows, width), bf16),
            jax.ShapeDtypeStruct((8, width), f32),
        ],
        scratch_shapes=[pltpu.VMEM((rows, width), f32)] * 2
        + [pltpu.VMEM((rows, width), bf16)]
        + [pltpu.VMEM((width, rows), bf16)] * 2,
        compiler_params=pltpu.CompilerParams(vmem_limit_bytes=62 * 2**20),
    )(*singles, *ups, *downs, *activated, *slopes)


def finish_kernel(layers, wide, *refs):
    layer_in, above, share_a, share_b, gain, up_blocks, head_blocks = refs[:7]
    sums, biases, heads = refs[7 : 7 + layers], refs[7 + layers : 7 + 2 * layers], refs[7 + 2 * layers : 7 + 4 * layers]
    grad, low, *small = refs[7 + 4 * layers :]
    grad_normed = share_a[...] + share_b[...].astype(f32)
    value, gain_one, shift_one = norm_back(layer_in[...], gain[0:1, :], grad_normed)
    value = value + above[...]
    grad[...] = value
    low[...] = value[low.shape[0] :, :].astype(bf16)

    def reorder(part, blocks):
        return sum(nn_dot(piece, blocks[...]) for piece in split_low(part))

    for t in range(4):
        small[t][...] = jnp.zeros_like(small[t])
        small[t][0:1, :] = gain_one
        small[t][2 * layers : 2 * layers + 1, :] = shift_one
    for at in range(layers):
        rows = [(2 * at + 1, 1), (2 * (layers + at) + 1, 2)]
        rows += [(4 * layers + 2 * at, 3), (4 * layers + 2 * at + 1, 0)]
        if at + 1 < layers:
            rows += [(2 * (at + 1), 4), (2 * (layers + at + 1), 5)]
        bias = reorder(biases[at][...], up_blocks)
        for t in range(4):
            for dest, source in rows:
                small[t][dest : dest + 1, :] = sums[at][source : source + 1, :]
            small[t][6 * layers + at : 6 * layers + at + 1, :] = bias[t : t + 1, :]
        for group in range(2):
            both = heads[2 * at + group]
            for i, first in enumerate((0, 2 * wide)):
                dest = 7 * layers + 2 * at + i
                row = reorder(both[:, first : first + wide], head_blocks)
                small[2 * group][dest : dest + 1, :] = row[0:1, :]


def finish(layers, quarter, wide, fronts, sums, biases, heads):
    rows, width = fronts[0].shape
    operands = (*fronts, *sums, *biases, *heads)
    count = -(-9 * layers // 8) * 8
    outs = [jax.ShapeDtypeStruct((rows, width), f32), jax.ShapeDtypeStruct((rows - quarter, width), bf16)]
    outs += [jax.ShapeDtypeStruct((count, width), f32)] * 4
    return pl.pallas_call(
        functools.partial(finish_kernel, layers, wide),
        grid=(1,),
        in_specs=[single(part.shape) for part in operands],
        out_specs=[whole(part.shape) for part in outs],
        out_shape=outs,
        compiler_params=pltpu.CompilerParams(vmem_limit_bytes=56 * 2**20),
    )(*operands)


def local(
    frames,
    cotangent,
    qkv_weight,
    out_weight,
    up_weight,
    down_weight,
    qv_bias,
    up_bias,
    norm_gains,
    norm_shifts,
    out_biases,
):
    layers, block = qkv_weight.shape[:2]
    wide = qkv_weight.shape[3]
    row_count, width = frames.shape[1:]
    hidden = up_weight.shape[2]
    quarter = -(-row_count // 128) * 128
    rows = 2 * quarter
    me = lax.axis_index("dp")
    t_me = lax.axis_index("tensor")
    y_me = t_me // 2

    def blocks_of(size, part):
        lane = jnp.arange(width)
        source = (relative_mask(lane // block) ^ me) * part + lane % block
        return (
            (jnp.arange(size)[:, None] == source[None, :]) & (lane % block < part)[None, :]
        ).astype(bf16)

    norm_part, up_part, qv_part = norm_gains.shape[2], up_bias.shape[1], qv_bias.shape[2]

    def place(part, size, at):
        room = jnp.zeros((part.shape[0], size), f32)
        return lax.dynamic_update_slice(room, part, (0, at))

    groups = []
    for at in range(layers):
        qk = jnp.concatenate([qkv_weight[at, :, 0], qkv_weight[at, :, 1]], axis=1)
        vo = jnp.concatenate([qkv_weight[at, :, 2], out_weight[at].T], axis=1)
        groups += [(qk, vo), (up_weight[at], down_weight[at].T)]
    gathering = Gathering(groups)
    norm_gains, up_bias, frames, cotangent = behind(
        (norm_gains, up_bias, frames, cotangent), *gathering.states[0]
    )
    by_width = jnp.stack([norm_gains, norm_shifts, out_biases]).reshape(6 * layers, norm_part)
    by_width = place(by_width, 4 * norm_part, t_me * norm_part)
    by_hidden = jnp.concatenate(
        [
            place(up_bias, width, me * up_part),
            place(qv_bias.reshape(2 * layers, qv_part), width, me * qv_part),
        ]
    )

    to_relative = blocks_of(width, block)
    first = y_me == 0

    def other_clip(value):
        return jnp.where(first, value[1], value[0])

    def take_clip(value, theirs):
        mine = jnp.where(first, value[0], value[1])
        padding = ((0, 0), (0, quarter - row_count), (0, 0))
        both = jnp.pad(jnp.stack([mine, theirs]), padding).reshape(rows, width)
        return nn_dot(both, to_relative)

    def give_half(value):
        return exchange(value[quarter:].astype(bf16), "tensor", 2)

    def give_clip(value, theirs):
        mine = value[:quarter]
        theirs = nt_dot(theirs, to_relative)[:row_count]
        high = mine.astype(bf16)
        low = (mine - high.astype(f32)).astype(bf16)
        mine = (nt_dot(high, to_relative) + nt_dot(low, to_relative))[:row_count]
        return jnp.stack([jnp.where(first, mine, theirs), jnp.where(first, theirs, mine)])

    current = take_clip(frames, exchange(other_clip(frames), "tensor", 2))
    clip = other_clip(cotangent)

    for mask in dp_masks():
        got = exchange(by_width, "dp", mask), exchange(by_hidden, "dp", mask)
        if mask == 2:
            got = gathering.advance(*got)
        else:
            got = together(*got)
        by_width = jnp.concatenate([by_width, got[0]], axis=1)
        by_hidden = by_hidden + got[1]
    cut = 6 * layers
    own = jnp.concatenate([by_width, by_hidden])
    got, clip = gathering.advance(exchange(own[: cut + layers], "tensor", 1), clip)
    own = jnp.concatenate([own[:cut] + got[:cut], own[cut : cut + layers], got[cut:], own[cut + layers :]])
    (got,) = gathering.advance(exchange(own, "tensor", 2))
    vectors = own[:cut] + got[:cut]
    end = cut + 2 * layers
    biases = jnp.concatenate([own[cut:end], got[cut:end], own[end:], got[end:]])
    gain_all, shift_all = vectors[: 2 * layers], vectors[2 * layers : 4 * layers]

    def feed_weights(group):
        parts = gathering.until(group)
        return [
            [parts[2 * i], exchange(parts[2 * i], "tensor", 1), parts[2 * i + 1], exchange(parts[2 * i + 1], "tensor", 1)]
            for i in range(2)
        ]

    weights = []
    saved = []
    unit, _ = normalized(current)
    normed_a = (unit * gain_all[0] + shift_all[0]).astype(bf16)
    (normed_b,) = gathering.advance(exchange(normed_a, "tensor", 1))
    for at in range(layers):
        final = at == layers - 1
        w_qk, w_qk_other, w_vo, w_vo_other = gathering.until(2 * at)
        w_attn = ((w_qk, w_vo), (w_qk_other, w_vo_other))
        heads = []
        for t in range(2):
            before = (heads[0][1], w_attn[0][1]) if t else ()
            ready = behind((normed_a, normed_b), *gathering.tokens, *before[:1])
            row = 4 * layers + 2 * (t * layers + at)
            out = attend(row_count, quarter, row, *ready, *w_attn[t], biases, before)
            *shares, qkv, o, lse = gathering.advance(*out)
            heads.append((qkv, o, lse))
        share_b = exchange(shares[1], "tensor", 1)
        if not final:
            (share_b,) = gathering.advance(share_b)
        w_up, w_down = feed_weights(2 * at + 1)
        fed = feed(at, layers, current, shares[0], share_b, vectors, biases, w_up, w_down)
        if not final:
            fed = gathering.advance(*fed, *([exchange(clip, "tensor", 2)] if at == 0 else []))
            if at == 0:
                *fed, clip = fed
        weights.append((w_attn, w_up, w_down))
        normed = jnp.concatenate([normed_a, normed_b], axis=0)
        saved.append((current, normed, heads, fed[:4], fed[4:8], fed[8], fed[9]))
        current = fed[10]
        if not final:
            normed_a = fed[11]
            normed_b = exchange(normed_a, "tensor", 1)
    if layers == 1:
        clip = exchange(clip, "tensor", 2)
    small_grads = [None] * layers
    weight_grads = [None] * layers
    folding = None
    fronts = (take_clip(cotangent, clip),)
    for at in reversed(range(layers)):
        final = at == layers - 1
        w_attn, w_up, w_down = weights[at]
        layer_in, normed, heads, activated, slopes, middle, normed_two = saved[at]
        uppers = [] if folding is None else [folding]
        if uppers:
            fronts = behind(fronts, *folding.tokens())
        fed = feed_back(
            at, layers, fronts, middle, normed_two, vectors, w_up, w_down, activated, slopes
        )
        if final:
            *fed, encoded_half = together(*fed, give_half(current))
        own, other, bup, gradient, branch_a, sums = advance(uppers, *fed)
        branch_b = exchange(branch_a, "tensor", 1)
        core = Folding(own, other)

        def weight_grad(t, dqkv):
            dw = tn_dot(normed, dqkv).astype(bf16)
            o = heads[t][1]
            dw_o = (tn_dot(branch_a, o[:rows]) + tn_dot(branch_b, o[rows:])).astype(bf16)
            return dw[:, : 2 * wide], jnp.concatenate([dw[:, 2 * wide :], dw_o], axis=1)

        def state_tokens():
            return [part for fold in (core, *uppers) for part in fold.tokens()]

        if at == 0:
            advance([core, *uppers])
        elif uppers:
            advance(uppers)
        ready = behind((branch_a, branch_b), *state_tokens())
        dqkv_other, sums_other = advance(
            [core, *uppers],
            *attend_back(row_count, quarter, *ready, *w_attn[1], *heads[1], ()),
        )
        if at == 0:
            sent = jnp.concatenate(weight_grad(1, dqkv_other), axis=1)
            got = (exchange(sent, "tensor", 2),)
        else:
            sent, got = dqkv_other, ()
        ready = behind((branch_a, branch_b), sent, *state_tokens())
        *got, share_a, share_b, dqkv_own, sums_own = advance(
            [core, *uppers],
            *got,
            *attend_back(
                row_count, quarter, *ready, *w_attn[0], *heads[0], (dqkv_other, *w_attn[1])
            ),
        )
        if uppers:
            weight_grads[at + 1] = folding.result()
        share_b = exchange(share_b, "tensor", 1)
        dw_own = weight_grad(0, dqkv_own)
        if at == 0:
            dw_own = add_low(jnp.concatenate(dw_own, axis=1), got[0])
            folding = LastFolding(dw_own, *core.feed)
        else:
            dw_other = weight_grad(1, dqkv_other)
            core.attn = together(*[jnp.stack(pair) for pair in zip(dw_own, dw_other)])
            folding = core
        fronts = (gradient, layer_in, share_a, share_b)
        small_grads[at] = (sums, (sums_own, sums_other), bup)
    out = finish(
        layers,
        quarter,
        wide,
        (
            layer_in,
            gradient,
            share_a,
            share_b,
            vectors,
            blocks_of(hidden, up_part),
            blocks_of(wide, qv_part),
        ),
        [small_grads[at][0] for at in range(layers)],
        [small_grads[at][2] for at in range(layers)],
        [part for at in range(layers) for part in small_grads[at][1]],
    )
    gradient, half, *small = advance([folding], *out)
    got = advance([folding], *[exchange(small[t], "tensor", t) for t in range(1, 4)])
    small = small[0] + got[0] + got[1] + got[2]
    half, small = together(half, small)
    half = exchange(half, "tensor", 2)
    frames_grad = give_clip(gradient, half)
    for mask in reversed(dp_masks()):
        got = exchange(small[:, small.shape[1] // 2 :], "dp", mask)
        if folding.step < 3:
            (got,) = advance([folding], got)
        small = small[:, : small.shape[1] // 2] + got
        if folding.step == 3 and mask == 1:
            small, current, encoded_half = together(small, current, encoded_half)
    encoded = give_clip(current, encoded_half)
    weight_grads[0] = folding.result()
    by_width = lax.dynamic_slice(small, (0, t_me * norm_part), (6 * layers, norm_part))
    gains, shifts, obiases = by_width.reshape(3, layers, 2, norm_part)
    bups = small[6 * layers : 7 * layers, :up_part]
    bqv = small[7 * layers : 9 * layers, :qv_part].reshape(layers, 2, qv_part)

    def stacked(make):
        return jnp.stack([make(*weight_grads[at]) for at in range(layers)])

    return (
        encoded,
        frames_grad,
        stacked(lambda qk, vo, up, down: jnp.stack([qk[:, :wide], qk[:, wide:], vo[:, :wide]], axis=1)),
        stacked(lambda qk, vo, up, down: vo[:, wide:].T),
        stacked(lambda qk, vo, up, down: up),
        stacked(lambda qk, vo, up, down: down.T),
        bqv,
        bups,
        gains,
        shifts,
        obiases,
    )


def solution(mesh):
    in_specs = (
        P("dp", "tensor", None),
        P("dp", "tensor", None),
        P(None, "dp", None, "tensor"),
        P(None, "tensor", "dp"),
        P(None, "dp", "tensor"),
        P(None, "tensor", "dp"),
        P(None, None, ("tensor", "dp")),
        P(None, ("tensor", "dp")),
        P(None, None, ("dp", "tensor")),
        P(None, None, ("dp", "tensor")),
        P(None, None, ("dp", "tensor")),
    )
    out_specs = (
        P("dp", "tensor", None),
        P("dp", "tensor", None),
        P(None, "dp", None, "tensor"),
        P(None, "tensor", "dp"),
        P(None, "dp", "tensor"),
        P(None, "tensor", "dp"),
        P(None, None, ("tensor", "dp")),
        P(None, ("tensor", "dp")),
        P(None, None, ("dp", "tensor")),
        P(None, None, ("dp", "tensor")),
        P(None, None, ("dp", "tensor")),
    )
    return jax.shard_map(local, mesh=mesh, in_specs=in_specs, out_specs=out_specs, check_vma=False)
```

```python
import functools
import math

import jax
import jax.numpy as jnp
from jax import lax
from jax.experimental import pallas as pl
from jax.experimental.pallas import tpu as pltpu
from jax.sharding import PartitionSpec as P

HD = 64
WIDE = 128
eps = 1e-05
LOG2E = 1.0 / math.log(2.0)
LN2 = math.log(2.0)
MASKED = -1e30
bf16 = jnp.bfloat16
f32 = jnp.float32


def exchange(value, axis, mask):
    count = lax.axis_size(axis)
    return lax.ppermute(value, axis, [(i, i ^ mask) for i in range(count)])


def dp_masks():
    count = lax.axis_size("dp")
    masks = []
    while count > 1:
        count //= 2
        masks.append(count)
    return masks


def relative_mask(position):
    result = 0
    for at, mask in enumerate(dp_masks()):
        result = result + ((position >> at) & 1) * mask
    return result


def together(*values):
    return lax.optimization_barrier(values)


def gather_steps(first, second):
    masks = dp_masks()
    cut = first.shape[1]

    def z_step(mask):
        return (
            lambda state: (exchange(state[0], "dp", mask),),
            lambda state, got: (jnp.concatenate([state[0], got[0]], axis=0),),
        )

    near = (
        lambda state: (exchange(state[0], "dp", masks[-1]), exchange(state[1], "tensor", 2)),
        lambda state, got: (
            jnp.concatenate([state[0], got[0]], axis=0),
            state[1],
            got[1],
        ),
    )
    last = (
        lambda state: (
            exchange(state[0], "tensor", 2),
            exchange(state[1], "dp", masks[-1]),
            exchange(state[2], "dp", masks[-1]),
        ),
        lambda state, got: (
            state[0],
            got[0],
            *[jnp.concatenate([state[1 + i], got[1 + i]], axis=0) for i in range(2)],
        ),
    )

    def split(finish):
        def cut_last(state, got):
            block = finish(state, got)[0]
            return block[:, :cut], block[:, cut:]

        return cut_last

    ahead = [z_step(mask) for mask in masks[:-1]]
    ahead[-1] = (ahead[-1][0], split(ahead[-1][1]))
    return (jnp.concatenate([first, second], axis=1),), ahead, [near, last]


class Gathering:
    def __init__(self, groups):
        made = [gather_steps(*group) for group in groups]
        self.states = [start for start, _, _ in made]
        self.plan = [[(0, step)] for step in made[0][1]]
        for at, (_, _, near) in enumerate(made):
            ahead = [1] if at == 0 else [at + 1, at + 2] if at % 2 else []
            ahead = [(g, made[g][1]) for g in ahead if g < len(made)]
            for i in range(max([len(near)] + [len(steps) for _, steps in ahead])):
                stage = [(at, near[i])] if i < len(near) else []
                self.plan.append(stage + [(g, steps[i]) for g, steps in ahead if i < len(steps)])
        self.ends = [
            max(i for i, stage in enumerate(self.plan) for g, _ in stage if g == at)
            for at in range(len(made))
        ]
        self.done = 0
        self.tokens = ()

    def advance(self, *others):
        stage = self.plan[self.done]
        self.done += 1
        if stage[0][0] == 0 and len(stage) > 1:
            return self.start(stage, others)
        flat = [part for g, _ in stage for part in self.states[g]]
        flat = behind(flat, *self.tokens)
        states, received, at = [], [], 0
        for g, (send, _) in stage:
            states.append(flat[at : at + len(self.states[g])])
            at += len(self.states[g])
            received.append(send(states[-1]))
        flat = together(*[part for got in received for part in got], *others)
        at = 0
        for (g, (_, finish)), state, got in zip(stage, states, received):
            self.states[g] = finish(state, flat[at : at + len(got)])
            at += len(got)
        self.tokens = [part for g, _ in stage for part in self.states[g][:1]]
        return flat[at:]

    def start(self, stage, others):
        (first, (send, finish)), (second, (send_more, finish_more)) = stage
        state = behind(self.states[first], *self.tokens[:1])
        more = behind(self.states[second], state[0])
        got, got_more = send(state), send_more(more)
        flat = together(*got, *others)
        self.states[first] = finish(state, flat[: len(got)])
        self.states[second] = finish_more(more, got_more)
        self.tokens = [self.states[first][0], self.states[second][0]]
        return flat[len(got) :]

    def until(self, group):
        while self.done <= self.ends[group]:
            self.advance()
        return self.states[group]


def behind(values, *tokens):
    return together(*values, *tokens)[: len(values)]


def add_low(kept, received):
    return (kept.astype(f32) + received.astype(f32)).astype(bf16)


def near_one_sent(first, second):
    return first[1], second[:, second.shape[1] // 2 :]


def near_one(sent):
    return exchange(sent[0], "tensor", 2), exchange(sent[1], "dp", dp_masks()[-1])


def near_one_sum(first, second, got):
    return add_low(first[0], got[0]), add_low(second[:, : second.shape[1] // 2], got[1])


def near_two(first, second):
    half = first.shape[0] // 2
    return exchange(first[half:], "dp", dp_masks()[-1]), exchange(second[1], "tensor", 2)


def near_two_sum(first, second, got):
    return add_low(first[: first.shape[0] // 2], got[0]), add_low(second[0], got[1])


def far(value, masks):
    for mask in masks[:-1]:
        value = far_sum(value, exchange(value[value.shape[0] // 2 :], "dp", mask))
    return value, exchange(value[value.shape[0] // 2 :], "dp", masks[-1])


def far_sum(value, got):
    return add_low(value[: value.shape[0] // 2], got)


class Folding:
    def __init__(self, own, other):
        masks = dp_masks()[-2::-1]
        self.masks = masks[:-1], masks[-1:]
        self.own, self.other = own, other
        self.half = own.shape[1] // 2
        self.attn = None
        self.step = 0

    def send(self):
        step = self.step
        if step == 0:
            return (exchange(self.other, "tensor", 1),)
        if step == 1:
            return near_one(self.feed)
        if step == 2:
            got = near_two(*self.feed)
            return got if self.attn is None else got + near_one(near_one_sent(*self.attn))
        if step == 3:
            self.feed, more = far(self.feed, self.masks[0])
            return *near_two(*self.attn), more
        self.attn, *got = far(self.attn, self.masks[step - 4])
        if step == 4:
            self.feed, more = far(self.feed, self.masks[1])
            got.append(more)
        return got

    def finish(self, got):
        step, half = self.step, self.half
        self.step += 1
        if step == 0:
            own, other = self.own, got[0]
            self.kept = (own[0], other[0], own[2:, :half], other[2:, :half])
            self.feed = together(
                add_low(own[1], other[1]), add_low(own[2:, half:], other[2:, half:])
            )
        elif step == 1:
            first = self.kept[0].astype(f32) + self.kept[1].astype(f32) + got[0].astype(f32)
            second = self.kept[2].astype(f32) + self.kept[3].astype(f32) + got[1].astype(f32)
            self.feed = together(first.astype(bf16), second.astype(bf16))
        elif step == 2:
            self.feed = together(*near_two_sum(*self.feed, got[:2]))
            if self.attn is not None:
                self.feed = jnp.concatenate(self.feed, axis=1)
                self.attn = near_one_sum(*self.attn, got[2:])
                self.feed, *self.attn = together(self.feed, *self.attn)
        elif step == 3:
            self.attn = jnp.concatenate(near_two_sum(*self.attn, got[:2]), axis=1)
            self.feed = far_sum(self.feed, got[2])
            self.attn, self.feed = together(self.attn, self.feed)
        else:
            self.attn = far_sum(self.attn, got[0])
            if step == 4:
                self.feed = far_sum(self.feed, got[1])
            self.attn, self.feed = together(self.attn, self.feed)

    def tokens(self):
        if self.step == 0:
            return []
        parts = self.feed if self.step < 3 and isinstance(self.feed, (list, tuple)) else (self.feed,)
        if self.attn is None:
            return list(parts)
        return [*parts, *(self.attn if isinstance(self.attn, (list, tuple)) else (self.attn,))]

    def result(self):
        half, low = self.attn.shape[1] // 2, self.feed.shape[1] // 2
        parts = self.attn[:, :half], self.attn[:, half:], self.feed[:, :low], self.feed[:, low:]
        return [part.astype(f32) for part in parts]


class LastFolding:
    def __init__(self, attn, up, down):
        self.masks = dp_masks()[-2::-1]
        self.attn = attn
        self.feed = jnp.concatenate([up, down], axis=1)
        self.step = 0

    def send(self):
        first, last = self.masks[:-1], self.masks[-1:]
        self.attn, *got = far(self.attn, (dp_masks()[-1:], first, last)[self.step])
        if self.step < 2:
            self.feed, more = far(self.feed, (first, last)[self.step])
            got.append(more)
        return got

    def finish(self, got):
        self.attn = far_sum(self.attn, got[0])
        if self.step < 2:
            self.feed = far_sum(self.feed, got[1])
        self.attn, self.feed = together(self.attn, self.feed)
        self.step += 1

    result = Folding.result


def advance(folds, *others):
    received = [fold.send() for fold in folds]
    flat = together(*[part for got in received for part in got], *others)
    at = 0
    for fold, got in zip(folds, received):
        fold.finish(flat[at : at + len(got)])
        at += len(got)
    return flat[at:]


def split_low(value):
    high = value.astype(bf16)
    rest = value - high.astype(f32)
    mid = rest.astype(bf16)
    return high, mid, (rest - mid.astype(f32)).astype(bf16)


def lane_at(rows):
    return lax.broadcasted_iota(jnp.int32, (rows, WIDE - HD), 1)


def key_extra(rows, row_count, quarter, ones):
    lane = lane_at(rows)
    row = lax.broadcasted_iota(jnp.int32, (rows, WIDE - HD), 0)
    masked = lax.rem(row, quarter) >= row_count
    bias = jnp.where(masked, MASKED, 0.0).astype(f32)
    value = jnp.where(lane == 0, bias, jnp.where(lane <= ones, 1.0, 0.0))
    return value.astype(bf16)


def ones_extra(rows, ones):
    return jnp.where(lane_at(rows) < ones, 1.0, 0.0).astype(bf16)


def widen(part, extra):
    return jnp.concatenate([part, extra], axis=1)


def nt_dot(left, right):
    return lax.dot_general(left, right, (((1,), (1,)), ((), ())), preferred_element_type=f32)


def nn_dot(left, right):
    return lax.dot_general(left, right, (((1,), (0,)), ((), ())), preferred_element_type=f32)


def tn_dot(left, right):
    return lax.dot_general(left, right, (((0,), (0,)), ((), ())), preferred_element_type=f32)


def whole(shape):
    return pl.BlockSpec(shape, lambda j: (0,) * len(shape))


def single(shape):
    return pl.BlockSpec(shape, lambda j: (0,) * len(shape), pipeline_mode=pl.Buffered(1))


def attend_kernel(row_count, quarter, step, row, first, *refs):
    normed_a, normed_b, w_qk, w_vo, bias = refs[:5]
    if first:
        qkv, o, lse, q_s, k_s, v_s, o_s = refs[5:]
    else:
        o_before, w_before, share_a, share_b, qkv, o, lse, q_s, k_s, v_s, o_s = refs[5:]
    rows = normed_a.shape[0]
    wide = o.shape[1]
    heads = wide // HD
    k_more = key_extra(rows, row_count, quarter, 0)
    one = ones_extra(rows, 1)
    lane = lax.broadcasted_iota(jnp.int32, (1, 2 * wide), 1)
    scale = jnp.where(lane < wide, HD**-0.5 * LOG2E, 1.0)
    for half, normed in enumerate((normed_a, normed_b)):
        at = pl.ds(half * rows, rows)
        qk = nn_dot(normed[...], w_qk[...]) + bias[row : row + 1, : 2 * wide]
        qk = (qk * scale).astype(bf16)
        v = nn_dot(normed[...], w_vo[:, :wide]) + bias[row + 1 : row + 2, :wide]
        v = v.astype(bf16)
        qkv[at, : 2 * wide] = qk
        qkv[at, 2 * wide :] = v
        for h in range(heads):
            low, high = h * HD, (h + 1) * HD
            q_s[h, at, :] = widen(qk[:, low:high], one)
            k_s[h, at, :] = widen(qk[:, wide + low : wide + high], k_more)
            v_s[h, at, :] = widen(v[:, low:high], one)

    def work(h, carry):
        is_total = lax.broadcasted_iota(jnp.int32, (step, WIDE), 1) == HD
        for part in range(2 * rows // step):
            at = pl.ds(part * step, step)
            scores = nt_dot(q_s[h, at, :], k_s[h])
            top = jnp.max(scores, axis=-1, keepdims=True)
            summed = nn_dot(jnp.exp2(scores - top).astype(bf16), v_s[h])
            total = summed[:, HD : HD + 1]
            o_s[h, at, :] = jnp.where(is_total, top + jnp.log2(total), summed / total)
        return carry

    lax.fori_loop(0, heads, work, 0)
    for h in range(heads):
        o[:, h * HD : (h + 1) * HD] = o_s[h][:, :HD].astype(bf16)
        lse[:, h : h + 1] = o_s[h][:, HD : HD + 1]
    if not first:
        for half, share in enumerate((share_a, share_b)):
            at = pl.ds(half * rows, rows)
            value = nt_dot(o_before[at, :], w_before[:, wide:]) + nt_dot(o[at, :], w_vo[:, wide:])
            share[...] = value.astype(share.dtype)


def attend(row_count, quarter, row, normed_a, normed_b, w_qk, w_vo, bias, before):
    rows, width = normed_a.shape
    wide = w_qk.shape[1] // 2
    heads = wide // HD
    operands = (normed_a, normed_b, w_qk, w_vo, bias, *before)
    outs = [
        jax.ShapeDtypeStruct((2 * rows, 3 * wide), bf16),
        jax.ShapeDtypeStruct((2 * rows, wide), bf16),
        jax.ShapeDtypeStruct((2 * rows, 8), f32),
    ]
    if before:
        outs = [jax.ShapeDtypeStruct((rows, width), kind) for kind in (f32, bf16)] + outs
    return pl.pallas_call(
        functools.partial(attend_kernel, row_count, quarter, min(512, 2 * rows), row, not before),
        grid=(1,),
        in_specs=[single(part.shape) for part in operands],
        out_specs=[whole(part.shape) for part in outs],
        out_shape=outs,
        scratch_shapes=[pltpu.VMEM((heads, 2 * rows, WIDE), bf16)] * 3
        + [pltpu.VMEM((heads, 2 * rows, WIDE), f32)],
        compiler_params=pltpu.CompilerParams(vmem_limit_bytes=60 * 2**20),
    )(*operands)


def attend_back_kernel(row_count, quarter, step, first, *refs):
    branch_a, branch_b, w_qk, w_vo, qkv, o, lse = refs[:7]
    if first:
        dqkv, sums, q_s, k_s, kt_s, v_s, do_s, dq_s, dk_s, dv_s = refs[7:]
    else:
        dqkv_before, w_qk_before, w_vo_before, dn_a, dn_b = refs[7:12]
        dqkv, sums, q_s, k_s, kt_s, v_s, do_s, dq_s, dk_s, dv_s = refs[12:]
    rows = branch_a.shape[0]
    wide = o.shape[1]
    heads = wide // HD
    k_more = key_extra(rows, row_count, quarter, 3)
    three = ones_extra(rows, 3)
    lane = lane_at(rows)

    def spread_lanes(first, parts):
        value = jnp.where(lane < first, 1.0, 0.0).astype(f32)
        for at, part in enumerate(parts):
            value = jnp.where(lane == first + at, part.astype(f32), value)
        return value.astype(bf16)

    for half, branch in enumerate((branch_a, branch_b)):
        at = pl.ds(half * rows, rows)
        grad_all = nn_dot(branch[...], w_vo[:, wide:]).astype(bf16)
        for h in range(heads):
            low, high = h * HD, (h + 1) * HD
            minus_lse = split_low(-lse[at, h : h + 1])
            q_s[h, at, :] = widen(qkv[at, low:high], spread_lanes(1, minus_lse))
            keys = widen(qkv[at, wide + low : wide + high], k_more)
            k_s[h, at, :] = keys
            kt_s[h, :, at] = jnp.transpose(keys.astype(f32)).astype(bf16)
            v_s[h, at, :] = widen(qkv[at, 2 * wide + low : 2 * wide + high], three)
            grad = grad_all[:, low:high]
            inner = jnp.sum(grad.astype(f32) * o[at, low:high].astype(f32), axis=1, keepdims=True)
            do_s[h, at, :] = widen(grad, spread_lanes(0, split_low(-inner)))

    def work(h, carry):
        for part in range(2 * rows // step):
            at = pl.ds(part * step, step)
            queries = q_s[h, at, :]
            grad_out = do_s[h, at, :]
            probs = jnp.exp2(nt_dot(k_s[h], queries))
            grad_scores = (probs * nt_dot(v_s[h], grad_out)).astype(bf16)
            grad_values = nn_dot(probs.astype(bf16), grad_out)
            grad_keys = nn_dot(grad_scores, queries)
            if part == 0:
                dv_s[h] = grad_values
                dk_s[h] = grad_keys
            else:
                dv_s[h] += grad_values
                dk_s[h] += grad_keys
            dq_s[h, at, :] = jnp.transpose(nn_dot(kt_s[h], grad_scores))
        return carry

    lax.fori_loop(0, heads, work, 0)
    for h in range(heads):
        low, high = h * HD, (h + 1) * HD
        dqkv[:, low:high] = (dq_s[h][:, :HD] * HD**-0.5).astype(bf16)
        dqkv[:, wide + low : wide + high] = (dk_s[h][:, :HD] * LN2).astype(bf16)
        dqkv[:, 2 * wide + low : 2 * wide + high] = dv_s[h][:, :HD].astype(bf16)
    sums[...] = jnp.zeros_like(sums)
    sums[0:1, :] = jnp.sum(dqkv[...].astype(f32), axis=0, keepdims=True)
    if not first:
        for half, dest in enumerate((dn_a, dn_b)):
            at = pl.ds(half * rows, rows)
            part = nt_dot(dqkv[at, : 2 * wide], w_qk[...])
            part = part + nt_dot(dqkv[at, 2 * wide :], w_vo[:, :wide])
            part = part + nt_dot(dqkv_before[at, : 2 * wide], w_qk_before[...])
            part = part + nt_dot(dqkv_before[at, 2 * wide :], w_vo_before[:, :wide])
            dest[...] = part.astype(dest.dtype)


def attend_back(row_count, quarter, branch_a, branch_b, w_qk, w_vo, qkv, o, lse, before):
    rows, width = branch_a.shape
    wide = o.shape[1]
    heads = wide // HD
    operands = (branch_a, branch_b, w_qk, w_vo, qkv, o, lse, *before)
    outs = [
        jax.ShapeDtypeStruct((2 * rows, 3 * wide), bf16),
        jax.ShapeDtypeStruct((8, 3 * wide), f32),
    ]
    if before:
        outs = [jax.ShapeDtypeStruct((rows, width), kind) for kind in (f32, bf16)] + outs
    return pl.pallas_call(
        functools.partial(attend_back_kernel, row_count, quarter, min(512, 2 * rows), not before),
        grid=(1,),
        in_specs=[single(part.shape) for part in operands],
        out_specs=[whole(part.shape) for part in outs],
        out_shape=outs,
        scratch_shapes=[
            pltpu.VMEM((heads, 2 * rows, WIDE), bf16),
            pltpu.VMEM((heads, 2 * rows, WIDE), bf16),
            pltpu.VMEM((heads, WIDE, 2 * rows), bf16),
            pltpu.VMEM((heads, 2 * rows, WIDE), bf16),
            pltpu.VMEM((heads, 2 * rows, WIDE), bf16),
            pltpu.VMEM((heads, 2 * rows, WIDE), f32),
            pltpu.VMEM((heads, 2 * rows, WIDE), f32),
            pltpu.VMEM((heads, 2 * rows, WIDE), f32),
        ],
        compiler_params=pltpu.CompilerParams(vmem_limit_bytes=62 * 2**20),
    )(*operands)


def normalized(value):
    centred = value - jnp.mean(value, axis=-1, keepdims=True)
    scale = lax.rsqrt(jnp.mean(centred * centred, axis=-1, keepdims=True) + eps)
    return centred * scale, scale


def norm_back(value, gain, grad):
    unit, scale = normalized(value)
    scaled = grad * gain
    result = scale * (
        scaled
        - jnp.mean(scaled, axis=-1, keepdims=True)
        - unit * jnp.mean(scaled * unit, axis=-1, keepdims=True)
    )
    sums = [jnp.sum(part, axis=0, keepdims=True) for part in (grad * unit, grad)]
    return result, *sums


def gelu_both(value):
    share = 0.5 * (1.0 + lax.erf(value * math.sqrt(0.5)))
    density = jnp.exp(-0.5 * value * value) * (1.0 / math.sqrt(2.0 * math.pi))
    return (value * share).astype(bf16), (share + value * density).astype(bf16)


def feed_kernel(at, layers, *refs):
    final = at == layers - 1
    gain, shift, obias = 2 * at, 2 * layers + 2 * at, 4 * layers + 2 * at
    current, share_a, share_b, vectors, bias = refs[:5]
    ups, downs, activated, slopes = [refs[5 + 4 * i : 9 + 4 * i] for i in range(4)]
    middle, normed, total = refs[21:24]
    j = pl.program_id(0)

    @pl.when(j == 0)
    def _():
        value = current[...] + (share_a[...] + share_b[...].astype(f32) + vectors[obias : obias + 1, :])
        middle[...] = value
        unit, _ = normalized(value)
        unit = unit * vectors[gain + 1 : gain + 2, :] + vectors[shift + 1 : shift + 2, :]
        normed[...] = unit.astype(bf16)
        total[...] = value + vectors[obias + 1 : obias + 2, :]

    rows_in = normed[...]
    for t in range(4):
        upward = nn_dot(rows_in, ups[t][...]) + bias[t * layers + at : t * layers + at + 1, :]
        activated[t][...], slopes[t][...] = gelu_both(upward)
    joined = jnp.concatenate([ref[...] for ref in activated], axis=1)
    down = jnp.concatenate([ref[...] for ref in downs], axis=1)
    total[...] += nt_dot(joined, down)
    if not final:
        following = refs[24]

        @pl.when(j == pl.num_programs(0) - 1)
        def _():
            unit, _ = normalized(total[...])
            unit = unit * vectors[gain + 2 : gain + 3, :] + vectors[shift + 2 : shift + 3, :]
            following[...] = unit.astype(bf16)


def column_block(rows, step):
    return pl.BlockSpec((rows, step), lambda j: (0, j))


def feed(at, layers, current, share_a, share_b, vectors, bias, ups, downs):
    rows, width = current.shape
    hidden = ups[0].shape[1]
    step = min(256, hidden)
    rest = [f32, bf16, f32] if at == layers - 1 else [f32, bf16, f32, bf16]
    fronts = (current, share_a, share_b, vectors)
    return pl.pallas_call(
        functools.partial(feed_kernel, at, layers),
        grid=(hidden // step,),
        in_specs=[single(part.shape) for part in fronts]
        + [column_block(bias.shape[0], step)]
        + [column_block(width, step)] * 8,
        out_specs=[column_block(rows, step)] * 8 + [whole((rows, width))] * len(rest),
        out_shape=[jax.ShapeDtypeStruct((rows, hidden), bf16)] * 8
        + [jax.ShapeDtypeStruct((rows, width), kind) for kind in rest],
        compiler_params=pltpu.CompilerParams(vmem_limit_bytes=60 * 2**20),
    )(*fronts, bias, *ups, *downs)


def feed_back_kernel(at, layers, *refs):
    final = at == layers - 1
    gain = 2 * at
    count = 1 if final else 4
    fronts, refs = refs[:count], refs[count:]
    middle, normed, vectors = refs[:3]
    ups, downs, activated, slopes = [refs[3 + 4 * i : 7 + 4 * i] for i in range(4)]
    own, other, bias_grad, grad_out, branch, sums = refs[19:25]
    total, grad, grad_low, normed_t, grad_t = refs[25:]
    j = pl.program_id(0)

    @pl.when(j == 0)
    def _():
        sums[...] = jnp.zeros_like(sums)
        if final:
            value = fronts[0][...].astype(f32)
        else:
            above, layer_out, share_a, share_b = fronts
            grad_normed = share_a[...] + share_b[...].astype(f32)
            value, gain_one, shift_one = norm_back(
                layer_out[...], vectors[gain + 2 : gain + 3, :], grad_normed
            )
            value = value + above[...]
            sums[4:5, :], sums[5:6, :] = gain_one, shift_one
        grad[...] = value
        low = value.astype(bf16)
        grad_low[...] = low
        sums[0:1, :] = jnp.sum(low.astype(f32), axis=0, keepdims=True)
        normed_t[...] = jnp.transpose(normed[...].astype(f32)).astype(bf16)
        grad_t[...] = jnp.transpose(low.astype(f32)).astype(bf16)
        total[...] = jnp.zeros_like(total)

    grad_rows = grad_low[...]
    grad_ups = []
    for t in range(4):
        grad_act = nn_dot(grad_rows, downs[t][...])
        scaled = grad_act * slopes[t][...].astype(f32)
        grad_ups.append(scaled.astype(bf16))
        bias_grad[t : t + 1, :] = jnp.sum(scaled, axis=0, keepdims=True)
        dest = (own, other)[t % 2]
        dest[t // 2] = nn_dot(normed_t[...], grad_ups[t]).astype(bf16)
        dest[2 + t // 2] = nn_dot(grad_t[...], activated[t][...]).astype(bf16)
    joined = jnp.concatenate(grad_ups, axis=1)
    up = jnp.concatenate([ref[...] for ref in ups], axis=1)
    total[...] += nt_dot(joined, up)

    @pl.when(j == pl.num_programs(0) - 1)
    def _():
        value, gain_two, shift_two = norm_back(
            middle[...], vectors[gain + 1 : gain + 2, :], total[...]
        )
        value = value + grad[...]
        grad_out[...] = value
        low = value.astype(bf16)
        branch[...] = low
        sums[1:2, :], sums[2:3, :] = gain_two, shift_two
        sums[3:4, :] = jnp.sum(low.astype(f32), axis=0, keepdims=True)


def feed_back(at, layers, fronts, middle, normed, vectors, ups, downs, activated, slopes):
    rows, width = normed.shape
    hidden = activated[0].shape[1]
    step = min(256, hidden)
    stack = pl.BlockSpec((4, width, step), lambda j: (0, 0, j))
    singles = (*fronts, middle, normed, vectors)
    return pl.pallas_call(
        functools.partial(feed_back_kernel, at, layers),
        grid=(hidden // step,),
        in_specs=[single(part.shape) for part in singles]
        + [column_block(width, step)] * 8
        + [column_block(rows, step)] * 8,
        out_specs=[stack] * 2
        + [column_block(4, step)]
        + [whole((rows, width))] * 2
        + [whole((8, width))],
        out_shape=[jax.ShapeDtypeStruct((4, width, hidden), bf16)] * 2
        + [
            jax.ShapeDtypeStruct((4, hidden), f32),
            jax.ShapeDtypeStruct((rows, width), f32),
            jax.ShapeDtypeStruct((rows, width), bf16),
            jax.ShapeDtypeStruct((8, width), f32),
        ],
        scratch_shapes=[pltpu.VMEM((rows, width), f32)] * 2
        + [pltpu.VMEM((rows, width), bf16)]
        + [pltpu.VMEM((width, rows), bf16)] * 2,
        compiler_params=pltpu.CompilerParams(vmem_limit_bytes=62 * 2**20),
    )(*singles, *ups, *downs, *activated, *slopes)


def finish_kernel(layers, wide, *refs):
    layer_in, above, share_a, share_b, gain, up_blocks, head_blocks = refs[:7]
    sums, biases, heads = refs[7 : 7 + layers], refs[7 + layers : 7 + 2 * layers], refs[7 + 2 * layers : 7 + 4 * layers]
    grad, low, *small = refs[7 + 4 * layers :]
    grad_normed = share_a[...] + share_b[...].astype(f32)
    value, gain_one, shift_one = norm_back(layer_in[...], gain[0:1, :], grad_normed)
    value = value + above[...]
    grad[...] = value
    low[...] = value[low.shape[0] :, :].astype(bf16)

    def reorder(part, blocks):
        return sum(nn_dot(piece, blocks[...]) for piece in split_low(part))

    for t in range(4):
        small[t][...] = jnp.zeros_like(small[t])
        small[t][0:1, :] = gain_one
        small[t][2 * layers : 2 * layers + 1, :] = shift_one
    for at in range(layers):
        rows = [(2 * at + 1, 1), (2 * (layers + at) + 1, 2)]
        rows += [(4 * layers + 2 * at, 3), (4 * layers + 2 * at + 1, 0)]
        if at + 1 < layers:
            rows += [(2 * (at + 1), 4), (2 * (layers + at + 1), 5)]
        bias = reorder(biases[at][...], up_blocks)
        for t in range(4):
            for dest, source in rows:
                small[t][dest : dest + 1, :] = sums[at][source : source + 1, :]
            small[t][6 * layers + at : 6 * layers + at + 1, :] = bias[t : t + 1, :]
        for group in range(2):
            both = heads[2 * at + group]
            for i, first in enumerate((0, 2 * wide)):
                dest = 7 * layers + 2 * at + i
                row = reorder(both[:, first : first + wide], head_blocks)
                small[2 * group][dest : dest + 1, :] = row[0:1, :]


def finish(layers, quarter, wide, fronts, sums, biases, heads):
    rows, width = fronts[0].shape
    operands = (*fronts, *sums, *biases, *heads)
    count = -(-9 * layers // 8) * 8
    outs = [jax.ShapeDtypeStruct((rows, width), f32), jax.ShapeDtypeStruct((rows - quarter, width), bf16)]
    outs += [jax.ShapeDtypeStruct((count, width), f32)] * 4
    return pl.pallas_call(
        functools.partial(finish_kernel, layers, wide),
        grid=(1,),
        in_specs=[single(part.shape) for part in operands],
        out_specs=[whole(part.shape) for part in outs],
        out_shape=outs,
        compiler_params=pltpu.CompilerParams(vmem_limit_bytes=56 * 2**20),
    )(*operands)


def local(
    frames,
    cotangent,
    qkv_weight,
    out_weight,
    up_weight,
    down_weight,
    qv_bias,
    up_bias,
    norm_gains,
    norm_shifts,
    out_biases,
):
    layers, block = qkv_weight.shape[:2]
    wide = qkv_weight.shape[3]
    row_count, width = frames.shape[1:]
    hidden = up_weight.shape[2]
    quarter = -(-row_count // 128) * 128
    rows = 2 * quarter
    me = lax.axis_index("dp")
    t_me = lax.axis_index("tensor")
    y_me = t_me // 2

    def blocks_of(size, part):
        lane = jnp.arange(width)
        source = (relative_mask(lane // block) ^ me) * part + lane % block
        return (
            (jnp.arange(size)[:, None] == source[None, :]) & (lane % block < part)[None, :]
        ).astype(bf16)

    norm_part, up_part, qv_part = norm_gains.shape[2], up_bias.shape[1], qv_bias.shape[2]

    def place(part, size, at):
        room = jnp.zeros((part.shape[0], size), f32)
        return lax.dynamic_update_slice(room, part, (0, at))

    groups = []
    for at in range(layers):
        qk = jnp.concatenate([qkv_weight[at, :, 0], qkv_weight[at, :, 1]], axis=1)
        vo = jnp.concatenate([qkv_weight[at, :, 2], out_weight[at].T], axis=1)
        groups += [(qk, vo), (up_weight[at], down_weight[at].T)]
    gathering = Gathering(groups)
    norm_gains, up_bias, frames, cotangent = behind(
        (norm_gains, up_bias, frames, cotangent), *gathering.states[0]
    )
    by_width = jnp.stack([norm_gains, norm_shifts, out_biases]).reshape(6 * layers, norm_part)
    by_width = place(by_width, 4 * norm_part, t_me * norm_part)
    by_hidden = jnp.concatenate(
        [
            place(up_bias, width, me * up_part),
            place(qv_bias.reshape(2 * layers, qv_part), width, me * qv_part),
        ]
    )

    to_relative = blocks_of(width, block)
    first = y_me == 0

    def other_clip(value):
        return jnp.where(first, value[1], value[0])

    def take_clip(value, theirs):
        mine = jnp.where(first, value[0], value[1])
        padding = ((0, 0), (0, quarter - row_count), (0, 0))
        both = jnp.pad(jnp.stack([mine, theirs]), padding).reshape(rows, width)
        return nn_dot(both, to_relative)

    def give_half(value):
        return exchange(value[quarter:].astype(bf16), "tensor", 2)

    def give_clip(value, theirs):
        mine = value[:quarter]
        theirs = nt_dot(theirs, to_relative)[:row_count]
        high = mine.astype(bf16)
        low = (mine - high.astype(f32)).astype(bf16)
        mine = (nt_dot(high, to_relative) + nt_dot(low, to_relative))[:row_count]
        return jnp.stack([jnp.where(first, mine, theirs), jnp.where(first, theirs, mine)])

    current = take_clip(frames, exchange(other_clip(frames), "tensor", 2))
    clip = other_clip(cotangent)

    for mask in dp_masks():
        got = exchange(by_width, "dp", mask), exchange(by_hidden, "dp", mask)
        if mask == 2:
            got = gathering.advance(*got)
        else:
            got = together(*got)
        by_width = jnp.concatenate([by_width, got[0]], axis=1)
        by_hidden = by_hidden + got[1]
    cut = 6 * layers
    own = jnp.concatenate([by_width, by_hidden])
    got, clip = gathering.advance(exchange(own[: cut + layers], "tensor", 1), clip)
    own = jnp.concatenate([own[:cut] + got[:cut], own[cut : cut + layers], got[cut:], own[cut + layers :]])
    (got,) = gathering.advance(exchange(own, "tensor", 2))
    vectors = own[:cut] + got[:cut]
    end = cut + 2 * layers
    biases = jnp.concatenate([own[cut:end], got[cut:end], own[end:], got[end:]])
    gain_all, shift_all = vectors[: 2 * layers], vectors[2 * layers : 4 * layers]

    def feed_weights(group):
        parts = gathering.until(group)
        return [
            [parts[2 * i], exchange(parts[2 * i], "tensor", 1), parts[2 * i + 1], exchange(parts[2 * i + 1], "tensor", 1)]
            for i in range(2)
        ]

    weights = []
    saved = []
    unit, _ = normalized(current)
    normed_a = (unit * gain_all[0] + shift_all[0]).astype(bf16)
    (normed_b,) = gathering.advance(exchange(normed_a, "tensor", 1))
    for at in range(layers):
        final = at == layers - 1
        w_qk, w_qk_other, w_vo, w_vo_other = gathering.until(2 * at)
        w_attn = ((w_qk, w_vo), (w_qk_other, w_vo_other))
        heads = []
        for t in range(2):
            before = (heads[0][1], w_attn[0][1]) if t else ()
            ready = behind((normed_a, normed_b), *gathering.tokens, *before[:1])
            row = 4 * layers + 2 * (t * layers + at)
            out = attend(row_count, quarter, row, *ready, *w_attn[t], biases, before)
            *shares, qkv, o, lse = gathering.advance(*out)
            heads.append((qkv, o, lse))
        share_b = exchange(shares[1], "tensor", 1)
        if not final:
            (share_b,) = gathering.advance(share_b)
        w_up, w_down = feed_weights(2 * at + 1)
        fed = feed(at, layers, current, shares[0], share_b, vectors, biases, w_up, w_down)
        if not final:
            fed = gathering.advance(*fed, *([exchange(clip, "tensor", 2)] if at == 0 else []))
            if at == 0:
                *fed, clip = fed
        weights.append((w_attn, w_up, w_down))
        normed = jnp.concatenate([normed_a, normed_b], axis=0)
        saved.append((current, normed, heads, fed[:4], fed[4:8], fed[8], fed[9]))
        current = fed[10]
        if not final:
            normed_a = fed[11]
            normed_b = exchange(normed_a, "tensor", 1)
    if layers == 1:
        clip = exchange(clip, "tensor", 2)
    small_grads = [None] * layers
    weight_grads = [None] * layers
    folding = None
    fronts = (take_clip(cotangent, clip),)
    for at in reversed(range(layers)):
        final = at == layers - 1
        w_attn, w_up, w_down = weights[at]
        layer_in, normed, heads, activated, slopes, middle, normed_two = saved[at]
        uppers = [] if folding is None else [folding]
        if uppers:
            fronts = behind(fronts, *folding.tokens())
        fed = feed_back(
            at, layers, fronts, middle, normed_two, vectors, w_up, w_down, activated, slopes
        )
        if final:
            *fed, encoded_half = together(*fed, give_half(current))
        own, other, bup, gradient, branch_a, sums = advance(uppers, *fed)
        branch_b = exchange(branch_a, "tensor", 1)
        core = Folding(own, other)

        def weight_grad(t, dqkv):
            dw = tn_dot(normed, dqkv).astype(bf16)
            o = heads[t][1]
            dw_o = (tn_dot(branch_a, o[:rows]) + tn_dot(branch_b, o[rows:])).astype(bf16)
            return dw[:, : 2 * wide], jnp.concatenate([dw[:, 2 * wide :], dw_o], axis=1)

        def state_tokens():
            return [part for fold in (core, *uppers) for part in fold.tokens()]

        if at == 0:
            advance([core, *uppers])
        elif uppers:
            advance(uppers)
        ready = behind((branch_a, branch_b), *state_tokens())
        dqkv_other, sums_other = advance(
            [core, *uppers],
            *attend_back(row_count, quarter, *ready, *w_attn[1], *heads[1], ()),
        )
        if at == 0:
            sent = jnp.concatenate(weight_grad(1, dqkv_other), axis=1)
            got = (exchange(sent, "tensor", 2),)
        else:
            sent, got = dqkv_other, ()
        ready = behind((branch_a, branch_b), sent, *state_tokens())
        *got, share_a, share_b, dqkv_own, sums_own = advance(
            [core, *uppers],
            *got,
            *attend_back(
                row_count, quarter, *ready, *w_attn[0], *heads[0], (dqkv_other, *w_attn[1])
            ),
        )
        if uppers:
            weight_grads[at + 1] = folding.result()
        share_b = exchange(share_b, "tensor", 1)
        dw_own = weight_grad(0, dqkv_own)
        if at == 0:
            dw_own = add_low(jnp.concatenate(dw_own, axis=1), got[0])
            folding = LastFolding(dw_own, *core.feed)
        else:
            dw_other = weight_grad(1, dqkv_other)
            core.attn = together(*[jnp.stack(pair) for pair in zip(dw_own, dw_other)])
            folding = core
        fronts = (gradient, layer_in, share_a, share_b)
        small_grads[at] = (sums, (sums_own, sums_other), bup)
    out = finish(
        layers,
        quarter,
        wide,
        (
            layer_in,
            gradient,
            share_a,
            share_b,
            vectors,
            blocks_of(hidden, up_part),
            blocks_of(wide, qv_part),
        ),
        [small_grads[at][0] for at in range(layers)],
        [small_grads[at][2] for at in range(layers)],
        [part for at in range(layers) for part in small_grads[at][1]],
    )
    gradient, half, *small = advance([folding], *out)
    got = advance([folding], *[exchange(small[t], "tensor", t) for t in range(1, 4)])
    small = small[0] + got[0] + got[1] + got[2]
    half, small, current, encoded_half = together(half, small, current, encoded_half)
    half = exchange(half, "tensor", 2)
    frames_grad = give_clip(gradient, half)
    for mask in reversed(dp_masks()):
        got = exchange(small[:, small.shape[1] // 2 :], "dp", mask)
        if folding.step < 3:
            (got,) = advance([folding], got)
        small = small[:, : small.shape[1] // 2] + got
    encoded = give_clip(current, encoded_half)
    weight_grads[0] = folding.result()
    by_width = lax.dynamic_slice(small, (0, t_me * norm_part), (6 * layers, norm_part))
    gains, shifts, obiases = by_width.reshape(3, layers, 2, norm_part)
    bups = small[6 * layers : 7 * layers, :up_part]
    bqv = small[7 * layers : 9 * layers, :qv_part].reshape(layers, 2, qv_part)

    def stacked(make):
        return jnp.stack([make(*weight_grads[at]) for at in range(layers)])

    return (
        encoded,
        frames_grad,
        stacked(lambda qk, vo, up, down: jnp.stack([qk[:, :wide], qk[:, wide:], vo[:, :wide]], axis=1)),
        stacked(lambda qk, vo, up, down: vo[:, wide:].T),
        stacked(lambda qk, vo, up, down: up),
        stacked(lambda qk, vo, up, down: down.T),
        bqv,
        bups,
        gains,
        shifts,
        obiases,
    )


def solution(mesh):
    in_specs = (
        P("dp", "tensor", None),
        P("dp", "tensor", None),
        P(None, "dp", None, "tensor"),
        P(None, "tensor", "dp"),
        P(None, "dp", "tensor"),
        P(None, "tensor", "dp"),
        P(None, None, ("tensor", "dp")),
        P(None, ("tensor", "dp")),
        P(None, None, ("dp", "tensor")),
        P(None, None, ("dp", "tensor")),
        P(None, None, ("dp", "tensor")),
    )
    out_specs = (
        P("dp", "tensor", None),
        P("dp", "tensor", None),
        P(None, "dp", None, "tensor"),
        P(None, "tensor", "dp"),
        P(None, "dp", "tensor"),
        P(None, "tensor", "dp"),
        P(None, None, ("tensor", "dp")),
        P(None, ("tensor", "dp")),
        P(None, None, ("dp", "tensor")),
        P(None, None, ("dp", "tensor")),
        P(None, None, ("dp", "tensor")),
    )
    return jax.shard_map(local, mesh=mesh, in_specs=in_specs, out_specs=out_specs, check_vma=False)
```
